32 devices in a mesh: dp: 4 (over z), ctx: 4 (over x, core), uly: 2 (over y).
Axes of the slice: x: 2, y: 2, z: 4, core: 2. Of those that a mesh axis runs over, the one named last changes fastest.
Arguments:
- layer_input: bfloat16 [8192, 1536], P(('dp', 'ctx', 'uly')), may hold values from -6 to 6
- span_order: int32 [4, 8], P('dp'), may hold values from 0 to 7, as said below
- doc_lengths: int32 [4, 3], P('dp'), may hold values from 1 to 1536, as said below
- pad_mask: int32 [4, 2048], P('dp'), may hold values 0 or 1
- w_qkv: bfloat16 [1536, 2048], P(('dp', 'ctx', 'uly')), may hold values from -0.15625 to 0.15625
- b_qkv: bfloat16 [2048], P(('dp', 'ctx', 'uly')), may hold values from -3 to 3
- w_out: bfloat16 [1536, 1536], P(None, ('dp', 'ctx', 'uly')), may hold values from -2.5 to 2.5
- norm_gain_attn: bfloat16 [1536], P(('dp', 'ctx', 'uly')), may hold values from 0.5 to 1.5
- norm_gain_mlp: bfloat16 [1536], P(('dp', 'ctx', 'uly')), may hold values from 0.5 to 1.5
- w_mlp: bfloat16 [1536, 26880], P(('dp', 'ctx', 'uly')), may hold values from -0.25 to 0.25
- cotangent: bfloat16 [8192, 1536], P(('dp', 'ctx', 'uly')), may hold values from -6 to 6
Outputs:
- block_output: bfloat16 [8192, 1536], P(('dp', 'ctx', 'uly'))
- input_grad: float32 [8192, 1536], P(('dp', 'ctx', 'uly'))
- grad_qkv: float32 [1536, 2048], P(('dp', 'ctx', 'uly'))
- grad_qkv_bias: float32 [2048], P(('dp', 'ctx', 'uly'))
- grad_out: float32 [1536, 1536], P(None, ('dp', 'ctx', 'uly'))
- grad_gain_attn: float32 [1536], P(('dp', 'ctx', 'uly'))
- grad_gain_mlp: float32 [1536], P(('dp', 'ctx', 'uly'))
- grad_mlp: float32 [1536, 26880], P(('dp', 'ctx', 'uly'))
The draws below stay inside these ranges and needn't reach their ends.
Inputs may be any that keep to these rules, and one draw needn't show every extreme that they name: `span_order`: in each row, entries 2 c and 2 c + 1 are a span i < 4 and 7 - i; each row is a permutation of 0 to 7. `doc_lengths`: each row sums to 2048; the first document has 1024 tokens or more.
All inputs are finite; a program needn't handle non-finite values. No bound on the sum of `pad_mask` on one device may be relied on, other than what follows from the above.
Results may differ from the reference program's by a relative error of at most 0.025.
Values may be sent and summed in bfloat16 or wider, within the bound.
No kernel may reach another device: no remote copies, remote signals or barrier semaphores. Data moves between devices by JAX's collectives and lax.ppermute only.
A program may use at most 704 MiB of HBM per device.

```python
import jax
import jax.numpy as jnp
from jax import lax

D = 1536
HEADS = 12
KV_HEADS = 2
HEAD = 128
FF = 8960
TOK_DEV = 256
DOCS = 3
QDIM = 1536
QKV = 2048
BATCH = 2048
SPANS = 8
TOKENS = 8192
N_DP = 4
N_CTX = 4


def draw_span_order(key, part):
    key = jax.random.fold_in(key, 11)
    keys_all = jax.random.split(key, N_DP)
    ranked = jax.vmap(lambda one_key: jax.random.permutation(one_key, N_CTX))(keys_all).astype(jnp.int32)
    paired = jnp.stack([ranked, 2 * N_CTX - 1 - ranked], axis=-1)
    return paired.reshape(N_DP, SPANS).astype(jnp.int32)


def draw_doc_lengths(key, part):
    key = jax.random.fold_in(key, 23)
    first_key, share_key, pick_key = jax.random.split(key, 3)
    leading = BATCH // 2 + jax.random.randint(first_key, (N_DP, 1), 0, BATCH // 4 + 1, dtype=jnp.int32)
    chosen = jax.random.randint(pick_key, (), 0, N_DP, dtype=jnp.int32)
    is_chosen = jnp.arange(N_DP, dtype=jnp.int32)[:, None] == chosen
    leading = jnp.where(is_chosen, BATCH // 2 + BATCH // 4, leading).astype(jnp.int32)
    remaining = BATCH - leading
    shares = jax.random.randint(share_key, (N_DP, DOCS - 1), 1, 9, dtype=jnp.int32)
    pieces_len = remaining * shares // jnp.sum(shares, axis=1, keepdims=True)
    leftover = remaining[:, 0] - jnp.sum(pieces_len, axis=1)
    pieces_len = pieces_len.at[:, DOCS - 2].add(leftover)
    return jnp.concatenate([leading, pieces_len], axis=1).astype(jnp.int32)


def plant(array, own_key, least, high):
    index_at = [jax.random.randint(jax.random.fold_in(own_key, axis), (), 0, length) for axis, length in enumerate(array.shape)]
    widest = array.shape.index(max(array.shape))
    beside = index_at[:widest] + [(index_at[widest] + 1) % array.shape[widest]] + index_at[widest + 1:]
    return array.at[tuple(index_at)].set(least).at[tuple(beside)].set(high)


def shard_levels(rng, dims, shards, low, high):
    gain, own = 1.0, jax.random.fold_in(rng, 6)
    for axis_at, blocks in shards:
        steps = jnp.exp(jax.random.uniform(jax.random.fold_in(own, axis_at), (blocks,), jnp.float32, low / len(shards), high / len(shards)))
        gain = gain * jnp.repeat(steps, dims[axis_at] // blocks).reshape([-1 if axis == axis_at else 1 for axis in range(len(dims))])
    return gain


def bell_draw(key, dims, deviation, reach, cuts=(), kind=jnp.bfloat16):
    values = jax.random.normal(key, dims, jnp.float32) * deviation
    if len(cuts) > 0:
        values = shard_levels(key, dims, cuts, -0.22, 0.18) * values
    return jnp.clip(values, min=-reach, max=reach).astype(kind)


def setup_inputs(seed: int = 0) -> dict:
    streams_of = jax.random.split(jax.random.key(seed), 12)
    return {
        "layer_input": bell_draw(streams_of[0], (TOKENS, D), 1.0, 6.0, ((0, 32),)),
        "span_order": draw_span_order(jax.random.fold_in(streams_of[11], 71), 0),
        "doc_lengths": draw_doc_lengths(jax.random.fold_in(streams_of[11], 71), 0),
        "pad_mask": plant((jax.random.randint(streams_of[3], (N_DP, BATCH), 0, 8) < 7).astype(jnp.int32), jax.random.fold_in(streams_of[3], 1), 0, 1),
        "w_qkv": bell_draw(streams_of[4], (D, QKV), D ** -0.5, 0.15625, ((0, 32),)),
        "b_qkv": bell_draw(streams_of[5], (QKV,), 0.5, 3.0, ((0, 32),)),
        "w_out": bell_draw(streams_of[6], (QDIM, D), (max(QDIM // 256, 4)) ** -0.5, 2.5, ((1, 32),)),
        "norm_gain_attn": jnp.clip(1.0 + 0.1 * jax.random.normal(streams_of[7], (D,), jnp.float32), 0.5, 1.5).astype(jnp.bfloat16),
        "norm_gain_mlp": jnp.clip(1.0 + 0.1 * jax.random.normal(streams_of[8], (D,), jnp.float32), 0.5, 1.5).astype(jnp.bfloat16),
        "w_mlp": bell_draw(streams_of[9], (D, 3 * FF), (D // 3) ** -0.5, 0.25, ((0, 32),)),
        "cotangent": bell_draw(streams_of[10], (TOKENS, D), 1.0, 6.0, ((0, 32),)),
    }


@jax.custom_vjp
def low(v):
    return lax.optimization_barrier(v.astype(jnp.bfloat16)).astype(jnp.float32)

@jax.custom_vjp
def low_back(v):
    return v

def low_keep(v):
    return (low(v), None)

def low_pass(kept, grad):
    return (grad,)

def back_keep(v):
    return (v, None)

def back_low(kept, grad):
    return (low(grad),)
low.defvjp(low_keep, low_pass)
low_back.defvjp(back_keep, back_low)
NORM_EPS = 1e-06
ROPE_BASE = 1000000.0
NEG_FILL = -1e+30
HIGHEST = lax.Precision.HIGHEST

def seq_places(stored, order_row, length_row):
    blocks = order_row.shape[0]
    picked = (stored // TOK_DEV)[:, None] == jnp.arange(blocks, dtype=jnp.int32)[None, :]
    span_of = lax.optimization_barrier(jnp.sum(jnp.where(picked, order_row[None, :], 0), axis=1)).astype(jnp.int32)
    places = span_of * TOK_DEV + stored % TOK_DEV
    doc_ends = jnp.cumsum(length_row).astype(jnp.int32)
    passed = places[:, None] >= doc_ends[None, :]
    doc_ids = lax.optimization_barrier(jnp.sum(passed.astype(jnp.int32), axis=1)).astype(jnp.int32)
    begins = lax.optimization_barrier(jnp.max(jnp.where(passed, doc_ends[None, :], 0), axis=1)).astype(jnp.int32)
    return (places, doc_ids, places - begins)

def rms_norm(values):
    return values * lax.rsqrt(lax.optimization_barrier(jnp.mean(values * values, axis=-1, keepdims=True)) + NORM_EPS)

def rotate_pos(vector, inner_pos, direction):
    half_width = vector.shape[-1] // 2
    frequency = ROPE_BASE ** (-(jnp.arange(half_width, dtype=jnp.float32) * 2.0) / vector.shape[-1])
    angles = direction * inner_pos.astype(jnp.float32)[:, None] * frequency[None, :]
    cosine = jnp.cos(angles)[:, None, :]
    sine_part = jnp.sin(angles)[:, None, :]
    first_half = vector[..., :half_width]
    second_half = vector[..., half_width:]
    return jnp.concatenate([first_half * cosine - second_half * sine_part, second_half * cosine + first_half * sine_part], axis=-1)

def attend_batch(operands):
    query_rows, key_rows, value_rows, places, doc_ids, mask_flags, mask_weight = operands
    block_rows = min(512, BATCH)
    block_count = BATCH // block_rows
    stored = jnp.arange(BATCH, dtype=jnp.int32)
    keys_all = jnp.repeat(key_rows, HEADS // KV_HEADS, axis=1)
    values_all = jnp.repeat(value_rows, HEADS // KV_HEADS, axis=1)

    def one_block(pieces):
        query_blk, place_blk, doc_blk, stored_blk, weight_blk = pieces
        scores = jnp.einsum('qhd,khd->qhk', query_blk, keys_all, precision=HIGHEST) * HEAD ** (-0.5)
        scores = low_back(scores)
        allowed = (doc_ids[None, :] == doc_blk[:, None]) & (places[None, :] <= place_blk[:, None])
        allowed = allowed & ((mask_flags[None, :] == 1) | (stored[None, :] == stored_blk[:, None]))
        scores = jnp.where(allowed[:, None, :], scores, NEG_FILL)
        probs_all = jax.nn.softmax(scores, axis=-1)
        mixed_out = jnp.einsum('qhk,khd->qhd', low(probs_all), values_all, precision=HIGHEST)
        return mixed_out * weight_blk[:, None, None]
    pieces = (query_rows.reshape(block_count, block_rows, HEADS, HEAD), places.reshape(block_count, block_rows), doc_ids.reshape(block_count, block_rows), stored.reshape(block_count, block_rows), mask_weight.reshape(block_count, block_rows))
    return lax.map(jax.checkpoint(one_block), pieces).reshape(BATCH, HEADS, HEAD)

def reference(layer_input, span_order, doc_lengths, pad_mask, w_qkv, b_qkv, w_out, norm_gain_attn, norm_gain_mlp, w_mlp, cotangent):
    stored = jnp.arange(BATCH, dtype=jnp.int32)
    places, doc_ids, inner_pos = jax.vmap(seq_places, in_axes=(None, 0, 0))(stored, span_order, doc_lengths)
    inner_all = inner_pos.reshape(TOKENS)
    mask_weight = pad_mask.astype(jnp.float32)
    q_width = HEADS * HEAD
    kv_width = KV_HEADS * HEAD

    def forward(in_rows, w_proj, b_proj, w_mix, gain_one, gain_two, w_ffn):
        normed_in = low(rms_norm(in_rows) * gain_one)
        projected = low_back(jnp.dot(normed_in, w_proj, precision=HIGHEST) + b_proj)
        queries = projected[:, :q_width].reshape(TOKENS, HEADS, HEAD)
        keys_rot = projected[:, q_width:q_width + kv_width].reshape(TOKENS, KV_HEADS, HEAD)
        value_rows = projected[:, q_width + kv_width:].reshape(TOKENS, KV_HEADS, HEAD)
        queries = low(low_back(rotate_pos(queries, inner_all, 1.0)))
        keys_rot = low(low_back(rotate_pos(keys_rot, inner_all, 1.0)))
        value_rows = low(low_back(value_rows))
        attended = lax.map(attend_batch, (queries.reshape(N_DP, BATCH, HEADS, HEAD), keys_rot.reshape(N_DP, BATCH, KV_HEADS, HEAD), value_rows.reshape(N_DP, BATCH, KV_HEADS, HEAD), places, doc_ids, pad_mask, mask_weight))
        attended = low(low_back(attended.reshape(TOKENS, q_width)))
        branch_out = low_back(jnp.dot(attended, w_mix, precision=HIGHEST))
        middle = in_rows + branch_out
        normed_mid = low(rms_norm(middle) * gain_two)
        gate_up = jnp.dot(normed_mid, w_ffn[:, :2 * FF], precision=HIGHEST)
        gate_part = low_back(gate_up[:, :FF])
        up_part = low_back(gate_up[:, FF:])
        hidden_act = low(jax.nn.silu(gate_part) * up_part)
        mlp_out = low_back(jnp.dot(hidden_act, w_ffn[:, 2 * FF:].T, precision=HIGHEST))
        return middle + mlp_out
    output, pullback = jax.vjp(forward, layer_input.astype(jnp.float32), w_qkv.astype(jnp.float32), b_qkv.astype(jnp.float32), w_out.astype(jnp.float32), norm_gain_attn.astype(jnp.float32), norm_gain_mlp.astype(jnp.float32), w_mlp.astype(jnp.float32))
    gradients = pullback(cotangent.astype(jnp.float32))
    return (output.astype(jnp.bfloat16), gradients[0], gradients[1], gradients[2], gradients[3], gradients[4], gradients[5], gradients[6])
```

```python
import functools

import jax
import jax.numpy as jnp
from jax import lax
from jax.experimental import pallas as pl
from jax.experimental.pallas import tpu as pltpu
from jax.sharding import PartitionSpec as P

HEADS = 12
KV_HEADS = 2
HEAD = 128
TOK_DEV = 256
LANES = 128
GROUP = HEADS // KV_HEADS

NORM_EPS = 1e-06
ROPE_BASE = 1000000.0
NEG_FILL = -1e30
LOG2E = 1.4426950408889634
SCALE = HEAD ** (-0.5)
FAR = 1 << 30
PLANE = ("ctx", "uly")
EVERY = ("dp", "ctx", "uly")
VMEM_LIMIT = 56 * 1024 * 1024
F32 = jnp.float32
BF16 = jnp.bfloat16


def dot(left, right, left_dim, right_dim):
    return lax.dot_general(
        left, right, (((left_dim,), (right_dim,)), ((), ())), preferred_element_type=F32
    )


def block_bias(kinfo_ref, qinfo_ref, rows):
    info = kinfo_ref[rows, :]
    usable, place = info[:, 0:1], info[:, 1:2]
    q_place, q_begin = qinfo_ref[0:1, :], qinfo_ref[1:2, :]
    allowed = ((usable <= q_place) & (usable >= q_begin)) | (place == q_place)
    return jnp.where(allowed, 0.0, NEG_FILL)


def attn_fwd_kernel(
    need_ref, kinfo_ref, qinfo_ref, q_ref, kv_ref, o_ref, lse_ref, m_ref, l_ref, acc_ref, bias_ref
):
    blocks = kv_ref.shape[0] // TOK_DEV
    m_ref[...] = jnp.full(m_ref.shape, NEG_FILL, F32)
    l_ref[...] = jnp.zeros(l_ref.shape, F32)
    acc_ref[...] = jnp.zeros(acc_ref.shape, F32)

    def one_block(block, carry):
        @pl.when(need_ref[block] > 0)
        def _():
            rows = pl.ds(pl.multiple_of(block * TOK_DEV, TOK_DEV), TOK_DEV)
            bias_ref[...] = block_bias(kinfo_ref, qinfo_ref, rows)
            for group in range(KV_HEADS):
                key = kv_ref[rows, group * HEAD : (group + 1) * HEAD]
                value = kv_ref[rows, (KV_HEADS + group) * HEAD : (KV_HEADS + group + 1) * HEAD]
                value_t = value.T
                for head in range(group * GROUP, (group + 1) * GROUP):
                    span = slice(head * HEAD, (head + 1) * HEAD)
                    scores = dot(key, q_ref[span, :], 1, 0) * (SCALE * LOG2E) + bias_ref[...]
                    old = m_ref[head : head + 1, :]
                    new = jnp.maximum(old, jnp.max(scores, axis=0, keepdims=True))
                    weights = jnp.exp2(scores - new)
                    factor = jnp.exp2(old - new)
                    m_ref[head : head + 1, :] = new
                    l_ref[head : head + 1, :] = l_ref[head : head + 1, :] * factor + jnp.sum(
                        weights, axis=0, keepdims=True
                    )
                    acc_ref[span, :] = acc_ref[span, :] * factor + dot(
                        value_t, weights.astype(BF16), 1, 0
                    )

        return carry

    lax.fori_loop(0, blocks, one_block, 0)
    real = qinfo_ref[2:3, :].astype(F32)
    lse_ref[...] = jnp.zeros(lse_ref.shape, F32)
    for head in range(HEADS):
        span = slice(head * HEAD, (head + 1) * HEAD)
        total = l_ref[head : head + 1, :]
        o_ref[span, :] = (acc_ref[span, :] * (real / total)).astype(BF16)
        lse_ref[head : head + 1, :] = m_ref[head : head + 1, :] + jnp.log(total) * LOG2E


def attn_bwd_kernel(
    need_ref,
    kinfo_ref,
    qinfo_ref,
    cos_ref,
    sin_ref,
    q_ref,
    kv_ref,
    o_ref,
    do_ref,
    lse_ref,
    dq_ref,
    dkv_ref,
    dots_ref,
    acc_ref,
    bias_ref,
    low_ref,
):
    blocks = kv_ref.shape[0] // TOK_DEV
    real = qinfo_ref[2:3, :].astype(F32)
    for head in range(HEADS):
        span = slice(head * HEAD, (head + 1) * HEAD)
        grad = do_ref[span, :].astype(F32) * real
        low_ref[span, :] = grad.astype(BF16)
        dots_ref[head : head + 1, :] = jnp.sum(
            grad * o_ref[span, :].astype(F32), axis=0, keepdims=True
        )
    acc_ref[...] = jnp.zeros(acc_ref.shape, F32)

    def one_block(block, carry):
        rows = pl.ds(pl.multiple_of(block * TOK_DEV, TOK_DEV), TOK_DEV)

        @pl.when(need_ref[block] == 0)
        def _():
            dkv_ref[rows, :] = jnp.zeros((TOK_DEV, 2 * KV_HEADS * HEAD), BF16)

        @pl.when(need_ref[block] > 0)
        def _():
            bias_ref[...] = block_bias(kinfo_ref, qinfo_ref, rows)
            for group in range(KV_HEADS):
                key_cols = slice(group * HEAD, (group + 1) * HEAD)
                value_cols = slice((KV_HEADS + group) * HEAD, (KV_HEADS + group + 1) * HEAD)
                key = kv_ref[rows, key_cols]
                value = kv_ref[rows, value_cols]
                key_t = key.T
                key_grad = jnp.zeros((TOK_DEV, HEAD), F32)
                value_grad = jnp.zeros((TOK_DEV, HEAD), F32)
                for head in range(group * GROUP, (group + 1) * GROUP):
                    span = slice(head * HEAD, (head + 1) * HEAD)
                    query, grad = q_ref[span, :], low_ref[span, :]
                    scores = dot(key, query, 1, 0) * (SCALE * LOG2E) + bias_ref[...]
                    probs = jnp.exp2(scores - lse_ref[head : head + 1, :])
                    prob_grad = dot(value, grad, 1, 0)
                    score_grad = (probs * (prob_grad - dots_ref[head : head + 1, :])).astype(BF16)
                    acc_ref[span, :] += dot(key_t, score_grad, 1, 0)
                    key_grad += dot(score_grad, query, 1, 1)
                    value_grad += dot(probs.astype(BF16), grad, 1, 1)
                dkv_ref[rows, key_cols] = (key_grad * SCALE).astype(BF16)
                dkv_ref[rows, value_cols] = value_grad.astype(BF16)

        return carry

    lax.fori_loop(0, blocks, one_block, 0)
    cosine, sine = cos_ref[...], sin_ref[...]
    half = HEAD // 2
    for head in range(HEADS):
        start = head * HEAD
        whole = (acc_ref[start : start + HEAD, :] * SCALE).astype(BF16).astype(F32)
        first, second = whole[:half], whole[half:]
        turned = jnp.concatenate(
            [first * cosine + second * sine, second * cosine - first * sine], axis=0
        )
        dq_ref[:, start : start + HEAD] = turned.T.astype(BF16)


def vmem_specs(count):
    return [pl.BlockSpec(memory_space=pltpu.VMEM)] * count


def attention_forward(need, kinfo, qinfo, query_t, kv_all):
    rows = query_t.shape[1]
    return pl.pallas_call(
        attn_fwd_kernel,
        out_shape=(
            jax.ShapeDtypeStruct((HEADS * HEAD, rows), BF16),
            jax.ShapeDtypeStruct((16, rows), F32),
        ),
        in_specs=[pl.BlockSpec(memory_space=pltpu.SMEM)] + vmem_specs(4),
        out_specs=tuple(vmem_specs(2)),
        scratch_shapes=[
            pltpu.VMEM((16, rows), F32),
            pltpu.VMEM((16, rows), F32),
            pltpu.VMEM((HEADS * HEAD, rows), F32),
            pltpu.VMEM((TOK_DEV, rows), F32),
        ],
        compiler_params=pltpu.CompilerParams(vmem_limit_bytes=VMEM_LIMIT),
        cost_estimate=pl.CostEstimate(
            flops=4 * HEADS * rows * kv_all.shape[0] * HEAD,
            bytes_accessed=8 * 1024 * 1024,
            transcendentals=HEADS * rows * kv_all.shape[0],
        ),
    )(need, kinfo, qinfo, query_t, kv_all)


def attention_backward(need, kinfo, qinfo, cos_t, sin_t, query_t, kv_all, out_t, grad_t, lse):
    rows = query_t.shape[1]
    return pl.pallas_call(
        attn_bwd_kernel,
        out_shape=(
            jax.ShapeDtypeStruct((rows, HEADS * HEAD), BF16),
            jax.ShapeDtypeStruct(kv_all.shape, BF16),
        ),
        in_specs=[pl.BlockSpec(memory_space=pltpu.SMEM)] + vmem_specs(9),
        out_specs=tuple(vmem_specs(2)),
        scratch_shapes=[
            pltpu.VMEM((16, rows), F32),
            pltpu.VMEM((HEADS * HEAD, rows), F32),
            pltpu.VMEM((TOK_DEV, rows), F32),
            pltpu.VMEM((HEADS * HEAD, rows), BF16),
        ],
        compiler_params=pltpu.CompilerParams(vmem_limit_bytes=VMEM_LIMIT),
        cost_estimate=pl.CostEstimate(
            flops=10 * HEADS * rows * kv_all.shape[0] * HEAD,
            bytes_accessed=12 * 1024 * 1024,
            transcendentals=HEADS * rows * kv_all.shape[0],
        ),
    )(need, kinfo, qinfo, cos_t, sin_t, query_t, kv_all, out_t, grad_t, lse)


def ffn_kernel(parts, mid_ref, cot_ref, *refs):
    gate_w, up_w, down_w = refs[:parts], refs[parts : 2 * parts], refs[2 * parts : 3 * parts]
    hidden_ref, gate_grad_ref, up_grad_ref, mid_grad_ref, out_ref = refs[3 * parts :]
    depth = gate_w[0].shape[0]

    def through(rows_ref, weights):
        total = None
        for part in range(parts):
            term = dot(rows_ref[:, part * depth : (part + 1) * depth], weights[part][...], 1, 0)
            total = term if total is None else total + term
        return total

    gate = through(mid_ref, gate_w)
    up = through(mid_ref, up_w)
    hidden_grad = through(cot_ref, down_w)
    share = 1.0 / (1.0 + jnp.exp(-gate))
    acted = gate * share
    hidden = (acted * up).astype(BF16)
    up_grad = (hidden_grad * acted).astype(BF16)
    gate_grad = (hidden_grad * up * (share * (1.0 + gate * (1.0 - share)))).astype(BF16)
    hidden_ref[...] = hidden
    gate_grad_ref[...] = gate_grad
    up_grad_ref[...] = up_grad
    for part in range(parts):
        cols = slice(part * depth, (part + 1) * depth)
        mid_grad_ref[:, cols] = (
            dot(gate_grad, gate_w[part][...], 1, 1) + dot(up_grad, up_w[part][...], 1, 1)
        ).astype(BF16)
        out_ref[:, cols] = dot(hidden, down_w[part][...], 1, 1).astype(BF16)


def feed_forward(mid_rows, cot_rows, gate_w, up_w, down_w):
    parts = len(gate_w)
    tokens, width = mid_rows.shape
    depth, cols = gate_w[0].shape
    tile = TOK_DEV
    row_spec = pl.BlockSpec((tile, width), lambda i: (i, 0))
    act_spec = pl.BlockSpec((tile, cols), lambda i: (i, 0))
    w_spec = pl.BlockSpec((depth, cols), lambda i: (0, 0), pipeline_mode=pl.Buffered(1))
    return pl.pallas_call(
        functools.partial(ffn_kernel, parts),
        grid=(tokens // tile,),
        out_shape=(jax.ShapeDtypeStruct((tokens, cols), BF16),) * 3
        + (jax.ShapeDtypeStruct((tokens, width), BF16),) * 2,
        in_specs=[row_spec] * 2 + [w_spec] * (3 * parts),
        out_specs=(act_spec,) * 3 + (row_spec,) * 2,
        compiler_params=pltpu.CompilerParams(vmem_limit_bytes=VMEM_LIMIT),
        cost_estimate=pl.CostEstimate(
            flops=12 * tokens * width * cols,
            bytes_accessed=2 * (3 * width * cols + 3 * tokens * cols + 4 * tokens * width),
            transcendentals=tokens * cols,
        ),
    )(mid_rows, cot_rows, *gate_w, *up_w, *down_w)


def shift(array, axis, step):
    count = lax.axis_size(axis)
    return lax.ppermute(array, axis, [(i, (i + step) % count) for i in range(count)])


def ring_gather(block, axis):
    pieces = [block]
    for _ in range(lax.axis_size(axis) - 1):
        pieces.append(shift(pieces[-1], axis, -1))
    return pieces


def ring_reduce(block_of, axis):
    count = lax.axis_size(axis)
    running = block_of(count - 1)
    for r in range(count - 2, -1, -1):
        moved = shift(running, axis, 1)
        running = (moved.astype(F32) + block_of(r).astype(F32)).astype(BF16)
    return running


def plane_bits():
    ctx, uly = lax.axis_size("ctx"), lax.axis_size("uly")
    count = ctx * uly
    assert count & (count - 1) == 0 and ctx % 2 == 0
    core = uly
    near = [1 << i for i in range(uly.bit_length() - 1)]
    far = [core << i for i in range(1, (ctx // 2).bit_length())]
    return count, core, near, far


def swap(array, bit):
    count = lax.axis_size("ctx") * lax.axis_size("uly")
    return lax.ppermute(array, PLANE, [(i, i ^ bit) for i in range(count)])


def plane_gather(rows):
    count, core, near, far = plane_bits()
    half = rows.shape[0] // 2
    got = []
    for piece, order in ((rows[:half], far + near), (rows[half:], near + far)):
        held = {0: piece}
        for bit in order:
            for i in sorted(held):
                held[i ^ bit] = swap(held[i], bit)
        for i in sorted(held):
            held[i ^ core] = swap(held[i], core)
        got.append(held)
    return [(got[0][i], got[1][i]) for i in range(count)]


def plane_reduce(block_of):
    count, core, near, far = plane_bits()
    halves = []
    for which, order in ((0, near + far), (1, far + near)):
        held = {i: block_of(i)[which] for i in range(count)}
        for bit in [core] + order:
            kept = {}
            for i in sorted(held):
                if not i & bit:
                    moved = swap(held[i | bit], bit)
                    kept[i] = (held[i].astype(F32) + moved.astype(F32)).astype(BF16)
            held = kept
        halves.append(held[0])
    return jnp.concatenate(halves, axis=0)


def place_info(spans, row_in_span, length_row):
    places = spans * TOK_DEV + row_in_span
    begins = jnp.zeros_like(places)
    end = jnp.int32(0)
    for doc in range(length_row.shape[0]):
        end = end + length_row[doc]
        begins = jnp.where(places >= end, jnp.maximum(begins, end), begins)
    return places, begins


def inverse_rms(values):
    return lax.rsqrt(jnp.mean(values * values, axis=-1, keepdims=True) + NORM_EPS)


def norm_backward(values, inverse, scaled):
    return inverse * scaled - values * (
        inverse**3 * jnp.mean(scaled * values, axis=-1, keepdims=True)
    )


def turn(heads, cosine, sine):
    half = HEAD // 2
    first, second = heads[..., :half], heads[..., half:]
    return jnp.concatenate(
        [first * cosine - second * sine, second * cosine + first * sine], axis=-1
    )


def shards(
    layer_input,
    span_order,
    doc_lengths,
    pad_mask,
    w_qkv,
    b_qkv,
    w_out,
    norm_gain_attn,
    norm_gain_mlp,
    w_mlp,
    cotangent,
):
    tok_rows, width = layer_input.shape
    n_dp = lax.axis_size("dp")
    n_plane = lax.axis_size("ctx") * lax.axis_size("uly")
    n_all = n_dp * n_plane
    me = lax.axis_index("ctx") * lax.axis_size("uly") + lax.axis_index("uly")
    my_dp = lax.axis_index("dp")
    order_row, length_row, mask_row = span_order[0], doc_lengths[0], pad_mask[0]
    ffn_width = w_mlp.shape[1] // 3
    local_rows = w_mlp.shape[0]
    zone = local_rows * n_plane
    q_width, kv_width = HEADS * HEAD, KV_HEADS * HEAD
    qkv_width = q_width + 2 * kv_width
    bias_rows = b_qkv.shape[0]
    slice_cols = -(-(ffn_width // LANES) // n_plane) * LANES
    pad_cols = slice_cols * n_plane - ffn_width

    def to_slice(which):
        mine = w_mlp[:, which * ffn_width : (which + 1) * ffn_width]
        mine = jnp.pad(mine, ((0, 0), (0, pad_cols))).reshape(local_rows, n_plane, slice_cols)
        mine = mine.transpose(1, 0, 2).reshape(zone, slice_cols)
        mine = lax.all_to_all(mine, PLANE, split_axis=0, concat_axis=0, tiled=True)
        return ring_gather(mine, "dp")

    side = jnp.concatenate(
        [
            norm_gain_attn[:, None],
            norm_gain_mlp[:, None],
            jnp.zeros((local_rows, 62), BF16),
            jnp.pad(b_qkv[None, :], ((0, local_rows - 1), (0, 64 - bias_rows))),
        ],
        axis=1,
    )
    w_qkv_all = lax.all_gather(
        jnp.concatenate([w_qkv, side], axis=1), EVERY, axis=0, tiled=True
    )
    w_out_all = lax.all_gather(w_out.T, EVERY, axis=0, tiled=True)
    side_all = w_qkv_all[:, qkv_width:].astype(F32)
    gain_attn = side_all[:, 0]
    gain_mlp = side_all[:, 1]
    bias_all = side_all.reshape(n_all, local_rows, LANES)[:, 0, 64 : 64 + bias_rows].reshape(-1)

    gate_w, up_w, down_w = to_slice(0), to_slice(1), to_slice(2)

    row_in_span = jnp.arange(tok_rows, dtype=jnp.int32)
    stored_block = me ^ jnp.arange(n_plane, dtype=jnp.int32)
    spans = order_row[stored_block]
    own_place, own_begin = place_info(spans[0], row_in_span, length_row)
    flags = mask_row.reshape(n_plane, tok_rows)[stored_block]
    key_place = spans[:, None] * TOK_DEV + row_in_span[None, :]
    kinfo = jnp.stack(
        [jnp.where(flags == 1, key_place, FAR).reshape(-1), key_place.reshape(-1)], axis=1
    )
    qinfo = jnp.concatenate(
        [
            own_place[None],
            own_begin[None],
            flags[0][None],
            jnp.zeros((5, tok_rows), jnp.int32),
        ],
        axis=0,
    )
    need = ((spans <= spans[0]) & ((spans + 1) * TOK_DEV > own_begin[0])).astype(jnp.int32)

    inner = (own_place - own_begin).astype(F32)
    half = HEAD // 2
    frequency = ROPE_BASE ** (-(jnp.arange(half, dtype=F32) * 2.0) / HEAD)
    angles_t = frequency[:, None] * inner[None, :]
    cos_t, sin_t = jnp.cos(angles_t), jnp.sin(angles_t)
    cos_r, sin_r = cos_t.T[:, None, :], sin_t.T[:, None, :]

    inputs = layer_input.astype(F32)
    in_inverse = inverse_rms(inputs)
    normed_in = (inputs * in_inverse * gain_attn).astype(BF16)

    kv_proj = dot(normed_in, w_qkv_all[:, q_width:qkv_width], 1, 0) + bias_all[q_width:]
    key_own = turn(kv_proj[:, :kv_width].reshape(tok_rows, KV_HEADS, HEAD), cos_r, sin_r)
    kv_own = jnp.concatenate([key_own.reshape(tok_rows, kv_width), kv_proj[:, kv_width:]], axis=1)
    kv_pieces = plane_gather(kv_own.astype(BF16))
    kv_all = jnp.concatenate([half_rows for pair in kv_pieces for half_rows in pair], axis=0)

    q_proj = dot(w_qkv_all[:, :q_width], normed_in, 0, 1) + bias_all[:q_width, None]
    q_heads = q_proj.reshape(HEADS, 2, half, tok_rows)
    q_first, q_second = q_heads[:, 0], q_heads[:, 1]
    query_t = (
        jnp.stack(
            [q_first * cos_t - q_second * sin_t, q_second * cos_t + q_first * sin_t], axis=1
        )
        .reshape(q_width, tok_rows)
        .astype(BF16)
    )
    attended_t, lse = attention_forward(need, kinfo, qinfo, query_t, kv_all)

    middle = inputs + dot(attended_t, w_out_all, 0, 1)
    mid_inverse = inverse_rms(middle)
    normed_mid = (middle * mid_inverse * gain_mlp).astype(BF16)

    def turn_zone(array, zones):
        return lax.dynamic_slice_in_dim(
            jnp.concatenate([array, array], axis=1), zones * zone, width, 1
        )

    def gather_tokens(array):
        pieces = plane_gather(turn_zone(array, my_dp))
        return jnp.concatenate([rows for pair in pieces for rows in pair], axis=0)

    cot_rows = gather_tokens(cotangent)
    mid_rows = gather_tokens(normed_mid)
    hidden, gate_grad, up_grad, mid_grad_part, out_part = feed_forward(
        mid_rows, cot_rows, gate_w, up_w, down_w
    )

    def token_blocks(array):
        cut = tok_rows // 2
        return lambda i: (
            array[i * tok_rows : i * tok_rows + cut],
            array[i * tok_rows + cut : (i + 1) * tok_rows],
        )

    mid_grad = turn_zone(plane_reduce(token_blocks(mid_grad_part)), n_dp - my_dp).astype(F32)

    def slice_gradient(rows, columns):
        mine = ring_reduce(
            lambda r: dot(rows[:, r * zone : (r + 1) * zone], columns, 0, 0).astype(BF16), "dp"
        )
        mine = lax.all_to_all(mine, PLANE, split_axis=0, concat_axis=0, tiled=True)
        mine = mine.reshape(n_plane, local_rows, slice_cols).transpose(1, 0, 2)
        return mine.reshape(local_rows, n_plane * slice_cols)[:, :ffn_width].astype(F32)

    grad_down = slice_gradient(cot_rows, hidden)
    grad_gate = slice_gradient(mid_rows, gate_grad)
    grad_up = slice_gradient(mid_rows, up_grad)
    grad_mlp = jnp.concatenate([grad_gate, grad_up, grad_down], axis=1)

    out_grad = cotangent.astype(F32)
    gain_mlp_grad = jnp.sum(mid_grad * (middle * mid_inverse), axis=0)
    middle_grad = out_grad + norm_backward(middle, mid_inverse, mid_grad * gain_mlp)
    middle_low = middle_grad.astype(BF16)
    attended_grad_t = dot(w_out_all, middle_low, 0, 1).astype(BF16)
    out_weight_grad = dot(middle_low, attended_t, 0, 1).astype(BF16)
    grad_out = lax.psum_scatter(out_weight_grad, EVERY, scatter_dimension=0, tiled=True)
    query_grad, kv_grad = attention_backward(
        need, kinfo, qinfo, cos_t, sin_t, query_t, kv_all, attended_t, attended_grad_t, lse
    )
    kv_back = plane_reduce(token_blocks(kv_grad)).astype(F32)
    key_back = turn(kv_back[:, :kv_width].reshape(tok_rows, KV_HEADS, HEAD), cos_r, -sin_r)
    projected_grad = jnp.concatenate(
        [query_grad, key_back.reshape(tok_rows, kv_width).astype(BF16), kv_back[:, kv_width:].astype(BF16)],
        axis=1,
    )
    in_grad = dot(projected_grad, w_qkv_all[:, :qkv_width], 1, 1)
    gain_attn_grad = jnp.sum(in_grad * (inputs * in_inverse), axis=0)
    input_grad = middle_grad + norm_backward(inputs, in_inverse, in_grad * gain_attn)
    qkv_bias_grad = jnp.sum(projected_grad.astype(F32), axis=0)
    side_grad = jnp.zeros((n_all, local_rows, LANES), F32)
    side_grad = side_grad.at[:, :, 0].set(gain_attn_grad.reshape(n_all, local_rows))
    side_grad = side_grad.at[:, :, 1].set(gain_mlp_grad.reshape(n_all, local_rows))
    side_grad = side_grad.at[:, 0, 64 : 64 + bias_rows].set(qkv_bias_grad.reshape(n_all, bias_rows))
    side_grad = side_grad.reshape(n_all * local_rows, LANES).astype(BF16)
    qkv_weight_grad = dot(normed_in, projected_grad, 0, 0).astype(BF16)
    qkv_sum = lax.psum_scatter(
        jnp.concatenate([qkv_weight_grad, side_grad], axis=1),
        EVERY,
        scatter_dimension=0,
        tiled=True,
    ).astype(F32)

    mlp_out = turn_zone(plane_reduce(token_blocks(out_part)), n_dp - my_dp)
    block_output = (middle + mlp_out.astype(F32)).astype(BF16)
    return (
        block_output,
        input_grad,
        qkv_sum[:, :qkv_width],
        qkv_sum[0, qkv_width + 64 : qkv_width + 64 + bias_rows],
        grad_out.astype(F32).T,
        qkv_sum[:, qkv_width],
        qkv_sum[:, qkv_width + 1],
        grad_mlp,
    )


def solution(mesh):
    rows = P(EVERY, None)
    flat = P(EVERY)
    columns = P(None, EVERY)
    batch = P("dp", None)
    return jax.shard_map(
        shards,
        mesh=mesh,
        in_specs=(rows, batch, batch, batch, rows, flat, columns, flat, flat, rows, rows),
        out_specs=(rows, rows, rows, flat, columns, flat, flat, rows),
        check_vma=False,
    )
```

```python
import functools

import jax
import jax.numpy as jnp
from jax import lax
from jax.experimental import pallas as pl
from jax.experimental.pallas import tpu as pltpu
from jax.sharding import PartitionSpec as P

HEADS = 12
KV_HEADS = 2
HEAD = 128
TOK_DEV = 256
LANES = 128
GROUP = HEADS // KV_HEADS

NORM_EPS = 1e-06
ROPE_BASE = 1000000.0
NEG_FILL = -1e30
LOG2E = 1.4426950408889634
SCALE = HEAD ** (-0.5)
FAR = 1 << 30
PLANE = ("ctx", "uly")
EVERY = ("dp", "ctx", "uly")
VMEM_LIMIT = 56 * 1024 * 1024
SMALL = pl.CostEstimate(flops=1024, bytes_accessed=1024, transcendentals=0)
F32 = jnp.float32
BF16 = jnp.bfloat16


def dot(left, right, left_dim, right_dim):
    return lax.dot_general(
        left, right, (((left_dim,), (right_dim,)), ((), ())), preferred_element_type=F32
    )


def block_bias(kinfo_ref, qinfo_ref, rows):
    info = kinfo_ref[rows, :]
    usable, place = info[:, 0:1], info[:, 1:2]
    q_place, q_begin = qinfo_ref[0:1, :], qinfo_ref[1:2, :]
    allowed = ((usable <= q_place) & (usable >= q_begin)) | (place == q_place)
    return jnp.where(allowed, 0.0, NEG_FILL)


def attn_fwd_kernel(
    need_ref, kinfo_ref, qinfo_ref, q_ref, kv_ref, o_ref, lse_ref, m_ref, l_ref, acc_ref, bias_ref
):
    blocks = kv_ref.shape[0] // TOK_DEV
    m_ref[...] = jnp.full(m_ref.shape, NEG_FILL, F32)
    l_ref[...] = jnp.zeros(l_ref.shape, F32)
    acc_ref[...] = jnp.zeros(acc_ref.shape, F32)

    def one_block(block, carry):
        @pl.when(need_ref[block] > 0)
        def _():
            rows = pl.ds(pl.multiple_of(block * TOK_DEV, TOK_DEV), TOK_DEV)
            bias_ref[...] = block_bias(kinfo_ref, qinfo_ref, rows)
            for group in range(KV_HEADS):
                key = kv_ref[rows, group * HEAD : (group + 1) * HEAD]
                value = kv_ref[rows, (KV_HEADS + group) * HEAD : (KV_HEADS + group + 1) * HEAD]
                value_t = value.T
                for head in range(group * GROUP, (group + 1) * GROUP):
                    span = slice(head * HEAD, (head + 1) * HEAD)
                    scores = dot(key, q_ref[span, :], 1, 0) * (SCALE * LOG2E) + bias_ref[...]
                    old = m_ref[head : head + 1, :]
                    new = jnp.maximum(old, jnp.max(scores, axis=0, keepdims=True))
                    weights = jnp.exp2(scores - new)
                    factor = jnp.exp2(old - new)
                    m_ref[head : head + 1, :] = new
                    l_ref[head : head + 1, :] = l_ref[head : head + 1, :] * factor + jnp.sum(
                        weights, axis=0, keepdims=True
                    )
                    acc_ref[span, :] = acc_ref[span, :] * factor + dot(
                        value_t, weights.astype(BF16), 1, 0
                    )

        return carry

    lax.fori_loop(0, blocks, one_block, 0)
    real = qinfo_ref[2:3, :].astype(F32)
    lse_ref[...] = jnp.zeros(lse_ref.shape, F32)
    for head in range(HEADS):
        span = slice(head * HEAD, (head + 1) * HEAD)
        total = l_ref[head : head + 1, :]
        o_ref[span, :] = (acc_ref[span, :] * (real / total)).astype(BF16)
        lse_ref[head : head + 1, :] = m_ref[head : head + 1, :] + jnp.log(total) * LOG2E


def attn_bwd_kernel(
    need_ref,
    kinfo_ref,
    qinfo_ref,
    cos_ref,
    sin_ref,
    q_ref,
    kv_ref,
    o_ref,
    do_ref,
    lse_ref,
    dq_ref,
    dkv_ref,
    dots_ref,
    acc_ref,
    bias_ref,
    low_ref,
):
    blocks = kv_ref.shape[0] // TOK_DEV
    real = qinfo_ref[2:3, :].astype(F32)
    for head in range(HEADS):
        span = slice(head * HEAD, (head + 1) * HEAD)
        grad = do_ref[span, :].astype(F32) * real
        low_ref[span, :] = grad.astype(BF16)
        dots_ref[head : head + 1, :] = jnp.sum(
            grad * o_ref[span, :].astype(F32), axis=0, keepdims=True
        )
    acc_ref[...] = jnp.zeros(acc_ref.shape, F32)

    def one_block(block, carry):
        rows = pl.ds(pl.multiple_of(block * TOK_DEV, TOK_DEV), TOK_DEV)

        @pl.when(need_ref[block] == 0)
        def _():
            dkv_ref[rows, :] = jnp.zeros((TOK_DEV, 2 * KV_HEADS * HEAD), BF16)

        @pl.when(need_ref[block] > 0)
        def _():
            bias_ref[...] = block_bias(kinfo_ref, qinfo_ref, rows)
            for group in range(KV_HEADS):
                key_cols = slice(group * HEAD, (group + 1) * HEAD)
                value_cols = slice((KV_HEADS + group) * HEAD, (KV_HEADS + group + 1) * HEAD)
                key = kv_ref[rows, key_cols]
                value = kv_ref[rows, value_cols]
                key_t = key.T
                key_grad = jnp.zeros((TOK_DEV, HEAD), F32)
                value_grad = jnp.zeros((TOK_DEV, HEAD), F32)
                for head in range(group * GROUP, (group + 1) * GROUP):
                    span = slice(head * HEAD, (head + 1) * HEAD)
                    query, grad = q_ref[span, :], low_ref[span, :]
                    scores = dot(key, query, 1, 0) * (SCALE * LOG2E) + bias_ref[...]
                    probs = jnp.exp2(scores - lse_ref[head : head + 1, :])
                    prob_grad = dot(value, grad, 1, 0)
                    score_grad = (probs * (prob_grad - dots_ref[head : head + 1, :])).astype(BF16)
                    acc_ref[span, :] += dot(key_t, score_grad, 1, 0)
                    key_grad += dot(score_grad, query, 1, 1)
                    value_grad += dot(probs.astype(BF16), grad, 1, 1)
                dkv_ref[rows, key_cols] = (key_grad * SCALE).astype(BF16)
                dkv_ref[rows, value_cols] = value_grad.astype(BF16)

        return carry

    lax.fori_loop(0, blocks, one_block, 0)
    cosine, sine = cos_ref[...], sin_ref[...]
    half = HEAD // 2
    for head in range(HEADS):
        start = head * HEAD
        whole = (acc_ref[start : start + HEAD, :] * SCALE).astype(BF16).astype(F32)
        first, second = whole[:half], whole[half:]
        turned = jnp.concatenate(
            [first * cosine + second * sine, second * cosine - first * sine], axis=0
        )
        dq_ref[:, start : start + HEAD] = turned.T.astype(BF16)


def vmem_specs(count):
    return [pl.BlockSpec(memory_space=pltpu.VMEM)] * count


def attention_forward(need, kinfo, qinfo, query_t, kv_all):
    rows = query_t.shape[1]
    return pl.pallas_call(
        attn_fwd_kernel,
        out_shape=(
            jax.ShapeDtypeStruct((HEADS * HEAD, rows), BF16),
            jax.ShapeDtypeStruct((16, rows), F32),
        ),
        in_specs=[pl.BlockSpec(memory_space=pltpu.SMEM)] + vmem_specs(4),
        out_specs=tuple(vmem_specs(2)),
        scratch_shapes=[
            pltpu.VMEM((16, rows), F32),
            pltpu.VMEM((16, rows), F32),
            pltpu.VMEM((HEADS * HEAD, rows), F32),
            pltpu.VMEM((TOK_DEV, rows), F32),
        ],
        compiler_params=pltpu.CompilerParams(vmem_limit_bytes=VMEM_LIMIT),
        cost_estimate=SMALL,
    )(need, kinfo, qinfo, query_t, kv_all)


def attention_backward(need, kinfo, qinfo, cos_t, sin_t, query_t, kv_all, out_t, grad_t, lse):
    rows = query_t.shape[1]
    return pl.pallas_call(
        attn_bwd_kernel,
        out_shape=(
            jax.ShapeDtypeStruct((rows, HEADS * HEAD), BF16),
            jax.ShapeDtypeStruct(kv_all.shape, BF16),
        ),
        in_specs=[pl.BlockSpec(memory_space=pltpu.SMEM)] + vmem_specs(9),
        out_specs=tuple(vmem_specs(2)),
        scratch_shapes=[
            pltpu.VMEM((16, rows), F32),
            pltpu.VMEM((HEADS * HEAD, rows), F32),
            pltpu.VMEM((TOK_DEV, rows), F32),
            pltpu.VMEM((HEADS * HEAD, rows), BF16),
        ],
        compiler_params=pltpu.CompilerParams(vmem_limit_bytes=VMEM_LIMIT),
        cost_estimate=SMALL,
    )(need, kinfo, qinfo, cos_t, sin_t, query_t, kv_all, out_t, grad_t, lse)


def ffn_kernel(cols, first, with_grad, *refs):
    mid_near, mid_far, cot_near, cot_far, w_ref = refs[:5]
    refs = refs[5:]
    if not first:
        mid_sums, out_sums = refs[:2], refs[2:4]
        refs = refs[4:]
    mid_outs, out_outs = refs[:2], refs[2:4]
    if with_grad:
        grad_ref, act_ref, acc_ref, mid_ref, cot_ref = refs[4:]
    else:
        act_ref, mid_ref, cot_ref = refs[4:]
    step, last = pl.program_id(0), pl.num_programs(0) - 1
    near = step < pl.num_programs(0) // 2
    mid_ref[...] = jnp.where(near, mid_near[...], mid_far[...])
    cot_ref[...] = jnp.where(near, cot_near[...], cot_far[...])
    both = dot(mid_ref[...], w_ref[:, : 2 * cols], 1, 0)
    hidden_grad = dot(cot_ref[...], w_ref[:, 2 * cols :], 1, 0)
    gate, up = both[:, :cols], both[:, cols:]
    share = 1.0 / (1.0 + jnp.exp(-gate))
    acted = gate * share
    act_ref[:, :cols] = (hidden_grad * up * (share * (1.0 + gate * (1.0 - share)))).astype(BF16)
    act_ref[:, cols : 2 * cols] = (hidden_grad * acted).astype(BF16)
    act_ref[:, 2 * cols :] = (acted * up).astype(BF16)
    mid_grad = dot(act_ref[:, : 2 * cols], w_ref[:, : 2 * cols], 1, 1)
    out = dot(act_ref[:, 2 * cols :], w_ref[:, 2 * cols :], 1, 1)
    if not first:
        mid_grad = mid_grad + jnp.where(near, mid_sums[0][...], mid_sums[1][...]).astype(F32)
        out = out + jnp.where(near, out_sums[0][...], out_sums[1][...]).astype(F32)

    @pl.when(near)
    def _():
        mid_outs[0][...] = mid_grad.astype(BF16)
        out_outs[0][...] = out.astype(BF16)

    @pl.when(jnp.logical_not(near))
    def _():
        mid_outs[1][...] = mid_grad.astype(BF16)
        out_outs[1][...] = out.astype(BF16)

    if with_grad:

        @pl.when(step == 0)
        def _():
            acc_ref[:, : 2 * cols] = dot(mid_ref[...], act_ref[:, : 2 * cols], 0, 0)
            acc_ref[:, 2 * cols :] = dot(cot_ref[...], act_ref[:, 2 * cols :], 0, 0)

        @pl.when(step > 0)
        def _():
            acc_ref[:, : 2 * cols] += dot(mid_ref[...], act_ref[:, : 2 * cols], 0, 0)
            acc_ref[:, 2 * cols :] += dot(cot_ref[...], act_ref[:, 2 * cols :], 0, 0)

        @pl.when(step == last)
        def _():
            grad_ref[...] = acc_ref[...].astype(BF16)


def feed_forward(mid_halves, cot_halves, weights, sums, with_grad):
    half_tokens, width = mid_halves[0].shape
    cols = weights.shape[1] // 3
    half = half_tokens // TOK_DEV
    near_spec = pl.BlockSpec((TOK_DEV, width), lambda i: (jnp.minimum(i, half - 1), 0))
    far_spec = pl.BlockSpec((TOK_DEV, width), lambda i: (jnp.maximum(i - half, 0), 0))
    act_spec = pl.BlockSpec((TOK_DEV, 3 * cols), lambda i: (i, 0))
    once = pl.BlockSpec(weights.shape, lambda i: (0, 0), pipeline_mode=pl.Buffered(1))
    row_shape = jax.ShapeDtypeStruct((half_tokens, width), BF16)
    row_scratch = [pltpu.VMEM((TOK_DEV, width), BF16)] * 2
    if with_grad:
        last_shape, last_spec = jax.ShapeDtypeStruct(weights.shape, BF16), once
        scratch = [pltpu.VMEM((TOK_DEV, 3 * cols), BF16), pltpu.VMEM(weights.shape, F32)]
    else:
        last_shape, last_spec = jax.ShapeDtypeStruct((2 * half_tokens, 3 * cols), BF16), act_spec
        scratch = []
    return pl.pallas_call(
        functools.partial(ffn_kernel, cols, not sums, with_grad),
        grid=(2 * half,),
        out_shape=(row_shape,) * 4 + (last_shape,),
        in_specs=[near_spec, far_spec] * 2 + [once] + [near_spec, far_spec] * (len(sums) // 2),
        out_specs=(near_spec, far_spec) * 2 + (last_spec,),
        scratch_shapes=scratch + row_scratch,
        compiler_params=pltpu.CompilerParams(vmem_limit_bytes=VMEM_LIMIT),
        cost_estimate=SMALL,
    )(*mid_halves, *cot_halves, weights, *sums)


def ffn_grad_kernel(cols, mid_near, mid_far, cot_near, cot_far, act_ref, grad_ref):
    half = mid_near.shape[0]
    for near, far, part in (
        (mid_near, mid_far, slice(0, 2 * cols)),
        (cot_near, cot_far, slice(2 * cols, 3 * cols)),
    ):
        grad_ref[:, part] = (
            dot(near[...], act_ref[:half, part], 0, 0) + dot(far[...], act_ref[half:, part], 0, 0)
        ).astype(BF16)


def feed_forward_grad(mid_halves, cot_halves, act):
    half_tokens, width = mid_halves[0].shape
    cols = act.shape[1] // 3
    tile = 512 if width % 512 == 0 else width
    col_spec = pl.BlockSpec((half_tokens, tile), lambda i: (0, i))
    return pl.pallas_call(
        functools.partial(ffn_grad_kernel, cols),
        grid=(width // tile,),
        out_shape=jax.ShapeDtypeStruct((width, 3 * cols), BF16),
        in_specs=[col_spec] * 4
        + [pl.BlockSpec(act.shape, lambda i: (0, 0), pipeline_mode=pl.Buffered(1))],
        out_specs=pl.BlockSpec((tile, 3 * cols), lambda i: (i, 0)),
        compiler_params=pltpu.CompilerParams(vmem_limit_bytes=VMEM_LIMIT),
        cost_estimate=SMALL,
    )(*mid_halves, *cot_halves, act)


def slice_moves(n_plane, chunks, cols, total):
    for device in range(n_plane):
        for chunk in range(chunks):
            start = (device * chunks + chunk) * cols
            for kind in range(3):
                yield device, chunk, kind, kind * total + start, max(0, min(cols, total - start))


def pack_kernel(moves, cols, w_ref, out_ref):
    rows = w_ref.shape[0]
    for device, chunk, kind, source, real in moves:
        there = slice(device * rows, (device + 1) * rows)
        at = (chunk * 3 + kind) * cols
        if real:
            out_ref[there, at : at + real] = w_ref[:, source : source + real]
        if real < cols:
            out_ref[there, at + real : at + cols] = jnp.zeros((rows, cols - real), BF16)


def unpack_kernel(moves, cols, *refs):
    chunk_refs, out_ref = refs[:-1], refs[-1]
    rows = out_ref.shape[0]
    for device, chunk, kind, source, real in moves:
        if real:
            block = chunk_refs[chunk][
                device * rows : (device + 1) * rows, kind * cols : kind * cols + real
            ]
            out_ref[:, source : source + real] = block.astype(F32)


def pack_slices(w_mlp, n_plane, chunks, cols):
    rows, total = w_mlp.shape[0], w_mlp.shape[1] // 3
    if rows % 16:
        wide = jnp.pad(
            w_mlp.reshape(rows, 3, total), ((0, 0), (0, 0), (0, n_plane * chunks * cols - total))
        )
        wide = wide.reshape(rows, 3, n_plane, chunks, cols).transpose(2, 0, 3, 1, 4)
        return wide.reshape(n_plane * rows, 3 * chunks * cols)
    moves = list(slice_moves(n_plane, chunks, cols, total))
    return pl.pallas_call(
        functools.partial(pack_kernel, moves, cols),
        out_shape=jax.ShapeDtypeStruct((n_plane * rows, 3 * chunks * cols), BF16),
        in_specs=vmem_specs(1),
        out_specs=vmem_specs(1)[0],
        compiler_params=pltpu.CompilerParams(vmem_limit_bytes=VMEM_LIMIT),
        cost_estimate=SMALL,
    )(w_mlp)


def unpack_slices(chunk_arrays, rows, total, n_plane, cols):
    chunks = len(chunk_arrays)
    if rows % 16:
        stacked = jnp.stack(chunk_arrays, axis=0).reshape(chunks, n_plane, rows, 3, cols)
        stacked = stacked.transpose(2, 3, 1, 0, 4).reshape(rows, 3, -1)[:, :, :total]
        return stacked.reshape(rows, 3 * total).astype(F32)
    moves = list(slice_moves(n_plane, chunks, cols, total))
    return pl.pallas_call(
        functools.partial(unpack_kernel, moves, cols),
        out_shape=jax.ShapeDtypeStruct((rows, 3 * total), F32),
        in_specs=vmem_specs(chunks),
        out_specs=vmem_specs(1)[0],
        compiler_params=pltpu.CompilerParams(vmem_limit_bytes=VMEM_LIMIT),
        cost_estimate=SMALL,
    )(*chunk_arrays)


def after(array, *others):
    return lax.optimization_barrier((array, *others))[0]


class Plane:
    def __init__(self):
        ctx, uly = lax.axis_size("ctx"), lax.axis_size("uly")
        self.count = ctx * uly
        assert self.count & (self.count - 1) == 0 and ctx % 2 == 0
        self.me = lax.axis_index("ctx") * uly + lax.axis_index("uly")
        self.core = uly
        near = [1 << i for i in range(uly.bit_length() - 1)]
        far = [self.core << i for i in range(1, (ctx // 2).bit_length())]
        self.orders = (far + near, near + far)
        self.steps = len(near) + len(far)
        mine = (self.me // self.core) % 2 == 0
        masks = [[0], [0]]
        for which in (0, 1):
            for bit in self.orders[which]:
                masks[which] += [bit | mask for mask in masks[which]]
        pairs = list(zip(masks[0], masks[1]))
        near_slots = [jnp.where(mine, a, b) for a, b in pairs]
        far_slots = [jnp.where(mine, b, a) | self.core for a, b in pairs]
        self.devices = [self.me ^ mask for mask in near_slots + far_slots]

    def swap(self, array, step):
        pairs = []
        for i in range(self.count):
            if step == self.steps:
                bit = self.core
            else:
                bit = self.orders[(i // self.core) % 2][step]
            pairs.append((i, i ^ bit))
        return lax.ppermute(array, PLANE, pairs)

    def gather_step(self, held, step):
        return held + [self.swap(piece, step) for piece in held]

    def gather(self, rows):
        held = [rows]
        for step in range(self.steps + 1):
            held = self.gather_step(held, step)
        return held

    def gather_halves(self, held):
        near = jnp.concatenate(held, axis=0)
        return near, self.swap(near, self.steps)

    def fold(self, near, far, step):
        return (near.astype(F32) + self.swap(far, step).astype(F32)).astype(BF16)

    def fold_rest(self, rows, step):
        half = rows.shape[0] // 2
        return self.fold(rows[:half], rows[half:], step)

    def reduce_step(self, held, step):
        kept = len(held) // 2
        moved = [self.swap(piece, step) for piece in held[kept:]]
        return [
            (one.astype(F32) + other.astype(F32)).astype(BF16) for one, other in zip(held, moved)
        ]

    def reduce(self, blocks):
        held = list(blocks)
        for step in range(self.steps, -1, -1):
            held = self.reduce_step(held, step)
        return held[0]


def place_info(spans, row_in_span, length_row):
    places = spans * TOK_DEV + row_in_span
    begins = jnp.zeros_like(places)
    end = jnp.int32(0)
    for doc in range(length_row.shape[0]):
        end = end + length_row[doc]
        begins = jnp.where(places >= end, jnp.maximum(begins, end), begins)
    return places, begins


def inverse_rms(values):
    return lax.rsqrt(jnp.mean(values * values, axis=-1, keepdims=True) + NORM_EPS)


def norm_backward(values, inverse, scaled):
    return inverse * scaled - values * (
        inverse**3 * jnp.mean(scaled * values, axis=-1, keepdims=True)
    )


def turn(heads, cosine, sine):
    half = HEAD // 2
    first, second = heads[..., :half], heads[..., half:]
    return jnp.concatenate(
        [first * cosine - second * sine, second * cosine + first * sine], axis=-1
    )


def shards(
    layer_input,
    span_order,
    doc_lengths,
    pad_mask,
    w_qkv,
    b_qkv,
    w_out,
    norm_gain_attn,
    norm_gain_mlp,
    w_mlp,
    cotangent,
):
    tok_rows, width = layer_input.shape
    n_dp = lax.axis_size("dp")
    n_plane = lax.axis_size("ctx") * lax.axis_size("uly")
    n_all = n_dp * n_plane
    plane = Plane()
    order_row, length_row, mask_row = span_order[0], doc_lengths[0], pad_mask[0]
    ffn_width = w_mlp.shape[1] // 3
    local_rows = w_mlp.shape[0]
    zone = local_rows * n_plane
    q_width, kv_width = HEADS * HEAD, KV_HEADS * HEAD
    qkv_width = q_width + 2 * kv_width
    bias_rows = b_qkv.shape[0]
    slice_tiles = -(-(ffn_width // LANES) // n_plane)
    chunks = max(c for c in (1, 2, 3) if slice_tiles % c == 0)
    chunk_cols = slice_tiles // chunks * LANES
    w_cols = qkv_width + LANES

    def swap_rows(array):
        return lax.all_to_all(array, PLANE, split_axis=0, concat_axis=0, tiled=True)

    def zone_gather(array):
        return lax.all_gather(array, "dp", axis=0, tiled=True)

    def zone_sum(array):
        return lax.psum_scatter(array, "dp", scatter_dimension=0, tiled=True)

    def whole_rows(pieces):
        cols = pieces[0].shape[1]
        full = jnp.zeros((n_dp, n_plane, local_rows, cols), BF16)
        for device, piece in zip(plane.devices, pieces):
            piece = piece.reshape(n_dp, 1, local_rows, cols)
            full = lax.dynamic_update_slice(full, piece, (0, device, 0, 0))
        return full.reshape(n_all * local_rows, cols)

    def device_blocks(array):
        cols = array.shape[1]
        full = array.reshape(n_dp, n_plane, local_rows, cols)
        return [
            lax.dynamic_slice_in_dim(full, device, 1, 1).reshape(n_dp * local_rows, cols)
            for device in plane.devices
        ]

    side = jnp.concatenate(
        [
            norm_gain_attn[:, None],
            norm_gain_mlp[:, None],
            jnp.zeros((local_rows, 62), BF16),
            jnp.pad(b_qkv[None, :], ((0, local_rows - 1), (0, 64 - bias_rows))),
        ],
        axis=1,
    )
    attn_local = jnp.concatenate([w_qkv, side, w_out.T], axis=1)
    attn_zone = zone_gather(attn_local)

    row_in_span = jnp.arange(tok_rows, dtype=jnp.int32)
    stored_block = jnp.stack(plane.devices)
    spans = order_row[stored_block]
    own_place, own_begin = place_info(spans[0], row_in_span, length_row)
    flags = mask_row.reshape(n_plane, tok_rows)[stored_block]
    key_place = spans[:, None] * TOK_DEV + row_in_span[None, :]
    kinfo = jnp.stack(
        [jnp.where(flags == 1, key_place, FAR).reshape(-1), key_place.reshape(-1)], axis=1
    )
    qinfo = jnp.concatenate(
        [
            own_place[None],
            own_begin[None],
            flags[0][None],
            jnp.zeros((5, tok_rows), jnp.int32),
        ],
        axis=0,
    )
    need = ((spans <= spans[0]) & ((spans + 1) * TOK_DEV > own_begin[0])).astype(jnp.int32)

    inner = (own_place - own_begin).astype(F32)
    half = HEAD // 2
    frequency = ROPE_BASE ** (-(jnp.arange(half, dtype=F32) * 2.0) / HEAD)
    angles_t = frequency[:, None] * inner[None, :]
    cos_t, sin_t = jnp.cos(angles_t), jnp.sin(angles_t)
    cos_r, sin_r = cos_t.T[:, None, :], sin_t.T[:, None, :]

    packed = pack_slices(after(w_mlp, attn_local, kinfo, qinfo), n_plane, chunks, chunk_cols)
    chunk_width = 3 * chunk_cols
    mlp_zone = swap_rows(packed)
    mlp_weights = [
        zone_gather(mlp_zone[:, chunk * chunk_width : (chunk + 1) * chunk_width])
        for chunk in range(chunks)
    ]

    qkv_held = plane.gather(attn_zone[:, :w_cols])
    w_qkv_all = whole_rows(qkv_held)
    side_all = w_qkv_all[:, qkv_width:].astype(F32)
    gain_attn = side_all[:, 0]
    gain_mlp = side_all[:, 1]
    bias_all = side_all.reshape(n_all, local_rows, LANES)[:, 0, 64 : 64 + bias_rows].reshape(-1)

    inputs = layer_input.astype(F32)
    in_inverse = inverse_rms(inputs)
    normed_in = (inputs * in_inverse * gain_attn).astype(BF16)

    kv_proj = dot(normed_in, w_qkv_all[:, q_width:qkv_width], 1, 0) + bias_all[q_width:]
    key_own = turn(kv_proj[:, :kv_width].reshape(tok_rows, KV_HEADS, HEAD), cos_r, sin_r)
    kv_own = jnp.concatenate([key_own.reshape(tok_rows, kv_width), kv_proj[:, kv_width:]], axis=1)
    kv_pieces = plane.gather(kv_own.astype(BF16))
    kv_all = jnp.concatenate(kv_pieces, axis=0)
    w_out_all = whole_rows(plane.gather(after(attn_zone[:, w_cols:], qkv_held[n_plane // 2 - 1])))

    q_proj = dot(w_qkv_all[:, :q_width], normed_in, 0, 1) + bias_all[:q_width, None]
    q_heads = q_proj.reshape(HEADS, 2, half, tok_rows)
    q_first, q_second = q_heads[:, 0], q_heads[:, 1]
    query_t = (
        jnp.stack(
            [q_first * cos_t - q_second * sin_t, q_second * cos_t + q_first * sin_t], axis=1
        )
        .reshape(q_width, tok_rows)
        .astype(BF16)
    )
    attended_t, lse = attention_forward(need, kinfo, qinfo, query_t, kv_all)

    middle = inputs + dot(attended_t, w_out_all, 0, 1)
    mid_inverse = inverse_rms(middle)
    normed_mid = (middle * mid_inverse * gain_mlp).astype(BF16)

    mid_held, cot_held = [normed_mid], [after(cotangent, attended_t)]
    for step in range(plane.steps):
        mid_held = plane.gather_step(mid_held, step)
        cot_held = plane.gather_step(cot_held, step)
    mid_halves = plane.gather_halves(mid_held)
    cot_halves = plane.gather_halves(cot_held)
    sums, chunk_grads = (), []
    for chunk, weights in enumerate(mlp_weights):
        last = chunk == chunks - 1
        *sums, extra = feed_forward(mid_halves, cot_halves, weights, tuple(sums), not last)
        if not last:
            chunk_grads.append(extra)

    def token_blocks(array):
        return [array[k * tok_rows : (k + 1) * tok_rows] for k in range(n_plane)]

    chunk_sums = [zone_sum(grad) for grad in chunk_grads]
    mid_fold = plane.fold(sums[0], sums[1], plane.steps)
    chunk_grads.append(feed_forward_grad(mid_halves, cot_halves, after(extra, mid_fold)))
    chunk_sums.append(zone_sum(chunk_grads[-1]))
    for step in range(plane.steps - 1, -1, -1):
        half = mid_fold.shape[0] // 2
        kept, sent = mid_fold[:half], mid_fold[half:]
        if step == plane.steps - 1:
            kept = after(kept, chunk_grads[-1])
        mid_fold = plane.fold(kept, sent, step)
    mid_grad = after(mid_fold, *chunk_sums[:-1][:1]).astype(F32)

    out_grad = cotangent.astype(F32)
    gain_mlp_grad = jnp.sum(mid_grad * (middle * mid_inverse), axis=0)
    middle_grad = out_grad + norm_backward(middle, mid_inverse, mid_grad * gain_mlp)
    middle_low = middle_grad.astype(BF16)
    attended_grad_t = dot(w_out_all, middle_low, 0, 1).astype(BF16)
    out_weight_grad = dot(middle_low, attended_t, 0, 1).astype(BF16)
    out_held = plane.reduce_step(device_blocks(out_weight_grad), plane.steps)
    attended_grad_t = after(attended_grad_t, *out_held)
    query_grad, kv_grad = attention_backward(
        need, kinfo, qinfo, cos_t, sin_t, query_t, kv_all, attended_t, attended_grad_t, lse
    )
    kv_back = plane.reduce(token_blocks(kv_grad))
    for step in range(plane.steps - 1, -1, -1):
        out_held = plane.reduce_step(out_held, step)
    out_plane = out_held[0]
    kv_back = after(kv_back, out_plane)
    kv_back = kv_back.astype(F32)
    key_back = turn(kv_back[:, :kv_width].reshape(tok_rows, KV_HEADS, HEAD), cos_r, -sin_r)
    projected_grad = jnp.concatenate(
        [query_grad, key_back.reshape(tok_rows, kv_width).astype(BF16), kv_back[:, kv_width:].astype(BF16)],
        axis=1,
    )
    qkv_weight_grad = dot(normed_in, projected_grad, 0, 0).astype(BF16)
    qkv_held = plane.reduce_step(device_blocks(qkv_weight_grad), plane.steps)
    in_grad = dot(projected_grad, w_qkv_all[:, :qkv_width], 1, 1)
    gain_attn_grad = jnp.sum(in_grad * (inputs * in_inverse), axis=0)
    input_grad = middle_grad + norm_backward(inputs, in_inverse, in_grad * gain_attn)
    qkv_bias_grad = jnp.sum(projected_grad.astype(F32), axis=0)

    def side_row(array):
        array = array.reshape(n_dp, n_plane, 1, -1)
        return jnp.pad(array, ((0, 0), (0, 0), (0, 0), (0, LANES - array.shape[-1])))

    side_grad = jnp.concatenate(
        [side_row(gain_attn_grad), side_row(gain_mlp_grad), side_row(qkv_bias_grad)]
        + [jnp.zeros((n_dp, n_plane, 1, LANES), F32)] * 5,
        axis=2,
    ).astype(BF16)
    side_plane = plane.reduce(
        [
            lax.dynamic_slice_in_dim(side_grad, device, 1, 1).reshape(n_dp * 8, LANES)
            for device in plane.devices
        ]
    )
    side_plane = jnp.pad(
        side_plane.reshape(n_dp, 8, LANES), ((0, 0), (0, local_rows - 8), (0, 0))
    ).reshape(n_dp * local_rows, LANES)
    for step in range(plane.steps - 1, -1, -1):
        qkv_held = plane.reduce_step(qkv_held, step)
    qkv_plane = after(qkv_held[0], *chunk_sums[1:])
    attn_sum = zone_sum(jnp.concatenate([qkv_plane, side_plane, out_plane], axis=1)).astype(F32)
    qkv_sum, grad_out = attn_sum[:, :w_cols], attn_sum[:, w_cols:]

    mlp_out = plane.fold(after(sums[2], qkv_plane), sums[3], plane.steps)
    for step in range(plane.steps - 1, -1, -1):
        mlp_out = plane.fold_rest(mlp_out, step)
    grad_mlp = unpack_slices(
        [swap_rows(array) for array in chunk_sums], local_rows, ffn_width, n_plane, chunk_cols
    )
    block_output = (middle + mlp_out.astype(F32)).astype(BF16)
    return (
        block_output,
        input_grad,
        qkv_sum[:, :qkv_width],
        qkv_sum[2, qkv_width : qkv_width + bias_rows],
        grad_out.T,
        qkv_sum[0, qkv_width : qkv_width + local_rows],
        qkv_sum[1, qkv_width : qkv_width + local_rows],
        grad_mlp,
    )


def solution(mesh):
    rows = P(EVERY, None)
    flat = P(EVERY)
    columns = P(None, EVERY)
    batch = P("dp", None)
    return jax.shard_map(
        shards,
        mesh=mesh,
        in_specs=(rows, batch, batch, batch, rows, flat, columns, flat, flat, rows, rows),
        out_specs=(rows, rows, rows, flat, columns, flat, flat, rows),
        check_vma=False,
    )
```

```python
import functools

import jax
import jax.numpy as jnp
from jax import lax
from jax.experimental import pallas as pl
from jax.experimental.pallas import tpu as pltpu
from jax.sharding import PartitionSpec as P

HEADS = 12
KV_HEADS = 2
HEAD = 128
TOK_DEV = 256
LANES = 128
GROUP = HEADS // KV_HEADS

NORM_EPS = 1e-06
ROPE_BASE = 1000000.0
NEG_FILL = -1e30
LOG2E = 1.4426950408889634
SCALE = HEAD ** (-0.5)
FAR = 1 << 30
PLANE = ("ctx", "uly")
EVERY = ("dp", "ctx", "uly")
VMEM_LIMIT = 56 * 1024 * 1024
SMALL = pl.CostEstimate(flops=1024, bytes_accessed=1024, transcendentals=0)
F32 = jnp.float32
BF16 = jnp.bfloat16


def dot(left, right, left_dim, right_dim):
    return lax.dot_general(
        left, right, (((left_dim,), (right_dim,)), ((), ())), preferred_element_type=F32
    )


def block_bias(kinfo_ref, qinfo_ref, rows):
    info = kinfo_ref[rows, :]
    usable, place = info[:, 0:1], info[:, 1:2]
    q_place, q_begin = qinfo_ref[0:1, :], qinfo_ref[1:2, :]
    allowed = ((usable <= q_place) & (usable >= q_begin)) | (place == q_place)
    return jnp.where(allowed, 0.0, NEG_FILL)


def attn_fwd_kernel(
    need_ref, kinfo_ref, qinfo_ref, q_ref, kv_ref, o_ref, lse_ref, m_ref, l_ref, acc_ref, bias_ref
):
    blocks = kv_ref.shape[0] // TOK_DEV
    m_ref[...] = jnp.full(m_ref.shape, NEG_FILL, F32)
    l_ref[...] = jnp.zeros(l_ref.shape, F32)
    acc_ref[...] = jnp.zeros(acc_ref.shape, F32)

    def one_block(block, carry):
        @pl.when(need_ref[block] > 0)
        def _():
            rows = pl.ds(pl.multiple_of(block * TOK_DEV, TOK_DEV), TOK_DEV)
            bias_ref[...] = block_bias(kinfo_ref, qinfo_ref, rows)
            for group in range(KV_HEADS):
                key = kv_ref[rows, group * HEAD : (group + 1) * HEAD]
                value = kv_ref[rows, (KV_HEADS + group) * HEAD : (KV_HEADS + group + 1) * HEAD]
                value_t = value.T
                for head in range(group * GROUP, (group + 1) * GROUP):
                    span = slice(head * HEAD, (head + 1) * HEAD)
                    scores = dot(key, q_ref[span, :], 1, 0) * (SCALE * LOG2E) + bias_ref[...]
                    old = m_ref[head : head + 1, :]
                    new = jnp.maximum(old, jnp.max(scores, axis=0, keepdims=True))
                    weights = jnp.exp2(scores - new)
                    factor = jnp.exp2(old - new)
                    m_ref[head : head + 1, :] = new
                    l_ref[head : head + 1, :] = l_ref[head : head + 1, :] * factor + jnp.sum(
                        weights, axis=0, keepdims=True
                    )
                    acc_ref[span, :] = acc_ref[span, :] * factor + dot(
                        value_t, weights.astype(BF16), 1, 0
                    )

        return carry

    lax.fori_loop(0, blocks, one_block, 0)
    real = qinfo_ref[2:3, :].astype(F32)
    lse_ref[...] = jnp.zeros(lse_ref.shape, F32)
    for head in range(HEADS):
        span = slice(head * HEAD, (head + 1) * HEAD)
        total = l_ref[head : head + 1, :]
        o_ref[span, :] = (acc_ref[span, :] * (real / total)).astype(BF16)
        lse_ref[head : head + 1, :] = m_ref[head : head + 1, :] + jnp.log(total) * LOG2E


def attn_bwd_kernel(
    need_ref,
    kinfo_ref,
    qinfo_ref,
    cos_ref,
    sin_ref,
    q_ref,
    kv_ref,
    o_ref,
    do_ref,
    lse_ref,
    dq_ref,
    near_ref,
    far_ref,
    dots_ref,
    acc_ref,
    bias_ref,
    low_ref,
):
    blocks = kv_ref.shape[0] // TOK_DEV
    real = qinfo_ref[2:3, :].astype(F32)
    for head in range(HEADS):
        span = slice(head * HEAD, (head + 1) * HEAD)
        grad = do_ref[span, :].astype(F32) * real
        low_ref[span, :] = grad.astype(BF16)
        dots_ref[head : head + 1, :] = jnp.sum(
            grad * o_ref[span, :].astype(F32), axis=0, keepdims=True
        )
    acc_ref[...] = jnp.zeros(acc_ref.shape, F32)

    def one_block(dkv_ref, first, at, carry):
        block = first + at
        rows = pl.ds(pl.multiple_of(block * TOK_DEV, TOK_DEV), TOK_DEV)
        out_rows = pl.ds(pl.multiple_of(at * TOK_DEV, TOK_DEV), TOK_DEV)

        @pl.when(need_ref[block] == 0)
        def _():
            dkv_ref[out_rows, :] = jnp.zeros((TOK_DEV, 2 * KV_HEADS * HEAD), BF16)

        @pl.when(need_ref[block] > 0)
        def _():
            bias_ref[...] = block_bias(kinfo_ref, qinfo_ref, rows)
            for group in range(KV_HEADS):
                key_cols = slice(group * HEAD, (group + 1) * HEAD)
                value_cols = slice((KV_HEADS + group) * HEAD, (KV_HEADS + group + 1) * HEAD)
                key = kv_ref[rows, key_cols]
                value = kv_ref[rows, value_cols]
                key_t = key.T
                key_grad = jnp.zeros((TOK_DEV, HEAD), F32)
                value_grad = jnp.zeros((TOK_DEV, HEAD), F32)
                for head in range(group * GROUP, (group + 1) * GROUP):
                    span = slice(head * HEAD, (head + 1) * HEAD)
                    query, grad = q_ref[span, :], low_ref[span, :]
                    scores = dot(key, query, 1, 0) * (SCALE * LOG2E) + bias_ref[...]
                    probs = jnp.exp2(scores - lse_ref[head : head + 1, :])
                    prob_grad = dot(value, grad, 1, 0)
                    score_grad = (probs * (prob_grad - dots_ref[head : head + 1, :])).astype(BF16)
                    acc_ref[span, :] += dot(key_t, score_grad, 1, 0)
                    key_grad += dot(score_grad, query, 1, 1)
                    value_grad += dot(probs.astype(BF16), grad, 1, 1)
                dkv_ref[out_rows, key_cols] = (key_grad * SCALE).astype(BF16)
                dkv_ref[out_rows, value_cols] = value_grad.astype(BF16)

        return carry

    half_blocks = blocks // 2
    lax.fori_loop(0, half_blocks, functools.partial(one_block, near_ref, 0), 0)
    lax.fori_loop(0, half_blocks, functools.partial(one_block, far_ref, half_blocks), 0)
    cosine, sine = cos_ref[...], sin_ref[...]
    half = HEAD // 2
    for head in range(HEADS):
        start = head * HEAD
        whole = (acc_ref[start : start + HEAD, :] * SCALE).astype(BF16).astype(F32)
        first, second = whole[:half], whole[half:]
        turned = jnp.concatenate(
            [first * cosine + second * sine, second * cosine - first * sine], axis=0
        )
        dq_ref[:, start : start + HEAD] = turned.T.astype(BF16)


def vmem_specs(count):
    return [pl.BlockSpec(memory_space=pltpu.VMEM)] * count


def attention_forward(need, kinfo, qinfo, query_t, kv_all):
    rows = query_t.shape[1]
    return pl.pallas_call(
        attn_fwd_kernel,
        out_shape=(
            jax.ShapeDtypeStruct((HEADS * HEAD, rows), BF16),
            jax.ShapeDtypeStruct((16, rows), F32),
        ),
        in_specs=[pl.BlockSpec(memory_space=pltpu.SMEM)] + vmem_specs(4),
        out_specs=tuple(vmem_specs(2)),
        scratch_shapes=[
            pltpu.VMEM((16, rows), F32),
            pltpu.VMEM((16, rows), F32),
            pltpu.VMEM((HEADS * HEAD, rows), F32),
            pltpu.VMEM((TOK_DEV, rows), F32),
        ],
        compiler_params=pltpu.CompilerParams(vmem_limit_bytes=VMEM_LIMIT),
        cost_estimate=SMALL,
    )(need, kinfo, qinfo, query_t, kv_all)


def attention_backward(need, kinfo, qinfo, cos_t, sin_t, query_t, kv_all, out_t, grad_t, lse):
    rows = query_t.shape[1]
    return pl.pallas_call(
        attn_bwd_kernel,
        out_shape=(
            jax.ShapeDtypeStruct((rows, HEADS * HEAD), BF16),
            jax.ShapeDtypeStruct((kv_all.shape[0] // 2, kv_all.shape[1]), BF16),
            jax.ShapeDtypeStruct((kv_all.shape[0] // 2, kv_all.shape[1]), BF16),
        ),
        in_specs=[pl.BlockSpec(memory_space=pltpu.SMEM)] + vmem_specs(9),
        out_specs=tuple(vmem_specs(3)),
        scratch_shapes=[
            pltpu.VMEM((16, rows), F32),
            pltpu.VMEM((HEADS * HEAD, rows), F32),
            pltpu.VMEM((TOK_DEV, rows), F32),
            pltpu.VMEM((HEADS * HEAD, rows), BF16),
        ],
        compiler_params=pltpu.CompilerParams(vmem_limit_bytes=VMEM_LIMIT),
        cost_estimate=SMALL,
    )(need, kinfo, qinfo, cos_t, sin_t, query_t, kv_all, out_t, grad_t, lse)


def ffn_tile(cols, mid_ref, cot_ref, w_ref, sums, outs, act_ref, acc_ref):
    both = dot(mid_ref[...], w_ref[:, : 2 * cols], 1, 0)
    hidden_grad = dot(cot_ref[...], w_ref[:, 2 * cols :], 1, 0)
    gate, up = both[:, :cols], both[:, cols:]
    share = 1.0 / (1.0 + jnp.exp(-gate))
    acted = gate * share
    act_ref[:, :cols] = (hidden_grad * up * (share * (1.0 + gate * (1.0 - share)))).astype(BF16)
    act_ref[:, cols : 2 * cols] = (hidden_grad * acted).astype(BF16)
    act_ref[:, 2 * cols :] = (acted * up).astype(BF16)
    mid_grad = dot(act_ref[:, : 2 * cols], w_ref[:, : 2 * cols], 1, 1)
    out = dot(act_ref[:, 2 * cols :], w_ref[:, 2 * cols :], 1, 1)
    if sums:
        mid_grad = mid_grad + sums[0][...].astype(F32)
        out = out + sums[1][...].astype(F32)
    outs[0][...] = mid_grad.astype(BF16)
    outs[1][...] = out.astype(BF16)
    if acc_ref is not None:
        acc_ref[:, : 2 * cols] += dot(mid_ref[...], act_ref[:, : 2 * cols], 0, 0)
        acc_ref[:, 2 * cols :] += dot(cot_ref[...], act_ref[:, 2 * cols :], 0, 0)


def ffn_kernel(cols, first, with_grad, *refs):
    mids, cots, w_ref, refs = refs[:2], refs[2:4], refs[4], refs[5:]
    mid_sums = out_sums = None
    if not first:
        mid_sums, out_sums, refs = refs[:2], refs[2:4], refs[4:]
    mid_outs, out_outs, refs = refs[:2], refs[2:4], refs[4:]
    if with_grad:
        grad_ref, act_ref, acc_ref = refs
    else:
        (act_ref,), acc_ref = refs, None
    step, last = pl.program_id(0), pl.num_programs(0) - 1
    near = step < pl.num_programs(0) // 2

    if with_grad:

        @pl.when(step == 0)
        def _():
            acc_ref[...] = jnp.zeros(acc_ref.shape, F32)

    def tile(which):
        sums = () if first else (mid_sums[which], out_sums[which])
        outs = (mid_outs[which], out_outs[which])
        ffn_tile(cols, mids[which], cots[which], w_ref, sums, outs, act_ref, acc_ref)

    pl.when(near)(lambda: tile(0))
    pl.when(jnp.logical_not(near))(lambda: tile(1))

    if with_grad:

        @pl.when(step == last)
        def _():
            grad_ref[...] = acc_ref[...].astype(BF16)


def feed_forward(mid_halves, cot_halves, weights, sums, with_grad):
    half_tokens, width = mid_halves[0].shape
    cols = weights.shape[1] // 3
    half = half_tokens // TOK_DEV
    near_spec = pl.BlockSpec((TOK_DEV, width), lambda i: (jnp.minimum(i, half - 1), 0))
    far_spec = pl.BlockSpec((TOK_DEV, width), lambda i: (jnp.maximum(i - half, 0), 0))
    act_spec = pl.BlockSpec((TOK_DEV, 3 * cols), lambda i: (i, 0))
    once = pl.BlockSpec(weights.shape, lambda i: (0, 0), pipeline_mode=pl.Buffered(1))
    row_shape = jax.ShapeDtypeStruct((half_tokens, width), BF16)
    if with_grad:
        last_shape, last_spec = jax.ShapeDtypeStruct(weights.shape, BF16), once
        scratch = [pltpu.VMEM((TOK_DEV, 3 * cols), BF16), pltpu.VMEM(weights.shape, F32)]
    else:
        last_shape, last_spec = jax.ShapeDtypeStruct((2 * half_tokens, 3 * cols), BF16), act_spec
        scratch = []
    return pl.pallas_call(
        functools.partial(ffn_kernel, cols, not sums, with_grad),
        grid=(2 * half,),
        out_shape=(row_shape,) * 4 + (last_shape,),
        in_specs=[near_spec, far_spec] * 2 + [once] + [near_spec, far_spec] * (len(sums) // 2),
        out_specs=(near_spec, far_spec) * 2 + (last_spec,),
        scratch_shapes=scratch,
        compiler_params=pltpu.CompilerParams(vmem_limit_bytes=VMEM_LIMIT),
        cost_estimate=SMALL,
    )(*mid_halves, *cot_halves, weights, *sums)


def ffn_grad_kernel(cols, mid_near, mid_far, cot_near, cot_far, act_ref, grad_ref):
    half = mid_near.shape[0]
    for near, far, part in (
        (mid_near, mid_far, slice(0, 2 * cols)),
        (cot_near, cot_far, slice(2 * cols, 3 * cols)),
    ):
        grad_ref[:, part] = (
            dot(near[...], act_ref[:half, part], 0, 0) + dot(far[...], act_ref[half:, part], 0, 0)
        ).astype(BF16)


def feed_forward_grad(mid_halves, cot_halves, act):
    half_tokens, width = mid_halves[0].shape
    cols = act.shape[1] // 3
    tile = 512 if width % 512 == 0 else width
    col_spec = pl.BlockSpec((half_tokens, tile), lambda i: (0, i))
    return pl.pallas_call(
        functools.partial(ffn_grad_kernel, cols),
        grid=(width // tile,),
        out_shape=jax.ShapeDtypeStruct((width, 3 * cols), BF16),
        in_specs=[col_spec] * 4
        + [pl.BlockSpec(act.shape, lambda i: (0, 0), pipeline_mode=pl.Buffered(1))],
        out_specs=pl.BlockSpec((tile, 3 * cols), lambda i: (i, 0)),
        compiler_params=pltpu.CompilerParams(vmem_limit_bytes=VMEM_LIMIT),
        cost_estimate=SMALL,
    )(*mid_halves, *cot_halves, act)


def slice_moves(n_plane, chunks, cols, total):
    for device in range(n_plane):
        for chunk in range(chunks):
            start = (device * chunks + chunk) * cols
            for kind in range(3):
                yield device, chunk, kind, kind * total + start, max(0, min(cols, total - start))


def pack_kernel(moves, cols, w_ref, out_ref):
    rows = w_ref.shape[0]
    for device, chunk, kind, source, real in moves:
        there = slice(device * rows, (device + 1) * rows)
        at = (chunk * 3 + kind) * cols
        if real:
            out_ref[there, at : at + real] = w_ref[:, source : source + real]
        if real < cols:
            out_ref[there, at + real : at + cols] = jnp.zeros((rows, cols - real), BF16)


def unpack_kernel(moves, cols, in_ref, out_ref):
    rows = out_ref.shape[0]
    for device, chunk, kind, source, real in moves:
        if real:
            at = (chunk * 3 + kind) * cols
            block = in_ref[device * rows : (device + 1) * rows, at : at + real]
            out_ref[:, source : source + real] = block.astype(F32)


def pack_slices(w_mlp, n_plane, chunks, cols):
    rows, total = w_mlp.shape[0], w_mlp.shape[1] // 3
    if rows % 16:
        wide = jnp.pad(
            w_mlp.reshape(rows, 3, total), ((0, 0), (0, 0), (0, n_plane * chunks * cols - total))
        )
        wide = wide.reshape(rows, 3, n_plane, chunks, cols).transpose(2, 0, 3, 1, 4)
        return wide.reshape(n_plane * rows, 3 * chunks * cols)
    moves = list(slice_moves(n_plane, chunks, cols, total))
    return pl.pallas_call(
        functools.partial(pack_kernel, moves, cols),
        out_shape=jax.ShapeDtypeStruct((n_plane * rows, 3 * chunks * cols), BF16),
        in_specs=vmem_specs(1),
        out_specs=vmem_specs(1)[0],
        compiler_params=pltpu.CompilerParams(vmem_limit_bytes=VMEM_LIMIT),
        cost_estimate=SMALL,
    )(w_mlp)


def unpack_slices(array, rows, total, n_plane, chunks, cols):
    if rows % 16:
        stacked = array.reshape(n_plane, rows, chunks, 3, cols).transpose(1, 3, 0, 2, 4)
        return stacked.reshape(rows, 3, -1)[:, :, :total].reshape(rows, 3 * total).astype(F32)
    moves = list(slice_moves(n_plane, chunks, cols, total))
    return pl.pallas_call(
        functools.partial(unpack_kernel, moves, cols),
        out_shape=jax.ShapeDtypeStruct((rows, 3 * total), F32),
        in_specs=vmem_specs(1),
        out_specs=vmem_specs(1)[0],
        compiler_params=pltpu.CompilerParams(vmem_limit_bytes=VMEM_LIMIT),
        cost_estimate=SMALL,
    )(array)


def weight_grad_kernel(n_dp, local_rows, across, dev_ref, *refs):
    count = len(across)
    lefts, rights = refs[: 2 * count : 2], refs[1 : 2 * count : 2]
    sides, (near_ref, far_ref, turned_ref, block_ref) = refs[2 * count : -4], refs[-4:]
    half = near_ref.shape[0] // (n_dp * local_rows)
    tile = block_ref.shape[1]

    def move(from_ref, at):
        cols = slice(at, at + from_ref.shape[1])
        for slot in range(2 * half):
            out_ref = near_ref if slot < half else far_ref
            for zone in range(n_dp):
                source = (zone * 2 * half + dev_ref[slot]) * local_rows
                source = pl.ds(pl.multiple_of(source, local_rows), local_rows)
                there = ((slot % half) * n_dp + zone) * local_rows
                out_ref[there : there + local_rows, cols] = from_ref[source, :]

    at = 0
    for left, right, is_across in zip(lefts, rights, across):
        turned_ref[...] = left[...].T
        cols = right.shape[0] if is_across else right.shape[1]
        for start in range(0, cols, tile):
            span = slice(start, start + tile)
            if is_across:
                block = dot(turned_ref[...], right[span, :], 1, 1)
            else:
                block = dot(turned_ref[...], right[:, span], 1, 0)
            block_ref[...] = block.astype(BF16)
            move(block_ref, at)
            at += tile
    for side_ref in sides:
        move(side_ref, at)


def weight_grads(plane, local_rows, terms, side=None):
    n_dp = lax.axis_size("dp")
    tokens, width = terms[0][0].shape
    widths = [right.shape[0 if across else 1] for _, right, across in terms]
    if local_rows % 16:
        full = jnp.concatenate(
            [dot(left, right, 0, 1 if across else 0) for left, right, across in terms], axis=1
        ).astype(BF16)
        if side is not None:
            full = jnp.concatenate([full, side], axis=1)
        full = full.reshape(n_dp, plane.count, local_rows, full.shape[1])
        blocks = [
            lax.dynamic_slice_in_dim(full, device, 1, 1).reshape(n_dp * local_rows, -1)
            for device in plane.devices
        ]
        half = plane.count // 2
        return jnp.concatenate(blocks[:half]), jnp.concatenate(blocks[half:])
    tile = 512
    extra = [] if side is None else [side]
    total = sum(widths) + sum(array.shape[1] for array in extra)
    shape = jax.ShapeDtypeStruct((width // 2, total), BF16)
    return pl.pallas_call(
        functools.partial(weight_grad_kernel, n_dp, local_rows, [term[2] for term in terms]),
        out_shape=(shape, shape),
        in_specs=[pl.BlockSpec(memory_space=pltpu.SMEM)]
        + vmem_specs(2 * len(terms) + len(extra)),
        out_specs=tuple(vmem_specs(2)),
        scratch_shapes=[pltpu.VMEM((width, tokens), BF16), pltpu.VMEM((width, tile), BF16)],
        compiler_params=pltpu.CompilerParams(vmem_limit_bytes=VMEM_LIMIT),
        cost_estimate=SMALL,
    )(jnp.stack(plane.devices), *[array for term in terms for array in term[:2]], *extra)


def after(array, *others):
    return lax.optimization_barrier((array, *others))[0]


class Plane:
    def __init__(self):
        ctx, uly = lax.axis_size("ctx"), lax.axis_size("uly")
        self.count = ctx * uly
        assert self.count & (self.count - 1) == 0 and ctx % 2 == 0
        self.me = lax.axis_index("ctx") * uly + lax.axis_index("uly")
        self.core = uly
        near = [1 << i for i in range(uly.bit_length() - 1)]
        far = [self.core << i for i in range(1, (ctx // 2).bit_length())]
        self.orders = (far + near, near + far)
        self.steps = len(near) + len(far)
        mine = (self.me // self.core) % 2 == 0
        masks = [[0], [0]]
        for which in (0, 1):
            for bit in self.orders[which]:
                masks[which] += [bit | mask for mask in masks[which]]
        pairs = list(zip(masks[0], masks[1]))
        near_slots = [jnp.where(mine, a, b) for a, b in pairs]
        far_slots = [jnp.where(mine, b, a) | self.core for a, b in pairs]
        self.devices = [self.me ^ mask for mask in near_slots + far_slots]

    def swap(self, array, step):
        pairs = []
        for i in range(self.count):
            if step == self.steps:
                bit = self.core
            else:
                bit = self.orders[(i // self.core) % 2][step]
            pairs.append((i, i ^ bit))
        return lax.ppermute(array, PLANE, pairs)

    def widen(self, rows, step):
        return jnp.concatenate([rows, self.swap(rows, step)], axis=0)

    def gather(self, rows, late_step=None, *others):
        stages = [rows]
        for step in range(self.steps):
            if step == late_step:
                stages[-1] = after(stages[-1], *others)
            stages.append(self.widen(stages[-1], step))
        return stages + [self.swap(stages[-1], self.steps)]

    def fold(self, near, far, step):
        return (near.astype(F32) + self.swap(far, step).astype(F32)).astype(BF16)

    def fold_rest(self, rows, step):
        half = rows.shape[0] // 2
        return self.fold(rows[:half], rows[half:], step)


def place_info(spans, row_in_span, length_row):
    places = spans * TOK_DEV + row_in_span
    begins = jnp.zeros_like(places)
    end = jnp.int32(0)
    for doc in range(length_row.shape[0]):
        end = end + length_row[doc]
        begins = jnp.where(places >= end, jnp.maximum(begins, end), begins)
    return places, begins


def inverse_rms(values):
    return lax.rsqrt(jnp.mean(values * values, axis=-1, keepdims=True) + NORM_EPS)


def norm_backward(values, inverse, scaled):
    return inverse * scaled - values * (
        inverse**3 * jnp.mean(scaled * values, axis=-1, keepdims=True)
    )


def turn(heads, cosine, sine):
    half = HEAD // 2
    first, second = heads[..., :half], heads[..., half:]
    return jnp.concatenate(
        [first * cosine - second * sine, second * cosine + first * sine], axis=-1
    )


def shards(
    layer_input,
    span_order,
    doc_lengths,
    pad_mask,
    w_qkv,
    b_qkv,
    w_out,
    norm_gain_attn,
    norm_gain_mlp,
    w_mlp,
    cotangent,
):
    tok_rows, width = layer_input.shape
    n_dp = lax.axis_size("dp")
    n_plane = lax.axis_size("ctx") * lax.axis_size("uly")
    n_all = n_dp * n_plane
    plane = Plane()
    ffn_width = w_mlp.shape[1] // 3
    local_rows = w_mlp.shape[0]
    zone = local_rows * n_plane
    q_width, kv_width = HEADS * HEAD, KV_HEADS * HEAD
    qkv_width = q_width + 2 * kv_width
    bias_rows = b_qkv.shape[0]
    slice_tiles = -(-(ffn_width // LANES) // n_plane)
    chunks = max(c for c in (1, 2, 3) if slice_tiles % c == 0)
    chunk_cols = slice_tiles // chunks * LANES
    kv_cols = 2 * kv_width + LANES

    def swap_rows(array):
        return lax.all_to_all(array, PLANE, split_axis=0, concat_axis=0, tiled=True)

    def zone_gather(array):
        return lax.all_gather(array, "dp", axis=0, tiled=True)

    def zone_sum(array):
        return lax.psum_scatter(array, "dp", scatter_dimension=0, tiled=True)

    def whole_rows(pieces):
        cols = pieces[0].shape[1]
        full = jnp.zeros((n_dp, n_plane, local_rows, cols), BF16)
        slots = [block for piece in pieces for block in jnp.split(piece, n_plane // 2)]
        for device, block in zip(plane.devices, slots):
            piece = block.reshape(n_dp, 1, local_rows, cols)
            full = lax.dynamic_update_slice(full, piece, (0, device, 0, 0))
        return full.reshape(n_all * local_rows, cols)

    def device_blocks(array):
        cols = array.shape[1]
        full = array.reshape(n_dp, n_plane, local_rows, cols)
        return [
            lax.dynamic_slice_in_dim(full, device, 1, 1).reshape(n_dp * local_rows, cols)
            for device in plane.devices
        ]

    side = jnp.concatenate(
        [
            norm_gain_attn[:, None],
            norm_gain_mlp[:, None],
            jnp.zeros((local_rows, 62), BF16),
            jnp.pad(b_qkv[None, :], ((0, local_rows - 1), (0, 64 - bias_rows))),
        ],
        axis=1,
    )
    my_dp = lax.axis_index("dp")

    def zone_rows(array):
        full = jnp.zeros((n_dp, *array.shape), BF16)
        for step in range(n_dp):
            moved = array
            if step:
                moved = lax.ppermute(array, "dp", [(i, (i + step) % n_dp) for i in range(n_dp)])
            full = lax.dynamic_update_slice(
                full, moved[None], ((my_dp + n_dp - step) % n_dp, 0, 0)
            )
        return full.reshape(n_dp * array.shape[0], array.shape[1])

    kv_local = jnp.concatenate([w_qkv[:, q_width:], side], axis=1)
    attn_local = jnp.concatenate([kv_local, w_qkv[:, :q_width], w_out.T], axis=1)
    attn_zone = zone_rows(attn_local)
    kv_zone = attn_zone[:, : kv_local.shape[1]]
    big_zone = attn_zone[:, kv_local.shape[1] :]

    packed = pack_slices(after(w_mlp, attn_local), n_plane, chunks, chunk_cols)
    chunk_width = 3 * chunk_cols
    mlp_zone = swap_rows(packed)
    mlp_weights = [
        zone_gather(mlp_zone[:, chunk * chunk_width : (chunk + 1) * chunk_width])
        for chunk in range(chunks)
    ]

    w_kv_stages = plane.gather(kv_zone, 1, mlp_zone)
    w_q_stages = plane.gather(after(big_zone[:, :q_width], w_kv_stages[1]))
    w_out_stages = plane.gather(after(big_zone[:, q_width:], w_q_stages[-2]))

    order_row, length_row, mask_row = after(
        (span_order[0], doc_lengths[0], pad_mask[0]), w_kv_stages[1]
    )
    row_in_span = jnp.arange(tok_rows, dtype=jnp.int32)
    stored_block = jnp.stack(plane.devices)
    spans = order_row[stored_block]
    own_place, own_begin = place_info(spans[0], row_in_span, length_row)
    flags = mask_row.reshape(n_plane, tok_rows)[stored_block]
    key_place = spans[:, None] * TOK_DEV + row_in_span[None, :]
    kinfo = jnp.stack(
        [jnp.where(flags == 1, key_place, FAR).reshape(-1), key_place.reshape(-1)], axis=1
    )
    qinfo = jnp.concatenate(
        [
            own_place[None],
            own_begin[None],
            flags[0][None],
            jnp.zeros((5, tok_rows), jnp.int32),
        ],
        axis=0,
    )
    need = ((spans <= spans[0]) & ((spans + 1) * TOK_DEV > own_begin[0])).astype(jnp.int32)

    inner = (own_place - own_begin).astype(F32)
    half = HEAD // 2
    frequency = ROPE_BASE ** (-(jnp.arange(half, dtype=F32) * 2.0) / HEAD)
    angles_t = frequency[:, None] * inner[None, :]
    cos_t, sin_t = jnp.cos(angles_t), jnp.sin(angles_t)
    cos_r, sin_r = cos_t.T[:, None, :], sin_t.T[:, None, :]

    w_kv_all = whole_rows(w_kv_stages[-2:])
    side_all = w_kv_all[:, 2 * kv_width :].astype(F32)
    gain_attn = side_all[:, 0]
    gain_mlp = side_all[:, 1]
    bias_all = side_all.reshape(n_all, local_rows, LANES)[:, 0, 64 : 64 + bias_rows].reshape(-1)

    inputs = layer_input.astype(F32)
    in_inverse = inverse_rms(inputs)
    normed_in = (inputs * in_inverse * gain_attn).astype(BF16)

    kv_proj = dot(normed_in, w_kv_all[:, : 2 * kv_width], 1, 0) + bias_all[q_width:]
    key_own = turn(kv_proj[:, :kv_width].reshape(tok_rows, KV_HEADS, HEAD), cos_r, sin_r)
    kv_own = jnp.concatenate([key_own.reshape(tok_rows, kv_width), kv_proj[:, kv_width:]], axis=1)
    kv_own = after(kv_own.astype(BF16), w_q_stages[1])
    kv_stages = plane.gather(kv_own, 1, w_out_stages[1])
    kv_all = jnp.concatenate(kv_stages[-2:], axis=0)
    w_q_all = whole_rows(w_q_stages[-2:])
    w_out_all = whole_rows(w_out_stages[-2:])

    q_proj = dot(w_q_all, normed_in, 0, 1) + bias_all[:q_width, None]
    q_heads = q_proj.reshape(HEADS, 2, half, tok_rows)
    q_first, q_second = q_heads[:, 0], q_heads[:, 1]
    query_t = (
        jnp.stack(
            [q_first * cos_t - q_second * sin_t, q_second * cos_t + q_first * sin_t], axis=1
        )
        .reshape(q_width, tok_rows)
        .astype(BF16)
    )
    need = after(need, w_out_stages[-2])
    attended_t, lse = attention_forward(need, kinfo, qinfo, query_t, kv_all)

    middle = inputs + dot(attended_t, w_out_all, 0, 1)
    mid_inverse = inverse_rms(middle)
    normed_mid = (middle * mid_inverse * gain_mlp).astype(BF16)

    cot_stages = plane.gather(after(cotangent, w_out_stages[-2]))
    cot_halves = cot_stages[-2:]
    mid_near = after(normed_mid, cot_stages[1])
    for step in range(plane.steps):
        mid_near = plane.widen(mid_near, step)
    mid_near = after(mid_near, mlp_weights[0])
    mid_halves = mid_near, plane.swap(mid_near, plane.steps)
    sums, chunk_grads = (), []
    for chunk, weights in enumerate(mlp_weights):
        last = chunk == chunks - 1
        *sums, extra = feed_forward(mid_halves, cot_halves, weights, tuple(sums), not last)
        if not last:
            chunk_grads.append(extra)

    def token_blocks(array):
        return [array[k * tok_rows : (k + 1) * tok_rows] for k in range(n_plane)]

    chunk_sums = [zone_sum(grad) for grad in chunk_grads]
    mid_fold = plane.fold(sums[0], sums[1], plane.steps)
    chunk_grads.append(feed_forward_grad(mid_halves, cot_halves, after(extra, mid_fold)))
    chunk_sums.append(zone_sum(chunk_grads[-1]))
    for step in range(plane.steps - 1, -1, -1):
        half = mid_fold.shape[0] // 2
        kept, sent = mid_fold[:half], mid_fold[half:]
        if step == plane.steps - 1:
            kept = after(kept, chunk_grads[-1])
        mid_fold = plane.fold(kept, sent, step)
        if step == 0:
            out_fold = plane.fold(after(sums[2], kept), sums[3], plane.steps)
    mid_grad = after(mid_fold, *chunk_sums[:-1][:1]).astype(F32)

    out_grad = cotangent.astype(F32)
    gain_mlp_grad = jnp.sum(mid_grad * (middle * mid_inverse), axis=0)
    middle_grad = out_grad + norm_backward(middle, mid_inverse, mid_grad * gain_mlp)
    middle_low = middle_grad.astype(BF16)
    attended_grad_t = dot(w_out_all, middle_low, 0, 1).astype(BF16)
    attended_grad_t = after(attended_grad_t, out_fold)
    query_grad, *kv_grads = attention_backward(
        need, kinfo, qinfo, cos_t, sin_t, query_t, kv_all, attended_t, attended_grad_t, lse
    )
    kv_fold = plane.fold(*kv_grads, plane.steps)
    mlp_out = after(out_fold, mid_fold)
    for step in range(plane.steps - 1, 0, -1):
        mlp_out = plane.fold_rest(mlp_out, step)
    big_grads = weight_grads(
        plane,
        local_rows,
        [
            (after(normed_in, mlp_out, kv_fold, *chunk_sums[1:-1]), query_grad, False),
            (middle_low, attended_t, True),
        ],
    )
    big_fold = plane.fold(*big_grads, plane.steps)
    mlp_out = plane.fold_rest(after(mlp_out, kv_fold), 0)
    for step in range(plane.steps - 1, -1, -1):
        kv_fold = plane.fold_rest(kv_fold, step)
    kv_back = after(kv_fold, big_fold, mlp_out)
    kv_back = kv_back.astype(F32)
    key_back = turn(kv_back[:, :kv_width].reshape(tok_rows, KV_HEADS, HEAD), cos_r, -sin_r)
    projected_grad = jnp.concatenate(
        [query_grad, key_back.reshape(tok_rows, kv_width).astype(BF16), kv_back[:, kv_width:].astype(BF16)],
        axis=1,
    )
    in_grad = dot(projected_grad[:, :q_width], w_q_all, 1, 1) + dot(
        projected_grad[:, q_width:], w_kv_all[:, : 2 * kv_width], 1, 1
    )
    gain_attn_grad = jnp.sum(in_grad * (inputs * in_inverse), axis=0)
    input_grad = middle_grad + norm_backward(inputs, in_inverse, in_grad * gain_attn)
    qkv_bias_grad = jnp.sum(projected_grad.astype(F32), axis=0)

    def side_rows(array):
        array = array.reshape(n_dp, n_plane, 1, -1)
        return jnp.pad(array, ((0, 0), (0, 0), (0, 0), (0, LANES - array.shape[-1])))

    side_grad = jnp.concatenate(
        [side_rows(gain_attn_grad), side_rows(gain_mlp_grad), side_rows(qkv_bias_grad)]
        + [jnp.zeros((n_dp, n_plane, 1, LANES), F32)] * 5,
        axis=2,
    )
    side_grad = jnp.pad(side_grad, ((0, 0), (0, 0), (0, local_rows - 8), (0, 0)))
    side_grad = side_grad.reshape(n_all * local_rows, LANES).astype(BF16)
    for step in range(plane.steps - 1, 0, -1):
        big_fold = plane.fold_rest(big_fold, step)
    small_grads = weight_grads(
        plane,
        local_rows,
        [(after(normed_in, big_fold), projected_grad[:, q_width:], False)],
        side_grad,
    )
    big_fold = plane.fold_rest(big_fold, 0)
    small_fold = plane.fold(*small_grads, plane.steps)
    for step in range(plane.steps - 1, -1, -1):
        rows = small_fold.shape[0] // 2
        kept, sent = small_fold[:rows], small_fold[rows:]
        if step == 0:
            kept = after(kept, chunk_sums[-1])
        small_fold = plane.fold(kept, sent, step)
    attn_plane = jnp.concatenate([big_fold, small_fold], axis=1)
    attn_sum = zone_sum(attn_plane).astype(F32)
    kv_at, side_at = q_width + width, qkv_width + width
    grad_qkv = jnp.concatenate([attn_sum[:, :q_width], attn_sum[:, kv_at:side_at]], axis=1)
    side_sum = attn_sum[:, side_at:]

    all_swapped = swap_rows(after(jnp.concatenate(chunk_sums, axis=1), attn_plane))
    grad_mlp = unpack_slices(
        all_swapped, local_rows, ffn_width, n_plane, chunks, chunk_cols
    )
    block_output = (middle + mlp_out.astype(F32)).astype(BF16)
    return (
        block_output,
        input_grad,
        grad_qkv,
        side_sum[2, :bias_rows],
        attn_sum[:, q_width:kv_at].T,
        side_sum[0, :local_rows],
        side_sum[1, :local_rows],
        grad_mlp,
    )


def solution(mesh):
    rows = P(EVERY, None)
    flat = P(EVERY)
    columns = P(None, EVERY)
    batch = P("dp", None)
    return jax.shard_map(
        shards,
        mesh=mesh,
        in_specs=(rows, batch, batch, batch, rows, flat, columns, flat, flat, rows, rows),
        out_specs=(rows, rows, rows, flat, columns, flat, flat, rows),
        check_vma=False,
    )
```

```python
import functools

import jax
import jax.numpy as jnp
from jax import lax
from jax.experimental import pallas as pl
from jax.experimental.pallas import tpu as pltpu
from jax.sharding import PartitionSpec as P

HEADS = 12
KV_HEADS = 2
HEAD = 128
TOK_DEV = 256
LANES = 128
GROUP = HEADS // KV_HEADS

NORM_EPS = 1e-06
ROPE_BASE = 1000000.0
NEG_FILL = -1e30
LOG2E = 1.4426950408889634
SCALE = HEAD ** (-0.5)
FAR = 1 << 30
PLANE = ("ctx", "uly")
EVERY = ("dp", "ctx", "uly")
VMEM_LIMIT = 56 * 1024 * 1024
SMALL = pl.CostEstimate(flops=1024, bytes_accessed=1024, transcendentals=0)
F32 = jnp.float32
BF16 = jnp.bfloat16


def dot(left, right, left_dim, right_dim):
    return lax.dot_general(
        left, right, (((left_dim,), (right_dim,)), ((), ())), preferred_element_type=F32
    )


def block_bias(kinfo_ref, qinfo_ref, rows):
    info = kinfo_ref[rows, :]
    usable, place = info[:, 0:1], info[:, 1:2]
    q_place, q_begin = qinfo_ref[0:1, :], qinfo_ref[1:2, :]
    allowed = ((usable <= q_place) & (usable >= q_begin)) | (place == q_place)
    return jnp.where(allowed, 0.0, NEG_FILL)


def attn_fwd_kernel(
    need_ref, kinfo_ref, qinfo_ref, q_ref, kv_ref, o_ref, lse_ref, m_ref, l_ref, acc_ref, bias_ref
):
    blocks = kv_ref.shape[0] // TOK_DEV
    m_ref[...] = jnp.full(m_ref.shape, NEG_FILL, F32)
    l_ref[...] = jnp.zeros(l_ref.shape, F32)
    acc_ref[...] = jnp.zeros(acc_ref.shape, F32)

    def one_block(block, carry):
        @pl.when(need_ref[block] > 0)
        def _():
            rows = pl.ds(pl.multiple_of(block * TOK_DEV, TOK_DEV), TOK_DEV)
            bias_ref[...] = block_bias(kinfo_ref, qinfo_ref, rows)
            for group in range(KV_HEADS):
                key = kv_ref[rows, group * HEAD : (group + 1) * HEAD]
                value = kv_ref[rows, (KV_HEADS + group) * HEAD : (KV_HEADS + group + 1) * HEAD]
                value_t = value.T
                for head in range(group * GROUP, (group + 1) * GROUP):
                    span = slice(head * HEAD, (head + 1) * HEAD)
                    scores = dot(key, q_ref[span, :], 1, 0) * (SCALE * LOG2E) + bias_ref[...]
                    old = m_ref[head : head + 1, :]
                    new = jnp.maximum(old, jnp.max(scores, axis=0, keepdims=True))
                    weights = jnp.exp2(scores - new)
                    factor = jnp.exp2(old - new)
                    m_ref[head : head + 1, :] = new
                    l_ref[head : head + 1, :] = l_ref[head : head + 1, :] * factor + jnp.sum(
                        weights, axis=0, keepdims=True
                    )
                    acc_ref[span, :] = acc_ref[span, :] * factor + dot(
                        value_t, weights.astype(BF16), 1, 0
                    )

        return carry

    lax.fori_loop(0, blocks, one_block, 0)
    real = qinfo_ref[2:3, :].astype(F32)
    lse_ref[...] = jnp.zeros(lse_ref.shape, F32)
    for head in range(HEADS):
        span = slice(head * HEAD, (head + 1) * HEAD)
        total = l_ref[head : head + 1, :]
        o_ref[span, :] = (acc_ref[span, :] * (real / total)).astype(BF16)
        lse_ref[head : head + 1, :] = m_ref[head : head + 1, :] + jnp.log(total) * LOG2E


def attn_bwd_kernel(
    need_ref,
    kinfo_ref,
    qinfo_ref,
    cos_ref,
    sin_ref,
    q_ref,
    kv_ref,
    o_ref,
    do_ref,
    lse_ref,
    dq_ref,
    near_ref,
    far_ref,
    dots_ref,
    acc_ref,
    bias_ref,
    low_ref,
):
    blocks = kv_ref.shape[0] // TOK_DEV
    real = qinfo_ref[2:3, :].astype(F32)
    for head in range(HEADS):
        span = slice(head * HEAD, (head + 1) * HEAD)
        grad = do_ref[span, :].astype(F32) * real
        low_ref[span, :] = grad.astype(BF16)
        dots_ref[head : head + 1, :] = jnp.sum(
            grad * o_ref[span, :].astype(F32), axis=0, keepdims=True
        )
    acc_ref[...] = jnp.zeros(acc_ref.shape, F32)

    def one_block(dkv_ref, first, at, carry):
        block = first + at
        rows = pl.ds(pl.multiple_of(block * TOK_DEV, TOK_DEV), TOK_DEV)
        out_rows = pl.ds(pl.multiple_of(at * TOK_DEV, TOK_DEV), TOK_DEV)

        @pl.when(need_ref[block] == 0)
        def _():
            dkv_ref[out_rows, :] = jnp.zeros((TOK_DEV, 2 * KV_HEADS * HEAD), BF16)

        @pl.when(need_ref[block] > 0)
        def _():
            bias_ref[...] = block_bias(kinfo_ref, qinfo_ref, rows)
            for group in range(KV_HEADS):
                key_cols = slice(group * HEAD, (group + 1) * HEAD)
                value_cols = slice((KV_HEADS + group) * HEAD, (KV_HEADS + group + 1) * HEAD)
                key = kv_ref[rows, key_cols]
                value = kv_ref[rows, value_cols]
                key_t = key.T
                key_grad = jnp.zeros((TOK_DEV, HEAD), F32)
                value_grad = jnp.zeros((TOK_DEV, HEAD), F32)
                for head in range(group * GROUP, (group + 1) * GROUP):
                    span = slice(head * HEAD, (head + 1) * HEAD)
                    query, grad = q_ref[span, :], low_ref[span, :]
                    scores = dot(key, query, 1, 0) * (SCALE * LOG2E) + bias_ref[...]
                    probs = jnp.exp2(scores - lse_ref[head : head + 1, :])
                    prob_grad = dot(value, grad, 1, 0)
                    score_grad = (probs * (prob_grad - dots_ref[head : head + 1, :])).astype(BF16)
                    acc_ref[span, :] += dot(key_t, score_grad, 1, 0)
                    key_grad += dot(score_grad, query, 1, 1)
                    value_grad += dot(probs.astype(BF16), grad, 1, 1)
                dkv_ref[out_rows, key_cols] = (key_grad * SCALE).astype(BF16)
                dkv_ref[out_rows, value_cols] = value_grad.astype(BF16)

        return carry

    half_blocks = blocks // 2
    lax.fori_loop(0, half_blocks, functools.partial(one_block, near_ref, 0), 0)
    lax.fori_loop(0, half_blocks, functools.partial(one_block, far_ref, half_blocks), 0)
    cosine, sine = cos_ref[...], sin_ref[...]
    half = HEAD // 2
    for head in range(HEADS):
        start = head * HEAD
        whole = (acc_ref[start : start + HEAD, :] * SCALE).astype(BF16).astype(F32)
        first, second = whole[:half], whole[half:]
        turned = jnp.concatenate(
            [first * cosine + second * sine, second * cosine - first * sine], axis=0
        )
        dq_ref[:, start : start + HEAD] = turned.T.astype(BF16)


def vmem_specs(count):
    return [pl.BlockSpec(memory_space=pltpu.VMEM)] * count


def attention_forward(need, kinfo, qinfo, query_t, kv_all):
    rows = query_t.shape[1]
    return pl.pallas_call(
        attn_fwd_kernel,
        out_shape=(
            jax.ShapeDtypeStruct((HEADS * HEAD, rows), BF16),
            jax.ShapeDtypeStruct((16, rows), F32),
        ),
        in_specs=[pl.BlockSpec(memory_space=pltpu.SMEM)] + vmem_specs(4),
        out_specs=tuple(vmem_specs(2)),
        scratch_shapes=[
            pltpu.VMEM((16, rows), F32),
            pltpu.VMEM((16, rows), F32),
            pltpu.VMEM((HEADS * HEAD, rows), F32),
            pltpu.VMEM((TOK_DEV, rows), F32),
        ],
        compiler_params=pltpu.CompilerParams(vmem_limit_bytes=VMEM_LIMIT),
        cost_estimate=SMALL,
    )(need, kinfo, qinfo, query_t, kv_all)


def attention_backward(need, kinfo, qinfo, cos_t, sin_t, query_t, kv_all, out_t, grad_t, lse):
    rows = query_t.shape[1]
    return pl.pallas_call(
        attn_bwd_kernel,
        out_shape=(
            jax.ShapeDtypeStruct((rows, HEADS * HEAD), BF16),
            jax.ShapeDtypeStruct((kv_all.shape[0] // 2, kv_all.shape[1]), BF16),
            jax.ShapeDtypeStruct((kv_all.shape[0] // 2, kv_all.shape[1]), BF16),
        ),
        in_specs=[pl.BlockSpec(memory_space=pltpu.SMEM)] + vmem_specs(9),
        out_specs=tuple(vmem_specs(3)),
        scratch_shapes=[
            pltpu.VMEM((16, rows), F32),
            pltpu.VMEM((HEADS * HEAD, rows), F32),
            pltpu.VMEM((TOK_DEV, rows), F32),
            pltpu.VMEM((HEADS * HEAD, rows), BF16),
        ],
        compiler_params=pltpu.CompilerParams(vmem_limit_bytes=VMEM_LIMIT),
        cost_estimate=SMALL,
    )(need, kinfo, qinfo, cos_t, sin_t, query_t, kv_all, out_t, grad_t, lse)


def ffn_tile(cols, mid_ref, cot_ref, w_ref, sums, outs, act_ref, acc_ref):
    both = dot(mid_ref[...], w_ref[:, : 2 * cols], 1, 0)
    hidden_grad = dot(cot_ref[...], w_ref[:, 2 * cols :], 1, 0)
    gate, up = both[:, :cols], both[:, cols:]
    share = 1.0 / (1.0 + jnp.exp(-gate))
    acted = gate * share
    act_ref[:, :cols] = (hidden_grad * up * (share * (1.0 + gate * (1.0 - share)))).astype(BF16)
    act_ref[:, cols : 2 * cols] = (hidden_grad * acted).astype(BF16)
    act_ref[:, 2 * cols :] = (acted * up).astype(BF16)
    mid_grad = dot(act_ref[:, : 2 * cols], w_ref[:, : 2 * cols], 1, 1)
    out = dot(act_ref[:, 2 * cols :], w_ref[:, 2 * cols :], 1, 1)
    if sums:
        mid_grad = mid_grad + sums[0][...].astype(F32)
        out = out + sums[1][...].astype(F32)
    outs[0][...] = mid_grad.astype(BF16)
    outs[1][...] = out.astype(BF16)
    if acc_ref is not None:
        acc_ref[:, : 2 * cols] += dot(mid_ref[...], act_ref[:, : 2 * cols], 0, 0)
        acc_ref[:, 2 * cols :] += dot(cot_ref[...], act_ref[:, 2 * cols :], 0, 0)


def ffn_kernel(cols, first, with_grad, *refs):
    mids, cots, w_ref, refs = refs[:2], refs[2:4], refs[4], refs[5:]
    mid_sums = out_sums = None
    if not first:
        mid_sums, out_sums, refs = refs[:2], refs[2:4], refs[4:]
    mid_outs, out_outs, refs = refs[:2], refs[2:4], refs[4:]
    if with_grad:
        grad_ref, act_ref, acc_ref = refs
    else:
        (act_ref,), acc_ref = refs, None
    step, last = pl.program_id(0), pl.num_programs(0) - 1
    near = step < pl.num_programs(0) // 2

    if with_grad:

        @pl.when(step == 0)
        def _():
            acc_ref[...] = jnp.zeros(acc_ref.shape, F32)

    def tile(which):
        sums = () if first else (mid_sums[which], out_sums[which])
        outs = (mid_outs[which], out_outs[which])
        ffn_tile(cols, mids[which], cots[which], w_ref, sums, outs, act_ref, acc_ref)

    pl.when(near)(lambda: tile(0))
    pl.when(jnp.logical_not(near))(lambda: tile(1))

    if with_grad:

        @pl.when(step == last)
        def _():
            grad_ref[...] = acc_ref[...].astype(BF16)


def feed_forward(mid_halves, cot_halves, weights, sums, with_grad):
    half_tokens, width = mid_halves[0].shape
    cols = weights.shape[1] // 3
    half = half_tokens // TOK_DEV
    near_spec = pl.BlockSpec((TOK_DEV, width), lambda i: (jnp.minimum(i, half - 1), 0))
    far_spec = pl.BlockSpec((TOK_DEV, width), lambda i: (jnp.maximum(i - half, 0), 0))
    act_spec = pl.BlockSpec((TOK_DEV, 3 * cols), lambda i: (i, 0))
    once = pl.BlockSpec(weights.shape, lambda i: (0, 0), pipeline_mode=pl.Buffered(1))
    row_shape = jax.ShapeDtypeStruct((half_tokens, width), BF16)
    if with_grad:
        last_shape, last_spec = jax.ShapeDtypeStruct(weights.shape, BF16), once
        scratch = [pltpu.VMEM((TOK_DEV, 3 * cols), BF16), pltpu.VMEM(weights.shape, F32)]
    else:
        last_shape, last_spec = jax.ShapeDtypeStruct((2 * half_tokens, 3 * cols), BF16), act_spec
        scratch = []
    return pl.pallas_call(
        functools.partial(ffn_kernel, cols, not sums, with_grad),
        grid=(2 * half,),
        out_shape=(row_shape,) * 4 + (last_shape,),
        in_specs=[near_spec, far_spec] * 2 + [once] + [near_spec, far_spec] * (len(sums) // 2),
        out_specs=(near_spec, far_spec) * 2 + (last_spec,),
        scratch_shapes=scratch,
        compiler_params=pltpu.CompilerParams(vmem_limit_bytes=VMEM_LIMIT),
        cost_estimate=SMALL,
    )(*mid_halves, *cot_halves, weights, *sums)


def ffn_grad_kernel(cols, mid_near, mid_far, cot_near, cot_far, act_ref, grad_ref):
    half = mid_near.shape[0]
    for near, far, part in (
        (mid_near, mid_far, slice(0, 2 * cols)),
        (cot_near, cot_far, slice(2 * cols, 3 * cols)),
    ):
        grad_ref[:, part] = (
            dot(near[...], act_ref[:half, part], 0, 0) + dot(far[...], act_ref[half:, part], 0, 0)
        ).astype(BF16)


def feed_forward_grad(mid_halves, cot_halves, act):
    half_tokens, width = mid_halves[0].shape
    cols = act.shape[1] // 3
    tile = 512 if width % 512 == 0 else width
    col_spec = pl.BlockSpec((half_tokens, tile), lambda i: (0, i))
    return pl.pallas_call(
        functools.partial(ffn_grad_kernel, cols),
        grid=(width // tile,),
        out_shape=jax.ShapeDtypeStruct((width, 3 * cols), BF16),
        in_specs=[col_spec] * 4
        + [pl.BlockSpec(act.shape, lambda i: (0, 0), pipeline_mode=pl.Buffered(1))],
        out_specs=pl.BlockSpec((tile, 3 * cols), lambda i: (i, 0)),
        compiler_params=pltpu.CompilerParams(vmem_limit_bytes=VMEM_LIMIT),
        cost_estimate=SMALL,
    )(*mid_halves, *cot_halves, act)


def slice_moves(n_plane, chunks, cols, total):
    for device in range(n_plane):
        for chunk in range(chunks):
            start = (device * chunks + chunk) * cols
            for kind in range(3):
                yield device, chunk, kind, kind * total + start, max(0, min(cols, total - start))


def pack_kernel(moves, cols, w_ref, out_ref):
    rows = w_ref.shape[0]
    for device, chunk, kind, source, real in moves:
        there = slice(device * rows, (device + 1) * rows)
        at = (chunk * 3 + kind) * cols
        if real:
            out_ref[there, at : at + real] = w_ref[:, source : source + real]
        if real < cols:
            out_ref[there, at + real : at + cols] = jnp.zeros((rows, cols - real), BF16)


def unpack_kernel(moves, cols, in_ref, out_ref):
    rows = out_ref.shape[0]
    for device, chunk, kind, source, real in moves:
        if real:
            at = (chunk * 3 + kind) * cols
            block = in_ref[device * rows : (device + 1) * rows, at : at + real]
            out_ref[:, source : source + real] = block.astype(F32)


def pack_slices(w_mlp, n_plane, chunks, cols):
    rows, total = w_mlp.shape[0], w_mlp.shape[1] // 3
    if rows % 16:
        wide = jnp.pad(
            w_mlp.reshape(rows, 3, total), ((0, 0), (0, 0), (0, n_plane * chunks * cols - total))
        )
        wide = wide.reshape(rows, 3, n_plane, chunks, cols).transpose(2, 0, 3, 1, 4)
        return wide.reshape(n_plane * rows, 3 * chunks * cols)
    moves = list(slice_moves(n_plane, chunks, cols, total))
    return pl.pallas_call(
        functools.partial(pack_kernel, moves, cols),
        out_shape=jax.ShapeDtypeStruct((n_plane * rows, 3 * chunks * cols), BF16),
        in_specs=vmem_specs(1),
        out_specs=vmem_specs(1)[0],
        compiler_params=pltpu.CompilerParams(vmem_limit_bytes=VMEM_LIMIT),
        cost_estimate=SMALL,
    )(w_mlp)


def unpack_slices(array, rows, total, n_plane, chunks, cols):
    if rows % 16:
        stacked = array.reshape(n_plane, rows, chunks, 3, cols).transpose(1, 3, 0, 2, 4)
        return stacked.reshape(rows, 3, -1)[:, :, :total].reshape(rows, 3 * total).astype(F32)
    moves = list(slice_moves(n_plane, chunks, cols, total))
    return pl.pallas_call(
        functools.partial(unpack_kernel, moves, cols),
        out_shape=jax.ShapeDtypeStruct((rows, 3 * total), F32),
        in_specs=vmem_specs(1),
        out_specs=vmem_specs(1)[0],
        compiler_params=pltpu.CompilerParams(vmem_limit_bytes=VMEM_LIMIT),
        cost_estimate=SMALL,
    )(array)


def weight_grad_kernel(n_dp, local_rows, across, dev_ref, *refs):
    count = len(across)
    lefts, rights = refs[: 2 * count : 2], refs[1 : 2 * count : 2]
    sides, (near_ref, far_ref, turned_ref, block_ref) = refs[2 * count : -4], refs[-4:]
    half = near_ref.shape[0] // (n_dp * local_rows)
    tile = block_ref.shape[1]

    def move(from_ref, at):
        cols = slice(at, at + from_ref.shape[1])
        for slot in range(2 * half):
            out_ref = near_ref if slot < half else far_ref
            for zone in range(n_dp):
                source = (zone * 2 * half + dev_ref[slot]) * local_rows
                source = pl.ds(pl.multiple_of(source, local_rows), local_rows)
                there = ((slot % half) * n_dp + zone) * local_rows
                out_ref[there : there + local_rows, cols] = from_ref[source, :]

    at = 0
    for left, right, is_across in zip(lefts, rights, across):
        turned_ref[...] = left[...].T
        cols = right.shape[0] if is_across else right.shape[1]
        for start in range(0, cols, tile):
            span = slice(start, start + tile)
            if is_across:
                block = dot(turned_ref[...], right[span, :], 1, 1)
            else:
                block = dot(turned_ref[...], right[:, span], 1, 0)
            block_ref[...] = block.astype(BF16)
            move(block_ref, at)
            at += tile
    for side_ref in sides:
        move(side_ref, at)


def weight_grads(plane, local_rows, terms, side=None):
    n_dp = lax.axis_size("dp")
    tokens, width = terms[0][0].shape
    widths = [right.shape[0 if across else 1] for _, right, across in terms]
    if local_rows % 16:
        full = jnp.concatenate(
            [dot(left, right, 0, 1 if across else 0) for left, right, across in terms], axis=1
        ).astype(BF16)
        if side is not None:
            full = jnp.concatenate([full, side], axis=1)
        full = full.reshape(n_dp, plane.count, local_rows, full.shape[1])
        blocks = [
            lax.dynamic_slice_in_dim(full, device, 1, 1).reshape(n_dp * local_rows, -1)
            for device in plane.devices
        ]
        half = plane.count // 2
        return jnp.concatenate(blocks[:half]), jnp.concatenate(blocks[half:])
    tile = 512
    extra = [] if side is None else [side]
    total = sum(widths) + sum(array.shape[1] for array in extra)
    shape = jax.ShapeDtypeStruct((width // 2, total), BF16)
    return pl.pallas_call(
        functools.partial(weight_grad_kernel, n_dp, local_rows, [term[2] for term in terms]),
        out_shape=(shape, shape),
        in_specs=[pl.BlockSpec(memory_space=pltpu.SMEM)]
        + vmem_specs(2 * len(terms) + len(extra)),
        out_specs=tuple(vmem_specs(2)),
        scratch_shapes=[pltpu.VMEM((width, tokens), BF16), pltpu.VMEM((width, tile), BF16)],
        compiler_params=pltpu.CompilerParams(vmem_limit_bytes=VMEM_LIMIT),
        cost_estimate=SMALL,
    )(jnp.stack(plane.devices), *[array for term in terms for array in term[:2]], *extra)


def spread_kernel(q_width, width, kv_cols, sum_ref, qkv_ref, out_ref, side_ref):
    qkv_ref[:, :q_width] = sum_ref[:, :q_width].astype(F32)
    at = q_width + width
    qkv_ref[:, q_width:] = sum_ref[:, at : at + kv_cols].astype(F32)
    out_ref[...] = sum_ref[:, q_width:at].astype(F32).T
    side_ref[...] = sum_ref[:8, at + kv_cols :].astype(F32)


def spread_sums(attn_sum, q_width, width, kv_cols):
    rows = attn_sum.shape[0]
    at = q_width + width
    if rows % 16:
        full = attn_sum.astype(F32)
        grad_qkv = jnp.concatenate([full[:, :q_width], full[:, at : at + kv_cols]], axis=1)
        return grad_qkv, full[:, q_width:at].T, full[:, at + kv_cols :]
    return pl.pallas_call(
        functools.partial(spread_kernel, q_width, width, kv_cols),
        out_shape=(
            jax.ShapeDtypeStruct((rows, q_width + kv_cols), F32),
            jax.ShapeDtypeStruct((width, rows), F32),
            jax.ShapeDtypeStruct((8, LANES), F32),
        ),
        in_specs=vmem_specs(1),
        out_specs=tuple(vmem_specs(3)),
        compiler_params=pltpu.CompilerParams(vmem_limit_bytes=VMEM_LIMIT),
        cost_estimate=SMALL,
    )(attn_sum)


def after(array, *others):
    return lax.optimization_barrier((array, *others))[0]


class Plane:
    def __init__(self):
        ctx, uly = lax.axis_size("ctx"), lax.axis_size("uly")
        self.count = ctx * uly
        assert self.count & (self.count - 1) == 0 and ctx % 2 == 0
        self.me = lax.axis_index("ctx") * uly + lax.axis_index("uly")
        self.core = uly
        near = [1 << i for i in range(uly.bit_length() - 1)]
        far = [self.core << i for i in range(1, (ctx // 2).bit_length())]
        self.orders = (far + near, near + far)
        self.steps = len(near) + len(far)
        mine = (self.me // self.core) % 2 == 0
        masks = [[0], [0]]
        for which in (0, 1):
            for bit in self.orders[which]:
                masks[which] += [bit | mask for mask in masks[which]]
        pairs = list(zip(masks[0], masks[1]))
        near_slots = [jnp.where(mine, a, b) for a, b in pairs]
        far_slots = [jnp.where(mine, b, a) | self.core for a, b in pairs]
        self.devices = [self.me ^ mask for mask in near_slots + far_slots]

    def swap(self, array, step):
        pairs = []
        for i in range(self.count):
            if step == self.steps:
                bit = self.core
            else:
                bit = self.orders[(i // self.core) % 2][step]
            pairs.append((i, i ^ bit))
        return lax.ppermute(array, PLANE, pairs)

    def widen(self, rows, step, *others):
        moved = self.swap(rows, step)
        return jnp.concatenate([after(rows, *others) if others else rows, moved], axis=0)

    def gather(self, rows, late_step=None, *others):
        stages = [rows]
        for step in range(self.steps):
            if step == late_step:
                stages[-1] = after(stages[-1], *others)
            stages.append(self.widen(stages[-1], step))
        return stages + [self.swap(stages[-1], self.steps)]

    def fold(self, near, far, step):
        return (near.astype(F32) + self.swap(far, step).astype(F32)).astype(BF16)

    def fold_rest(self, rows, step):
        half = rows.shape[0] // 2
        return self.fold(rows[:half], rows[half:], step)


def place_info(spans, row_in_span, length_row):
    places = spans * TOK_DEV + row_in_span
    begins = jnp.zeros_like(places)
    end = jnp.int32(0)
    for doc in range(length_row.shape[0]):
        end = end + length_row[doc]
        begins = jnp.where(places >= end, jnp.maximum(begins, end), begins)
    return places, begins


def inverse_rms(values):
    return lax.rsqrt(jnp.mean(values * values, axis=-1, keepdims=True) + NORM_EPS)


def norm_backward(values, inverse, scaled):
    return inverse * scaled - values * (
        inverse**3 * jnp.mean(scaled * values, axis=-1, keepdims=True)
    )


def turn(heads, cosine, sine):
    half = HEAD // 2
    first, second = heads[..., :half], heads[..., half:]
    return jnp.concatenate(
        [first * cosine - second * sine, second * cosine + first * sine], axis=-1
    )


def shards(
    layer_input,
    span_order,
    doc_lengths,
    pad_mask,
    w_qkv,
    b_qkv,
    w_out,
    norm_gain_attn,
    norm_gain_mlp,
    w_mlp,
    cotangent,
):
    tok_rows, width = layer_input.shape
    n_dp = lax.axis_size("dp")
    n_plane = lax.axis_size("ctx") * lax.axis_size("uly")
    n_all = n_dp * n_plane
    plane = Plane()
    ffn_width = w_mlp.shape[1] // 3
    local_rows = w_mlp.shape[0]
    zone = local_rows * n_plane
    q_width, kv_width = HEADS * HEAD, KV_HEADS * HEAD
    qkv_width = q_width + 2 * kv_width
    bias_rows = b_qkv.shape[0]
    slice_tiles = -(-(ffn_width // LANES) // n_plane)
    chunks = max(c for c in (1, 2, 3) if slice_tiles % c == 0)
    chunk_cols = slice_tiles // chunks * LANES
    kv_cols = 2 * kv_width + LANES

    def swap_rows(array):
        return lax.all_to_all(array, PLANE, split_axis=0, concat_axis=0, tiled=True)

    def zone_gather(array):
        return lax.all_gather(array, "dp", axis=0, tiled=True)

    def zone_sum(array):
        return lax.psum_scatter(array, "dp", scatter_dimension=0, tiled=True)

    def whole_rows(pieces):
        cols = pieces[0].shape[1]
        full = jnp.zeros((n_dp, n_plane, local_rows, cols), BF16)
        slots = [block for piece in pieces for block in jnp.split(piece, n_plane // 2)]
        for device, block in zip(plane.devices, slots):
            piece = block.reshape(n_dp, 1, local_rows, cols)
            full = lax.dynamic_update_slice(full, piece, (0, device, 0, 0))
        return full.reshape(n_all * local_rows, cols)

    def device_blocks(array):
        cols = array.shape[1]
        full = array.reshape(n_dp, n_plane, local_rows, cols)
        return [
            lax.dynamic_slice_in_dim(full, device, 1, 1).reshape(n_dp * local_rows, cols)
            for device in plane.devices
        ]

    side = jnp.concatenate(
        [
            norm_gain_attn[:, None],
            norm_gain_mlp[:, None],
            jnp.zeros((local_rows, 62), BF16),
            jnp.pad(b_qkv[None, :], ((0, local_rows - 1), (0, 64 - bias_rows))),
        ],
        axis=1,
    )
    my_dp = lax.axis_index("dp")

    def zone_rows(array):
        full = jnp.zeros((n_dp, *array.shape), BF16)
        for step in range(n_dp):
            moved = array
            if step:
                moved = lax.ppermute(array, "dp", [(i, (i + step) % n_dp) for i in range(n_dp)])
            full = lax.dynamic_update_slice(
                full, moved[None], ((my_dp + n_dp - step) % n_dp, 0, 0)
            )
        return full.reshape(n_dp * array.shape[0], array.shape[1])

    kv_local = jnp.concatenate([w_qkv[:, q_width:], side], axis=1)
    attn_local = jnp.concatenate([kv_local, w_qkv[:, :q_width], w_out.T], axis=1)
    attn_zone = zone_rows(attn_local)
    kv_zone = attn_zone[:, : kv_local.shape[1]]
    big_zone = attn_zone[:, kv_local.shape[1] :]

    packed = pack_slices(after(w_mlp, attn_local), n_plane, chunks, chunk_cols)
    chunk_width = 3 * chunk_cols
    mlp_zone = swap_rows(packed)
    mlp_weights = [
        zone_gather(mlp_zone[:, chunk * chunk_width : (chunk + 1) * chunk_width])
        for chunk in range(chunks)
    ]

    w_kv_stages = plane.gather(kv_zone, 1, mlp_zone)
    w_q_stages = plane.gather(after(big_zone[:, :q_width], w_kv_stages[1]))
    w_out_near = after(big_zone[:, q_width:], w_q_stages[-2])
    w_out_near = plane.widen(w_out_near, 0)

    order_row, length_row, mask_row = after(
        (span_order[0], doc_lengths[0], pad_mask[0]), packed
    )
    row_in_span = jnp.arange(tok_rows, dtype=jnp.int32)
    stored_block = jnp.stack(plane.devices)
    spans = order_row[stored_block]
    own_place, own_begin = place_info(spans[0], row_in_span, length_row)
    flags = mask_row.reshape(n_plane, tok_rows)[stored_block]
    key_place = spans[:, None] * TOK_DEV + row_in_span[None, :]
    kinfo = jnp.stack(
        [jnp.where(flags == 1, key_place, FAR).reshape(-1), key_place.reshape(-1)], axis=1
    )
    qinfo = jnp.concatenate(
        [
            own_place[None],
            own_begin[None],
            flags[0][None],
            jnp.zeros((5, tok_rows), jnp.int32),
        ],
        axis=0,
    )
    need = ((spans <= spans[0]) & ((spans + 1) * TOK_DEV > own_begin[0])).astype(jnp.int32)

    inner = (own_place - own_begin).astype(F32)
    half = HEAD // 2
    frequency = ROPE_BASE ** (-(jnp.arange(half, dtype=F32) * 2.0) / HEAD)
    angles_t = frequency[:, None] * inner[None, :]
    cos_t, sin_t = jnp.cos(angles_t), jnp.sin(angles_t)
    cos_r, sin_r = cos_t.T[:, None, :], sin_t.T[:, None, :]

    w_kv_all = whole_rows(w_kv_stages[-2:])
    side_all = w_kv_all[:, 2 * kv_width :].astype(F32)
    gain_attn = side_all[:, 0]
    gain_mlp = side_all[:, 1]
    bias_all = side_all.reshape(n_all, local_rows, LANES)[:, 0, 64 : 64 + bias_rows].reshape(-1)

    inputs = layer_input.astype(F32)
    in_inverse = inverse_rms(inputs)
    normed_in = (inputs * in_inverse * gain_attn).astype(BF16)

    kv_proj = dot(normed_in, w_kv_all[:, : 2 * kv_width], 1, 0) + bias_all[q_width:]
    key_own = turn(kv_proj[:, :kv_width].reshape(tok_rows, KV_HEADS, HEAD), cos_r, sin_r)
    kv_own = jnp.concatenate([key_own.reshape(tok_rows, kv_width), kv_proj[:, kv_width:]], axis=1)
    kv_own = after(kv_own.astype(BF16), w_q_stages[-2])
    kv_stages = plane.gather(kv_own, 1, w_out_near)
    kv_all = jnp.concatenate(kv_stages[-2:], axis=0)
    w_q_all = whole_rows(w_q_stages[-2:])

    q_proj = dot(w_q_all, normed_in, 0, 1) + bias_all[:q_width, None]
    q_heads = q_proj.reshape(HEADS, 2, half, tok_rows)
    q_first, q_second = q_heads[:, 0], q_heads[:, 1]
    query_t = (
        jnp.stack(
            [q_first * cos_t - q_second * sin_t, q_second * cos_t + q_first * sin_t], axis=1
        )
        .reshape(q_width, tok_rows)
        .astype(BF16)
    )
    cot_near = plane.widen(after(cotangent, kv_stages[-2]), 0)
    need = after(need, w_out_near, cot_near)
    attended_t, lse = attention_forward(need, kinfo, qinfo, query_t, kv_all)
    for step in range(1, plane.steps):
        w_out_near = plane.widen(after(w_out_near, kv_stages[-2]), step, attended_t)
    w_out_all = whole_rows([w_out_near, plane.swap(w_out_near, plane.steps)])
    for step in range(1, plane.steps):
        cot_near = plane.widen(cot_near, step, attended_t)
    attended_t = after(attended_t, cot_near)

    middle = inputs + dot(attended_t, w_out_all, 0, 1)
    mid_inverse = inverse_rms(middle)
    normed_mid = (middle * mid_inverse * gain_mlp).astype(BF16)

    mid_near = normed_mid
    for step in range(plane.steps):
        mid_near = plane.widen(mid_near, step)
    cot_halves = cot_near, plane.swap(cot_near, plane.steps)
    mid_near = after(mid_near, mlp_weights[0])
    mid_halves = mid_near, plane.swap(mid_near, plane.steps)
    sums, chunk_grads = (), []
    for chunk, weights in enumerate(mlp_weights):
        last = chunk == chunks - 1
        *sums, extra = feed_forward(mid_halves, cot_halves, weights, tuple(sums), not last)
        if not last:
            chunk_grads.append(extra)

    def token_blocks(array):
        return [array[k * tok_rows : (k + 1) * tok_rows] for k in range(n_plane)]

    chunk_sums = [zone_sum(grad) for grad in chunk_grads]
    mid_fold = plane.fold(sums[0], sums[1], plane.steps)
    chunk_grads.append(feed_forward_grad(mid_halves, cot_halves, after(extra, mid_fold)))
    chunk_sums.append(zone_sum(chunk_grads[-1]))
    for step in range(plane.steps - 1, -1, -1):
        half = mid_fold.shape[0] // 2
        kept, sent = mid_fold[:half], mid_fold[half:]
        if step == plane.steps - 1:
            kept = after(kept, chunk_grads[-1])
        mid_fold = plane.fold(kept, sent, step)
        if step == 0:
            out_fold = plane.fold(after(sums[2], kept), sums[3], plane.steps)
    mid_grad = after(mid_fold, *chunk_sums[:-1][:1]).astype(F32)

    out_grad = cotangent.astype(F32)
    gain_mlp_grad = jnp.sum(mid_grad * (middle * mid_inverse), axis=0)
    middle_grad = out_grad + norm_backward(middle, mid_inverse, mid_grad * gain_mlp)
    middle_low = middle_grad.astype(BF16)
    attended_grad_t = dot(w_out_all, middle_low, 0, 1).astype(BF16)
    attended_grad_t = after(attended_grad_t, out_fold)
    query_grad, *kv_grads = attention_backward(
        need, kinfo, qinfo, cos_t, sin_t, query_t, kv_all, attended_t, attended_grad_t, lse
    )
    kv_fold = plane.fold(*kv_grads, plane.steps)
    mlp_out = after(out_fold, mid_fold)
    for step in range(plane.steps - 1, 0, -1):
        mlp_out = plane.fold_rest(mlp_out, step)
    big_grads = weight_grads(
        plane,
        local_rows,
        [
            (after(normed_in, mlp_out, kv_fold), query_grad, False),
            (middle_low, attended_t, True),
        ],
    )
    big_fold = plane.fold(*big_grads, plane.steps)
    mlp_out = plane.fold_rest(after(mlp_out, kv_fold), 0)
    for step in range(plane.steps - 1, -1, -1):
        rows = kv_fold.shape[0] // 2
        kept, sent = kv_fold[:rows], kv_fold[rows:]
        if step == plane.steps - 1:
            kept = after(kept, big_fold, *chunk_sums[1:-1])
        kv_fold = plane.fold(kept, sent, step)
    kv_back = after(kv_fold, mlp_out)
    kv_back = kv_back.astype(F32)
    key_back = turn(kv_back[:, :kv_width].reshape(tok_rows, KV_HEADS, HEAD), cos_r, -sin_r)
    projected_grad = jnp.concatenate(
        [query_grad, key_back.reshape(tok_rows, kv_width).astype(BF16), kv_back[:, kv_width:].astype(BF16)],
        axis=1,
    )
    in_grad = dot(projected_grad[:, :q_width], w_q_all, 1, 1) + dot(
        projected_grad[:, q_width:], w_kv_all[:, : 2 * kv_width], 1, 1
    )
    gain_attn_grad = jnp.sum(in_grad * (inputs * in_inverse), axis=0)
    input_grad = middle_grad + norm_backward(inputs, in_inverse, in_grad * gain_attn)
    qkv_bias_grad = jnp.sum(projected_grad.astype(F32), axis=0)

    def side_rows(array):
        array = array.reshape(n_dp, n_plane, 1, -1)
        return jnp.pad(array, ((0, 0), (0, 0), (0, 0), (0, LANES - array.shape[-1])))

    side_grad = jnp.concatenate(
        [side_rows(gain_attn_grad), side_rows(gain_mlp_grad), side_rows(qkv_bias_grad)]
        + [jnp.zeros((n_dp, n_plane, 1, LANES), F32)] * 5,
        axis=2,
    )
    side_grad = jnp.pad(side_grad, ((0, 0), (0, 0), (0, local_rows - 8), (0, 0)))
    side_grad = side_grad.reshape(n_all * local_rows, LANES).astype(BF16)
    for step in range(plane.steps - 1, 0, -1):
        big_fold = plane.fold_rest(big_fold, step)
    small_grads = weight_grads(
        plane,
        local_rows,
        [(after(normed_in, big_fold), projected_grad[:, q_width:], False)],
        side_grad,
    )
    big_fold = plane.fold_rest(big_fold, 0)
    small_fold = plane.fold(*small_grads, plane.steps)
    for step in range(plane.steps - 1, -1, -1):
        rows = small_fold.shape[0] // 2
        kept, sent = small_fold[:rows], small_fold[rows:]
        if step == 0:
            kept = after(kept, chunk_sums[-1])
        small_fold = plane.fold(kept, sent, step)
    attn_plane = jnp.concatenate([big_fold, small_fold], axis=1)
    grad_qkv, grad_out, side_sum = spread_sums(
        zone_sum(attn_plane), q_width, width, 2 * kv_width
    )

    all_swapped = swap_rows(after(jnp.concatenate(chunk_sums, axis=1), attn_plane))
    grad_mlp = unpack_slices(
        all_swapped, local_rows, ffn_width, n_plane, chunks, chunk_cols
    )
    block_output = (middle + mlp_out.astype(F32)).astype(BF16)
    return (
        block_output,
        input_grad,
        grad_qkv,
        side_sum[2, :bias_rows],
        grad_out,
        side_sum[0, :local_rows],
        side_sum[1, :local_rows],
        grad_mlp,
    )


def solution(mesh):
    rows = P(EVERY, None)
    flat = P(EVERY)
    columns = P(None, EVERY)
    batch = P("dp", None)
    return jax.shard_map(
        shards,
        mesh=mesh,
        in_specs=(rows, batch, batch, batch, rows, flat, columns, flat, flat, rows, rows),
        out_specs=(rows, rows, rows, flat, columns, flat, flat, rows),
        check_vma=False,
    )
```

```python
import functools

import jax
import jax.numpy as jnp
from jax import lax
from jax.experimental import pallas as pl
from jax.experimental.pallas import tpu as pltpu
from jax.sharding import PartitionSpec as P

HEADS = 12
KV_HEADS = 2
HEAD = 128
TOK_DEV = 256
LANES = 128
GROUP = HEADS // KV_HEADS

NORM_EPS = 1e-06
ROPE_BASE = 1000000.0
NEG_FILL = -1e30
LOG2E = 1.4426950408889634
SCALE = HEAD ** (-0.5)
FAR = 1 << 30
PLANE = ("ctx", "uly")
EVERY = ("dp", "ctx", "uly")
VMEM_LIMIT = 56 * 1024 * 1024
SMALL = pl.CostEstimate(flops=1024, bytes_accessed=1024, transcendentals=0)
F32 = jnp.float32
BF16 = jnp.bfloat16


def dot(left, right, left_dim, right_dim):
    return lax.dot_general(
        left, right, (((left_dim,), (right_dim,)), ((), ())), preferred_element_type=F32
    )


def block_bias(kinfo_ref, qinfo_ref, rows):
    info = kinfo_ref[rows, :]
    usable, place = info[:, 0:1], info[:, 1:2]
    q_place, q_begin = qinfo_ref[0:1, :], qinfo_ref[1:2, :]
    allowed = ((usable <= q_place) & (usable >= q_begin)) | (place == q_place)
    return jnp.where(allowed, 0.0, NEG_FILL)


def attn_fwd_kernel(
    need_ref, kinfo_ref, qinfo_ref, q_ref, kv_ref, o_ref, lse_ref, m_ref, l_ref, acc_ref, bias_ref
):
    blocks = kv_ref.shape[0] // TOK_DEV
    m_ref[...] = jnp.full(m_ref.shape, NEG_FILL, F32)
    l_ref[...] = jnp.zeros(l_ref.shape, F32)
    acc_ref[...] = jnp.zeros(acc_ref.shape, F32)

    def one_block(block, carry):
        @pl.when(need_ref[block] > 0)
        def _():
            rows = pl.ds(pl.multiple_of(block * TOK_DEV, TOK_DEV), TOK_DEV)
            bias_ref[...] = block_bias(kinfo_ref, qinfo_ref, rows)
            for group in range(KV_HEADS):
                key = kv_ref[rows, group * HEAD : (group + 1) * HEAD]
                value = kv_ref[rows, (KV_HEADS + group) * HEAD : (KV_HEADS + group + 1) * HEAD]
                value_t = value.T
                for head in range(group * GROUP, (group + 1) * GROUP):
                    span = slice(head * HEAD, (head + 1) * HEAD)
                    scores = dot(key, q_ref[span, :], 1, 0) * (SCALE * LOG2E) + bias_ref[...]
                    old = m_ref[head : head + 1, :]
                    new = jnp.maximum(old, jnp.max(scores, axis=0, keepdims=True))
                    weights = jnp.exp2(scores - new)
                    factor = jnp.exp2(old - new)
                    m_ref[head : head + 1, :] = new
                    l_ref[head : head + 1, :] = l_ref[head : head + 1, :] * factor + jnp.sum(
                        weights, axis=0, keepdims=True
                    )
                    acc_ref[span, :] = acc_ref[span, :] * factor + dot(
                        value_t, weights.astype(BF16), 1, 0
                    )

        return carry

    lax.fori_loop(0, blocks, one_block, 0)
    real = qinfo_ref[2:3, :].astype(F32)
    lse_ref[...] = jnp.zeros(lse_ref.shape, F32)
    for head in range(HEADS):
        span = slice(head * HEAD, (head + 1) * HEAD)
        total = l_ref[head : head + 1, :]
        o_ref[span, :] = (acc_ref[span, :] * (real / total)).astype(BF16)
        lse_ref[head : head + 1, :] = m_ref[head : head + 1, :] + jnp.log(total) * LOG2E


def attn_bwd_kernel(
    need_ref,
    kinfo_ref,
    qinfo_ref,
    cos_ref,
    sin_ref,
    q_ref,
    kv_ref,
    o_ref,
    do_ref,
    lse_ref,
    dq_ref,
    near_ref,
    far_ref,
    dots_ref,
    acc_ref,
    bias_ref,
    low_ref,
):
    blocks = kv_ref.shape[0] // TOK_DEV
    real = qinfo_ref[2:3, :].astype(F32)
    for head in range(HEADS):
        span = slice(head * HEAD, (head + 1) * HEAD)
        grad = do_ref[span, :].astype(F32) * real
        low_ref[span, :] = grad.astype(BF16)
        dots_ref[head : head + 1, :] = jnp.sum(
            grad * o_ref[span, :].astype(F32), axis=0, keepdims=True
        )
    acc_ref[...] = jnp.zeros(acc_ref.shape, F32)

    def one_block(dkv_ref, first, at, carry):
        block = first + at
        rows = pl.ds(pl.multiple_of(block * TOK_DEV, TOK_DEV), TOK_DEV)
        out_rows = pl.ds(pl.multiple_of(at * TOK_DEV, TOK_DEV), TOK_DEV)

        @pl.when(need_ref[block] == 0)
        def _():
            dkv_ref[out_rows, :] = jnp.zeros((TOK_DEV, 2 * KV_HEADS * HEAD), BF16)

        @pl.when(need_ref[block] > 0)
        def _():
            bias_ref[...] = block_bias(kinfo_ref, qinfo_ref, rows)
            for group in range(KV_HEADS):
                key_cols = slice(group * HEAD, (group + 1) * HEAD)
                value_cols = slice((KV_HEADS + group) * HEAD, (KV_HEADS + group + 1) * HEAD)
                key = kv_ref[rows, key_cols]
                value = kv_ref[rows, value_cols]
                key_t = key.T
                key_grad = jnp.zeros((TOK_DEV, HEAD), F32)
                value_grad = jnp.zeros((TOK_DEV, HEAD), F32)
                for head in range(group * GROUP, (group + 1) * GROUP):
                    span = slice(head * HEAD, (head + 1) * HEAD)
                    query, grad = q_ref[span, :], low_ref[span, :]
                    scores = dot(key, query, 1, 0) * (SCALE * LOG2E) + bias_ref[...]
                    probs = jnp.exp2(scores - lse_ref[head : head + 1, :])
                    prob_grad = dot(value, grad, 1, 0)
                    score_grad = (probs * (prob_grad - dots_ref[head : head + 1, :])).astype(BF16)
                    acc_ref[span, :] += dot(key_t, score_grad, 1, 0)
                    key_grad += dot(score_grad, query, 1, 1)
                    value_grad += dot(probs.astype(BF16), grad, 1, 1)
                dkv_ref[out_rows, key_cols] = (key_grad * SCALE).astype(BF16)
                dkv_ref[out_rows, value_cols] = value_grad.astype(BF16)

        return carry

    half_blocks = blocks // 2
    lax.fori_loop(0, half_blocks, functools.partial(one_block, near_ref, 0), 0)
    lax.fori_loop(0, half_blocks, functools.partial(one_block, far_ref, half_blocks), 0)
    cosine, sine = cos_ref[...], sin_ref[...]
    half = HEAD // 2
    for head in range(HEADS):
        start = head * HEAD
        whole = (acc_ref[start : start + HEAD, :] * SCALE).astype(BF16).astype(F32)
        first, second = whole[:half], whole[half:]
        turned = jnp.concatenate(
            [first * cosine + second * sine, second * cosine - first * sine], axis=0
        )
        dq_ref[:, start : start + HEAD] = turned.T.astype(BF16)


def vmem_specs(count):
    return [pl.BlockSpec(memory_space=pltpu.VMEM)] * count


def attention_forward(need, kinfo, qinfo, query_t, kv_all):
    rows = query_t.shape[1]
    return pl.pallas_call(
        attn_fwd_kernel,
        out_shape=(
            jax.ShapeDtypeStruct((HEADS * HEAD, rows), BF16),
            jax.ShapeDtypeStruct((16, rows), F32),
        ),
        in_specs=[pl.BlockSpec(memory_space=pltpu.SMEM)] + vmem_specs(4),
        out_specs=tuple(vmem_specs(2)),
        scratch_shapes=[
            pltpu.VMEM((16, rows), F32),
            pltpu.VMEM((16, rows), F32),
            pltpu.VMEM((HEADS * HEAD, rows), F32),
            pltpu.VMEM((TOK_DEV, rows), F32),
        ],
        compiler_params=pltpu.CompilerParams(vmem_limit_bytes=VMEM_LIMIT),
        cost_estimate=SMALL,
    )(need, kinfo, qinfo, query_t, kv_all)


def attention_backward(need, kinfo, qinfo, cos_t, sin_t, query_t, kv_all, out_t, grad_t, lse):
    rows = query_t.shape[1]
    return pl.pallas_call(
        attn_bwd_kernel,
        out_shape=(
            jax.ShapeDtypeStruct((rows, HEADS * HEAD), BF16),
            jax.ShapeDtypeStruct((kv_all.shape[0] // 2, kv_all.shape[1]), BF16),
            jax.ShapeDtypeStruct((kv_all.shape[0] // 2, kv_all.shape[1]), BF16),
        ),
        in_specs=[pl.BlockSpec(memory_space=pltpu.SMEM)] + vmem_specs(9),
        out_specs=tuple(vmem_specs(3)),
        scratch_shapes=[
            pltpu.VMEM((16, rows), F32),
            pltpu.VMEM((HEADS * HEAD, rows), F32),
            pltpu.VMEM((TOK_DEV, rows), F32),
            pltpu.VMEM((HEADS * HEAD, rows), BF16),
        ],
        compiler_params=pltpu.CompilerParams(vmem_limit_bytes=VMEM_LIMIT),
        cost_estimate=SMALL,
    )(need, kinfo, qinfo, cos_t, sin_t, query_t, kv_all, out_t, grad_t, lse)


def ffn_tile(cols, mid_ref, cot_ref, w_refs, sums, outs, act_refs, acc_refs):
    mid_grad = out = None
    if sums:
        mid_grad, out = sums[0][...].astype(F32), sums[1][...].astype(F32)
    for w_ref, act_ref in zip(w_refs, act_refs):
        both = dot(mid_ref[...], w_ref[:, : 2 * cols], 1, 0)
        hidden_grad = dot(cot_ref[...], w_ref[:, 2 * cols :], 1, 0)
        gate, up = both[:, :cols], both[:, cols:]
        share = 1.0 / (1.0 + jnp.exp(-gate))
        acted = gate * share
        act_ref[:, :cols] = (
            hidden_grad * up * (share * (1.0 + gate * (1.0 - share)))
        ).astype(BF16)
        act_ref[:, cols : 2 * cols] = (hidden_grad * acted).astype(BF16)
        act_ref[:, 2 * cols :] = (acted * up).astype(BF16)
        mid_term = dot(act_ref[:, : 2 * cols], w_ref[:, : 2 * cols], 1, 1)
        out_term = dot(act_ref[:, 2 * cols :], w_ref[:, 2 * cols :], 1, 1)
        mid_grad = mid_term if mid_grad is None else mid_grad + mid_term
        out = out_term if out is None else out + out_term
    outs[0][...] = mid_grad.astype(BF16)
    outs[1][...] = out.astype(BF16)
    for act_ref, acc_ref in zip(act_refs, acc_refs):
        acc_ref[:, : 2 * cols] += dot(mid_ref[...], act_ref[:, : 2 * cols], 0, 0)
        acc_ref[:, 2 * cols :] += dot(cot_ref[...], act_ref[:, 2 * cols :], 0, 0)


def ffn_kernel(cols, count, first, with_grad, *refs):
    mids, cots, w_refs, refs = refs[:2], refs[2:4], refs[4 : 4 + count], refs[4 + count :]
    mid_sums = out_sums = None
    if not first:
        mid_sums, out_sums, refs = refs[:2], refs[2:4], refs[4:]
    mid_outs, out_outs, refs = refs[:2], refs[2:4], refs[4:]
    if with_grad:
        grad_refs, act_refs, acc_refs = refs[:count], refs[count : 2 * count], refs[2 * count :]
    else:
        grad_refs, act_refs, acc_refs = (), refs, ()
    step, last = pl.program_id(0), pl.num_programs(0) - 1
    near = step < pl.num_programs(0) // 2

    @pl.when(step == 0)
    def _():
        for acc_ref in acc_refs:
            acc_ref[...] = jnp.zeros(acc_ref.shape, F32)

    def tile(which):
        sums = () if first else (mid_sums[which], out_sums[which])
        outs = (mid_outs[which], out_outs[which])
        ffn_tile(cols, mids[which], cots[which], w_refs, sums, outs, act_refs, acc_refs)

    pl.when(near)(lambda: tile(0))
    pl.when(jnp.logical_not(near))(lambda: tile(1))

    @pl.when(step == last)
    def _():
        for grad_ref, acc_ref in zip(grad_refs, acc_refs):
            grad_ref[...] = acc_ref[...].astype(BF16)


def feed_forward(mid_halves, cot_halves, weights, sums, with_grad):
    half_tokens, width = mid_halves[0].shape
    count, shape = len(weights), weights[0].shape
    cols = shape[1] // 3
    half = half_tokens // TOK_DEV
    near_spec = pl.BlockSpec((TOK_DEV, width), lambda i: (jnp.minimum(i, half - 1), 0))
    far_spec = pl.BlockSpec((TOK_DEV, width), lambda i: (jnp.maximum(i - half, 0), 0))
    act_spec = pl.BlockSpec((TOK_DEV, 3 * cols), lambda i: (i, 0))
    once = pl.BlockSpec(shape, lambda i: (0, 0), pipeline_mode=pl.Buffered(1))
    row_shape = jax.ShapeDtypeStruct((half_tokens, width), BF16)
    if with_grad:
        last_shape, last_spec = jax.ShapeDtypeStruct(shape, BF16), once
        scratch = [pltpu.VMEM((TOK_DEV, 3 * cols), BF16)] * count
        scratch += [pltpu.VMEM(shape, F32)] * count
    else:
        last_shape, last_spec = jax.ShapeDtypeStruct((2 * half_tokens, 3 * cols), BF16), act_spec
        scratch = []
    return pl.pallas_call(
        functools.partial(ffn_kernel, cols, count, not sums, with_grad),
        grid=(2 * half,),
        out_shape=(row_shape,) * 4 + (last_shape,) * count,
        in_specs=[near_spec, far_spec] * 2
        + [once] * count
        + [near_spec, far_spec] * (len(sums) // 2),
        out_specs=(near_spec, far_spec) * 2 + (last_spec,) * count,
        scratch_shapes=scratch,
        compiler_params=pltpu.CompilerParams(vmem_limit_bytes=VMEM_LIMIT),
        cost_estimate=SMALL,
    )(*mid_halves, *cot_halves, *weights, *sums)


def ffn_grad_kernel(cols, mid_near, mid_far, cot_near, cot_far, act_ref, grad_ref):
    half = mid_near.shape[0]
    for near, far, part in (
        (mid_near, mid_far, slice(0, 2 * cols)),
        (cot_near, cot_far, slice(2 * cols, 3 * cols)),
    ):
        grad_ref[:, part] = (
            dot(near[...], act_ref[:half, part], 0, 0) + dot(far[...], act_ref[half:, part], 0, 0)
        ).astype(BF16)


def split_at(arrays, count):
    return *arrays[:count], list(arrays[count:])


def feed_forward_grad(mid_halves, cot_halves, act):
    half_tokens, width = mid_halves[0].shape
    cols = act.shape[1] // 3
    tile = 512 if width % 512 == 0 else width
    col_spec = pl.BlockSpec((half_tokens, tile), lambda i: (0, i))
    return pl.pallas_call(
        functools.partial(ffn_grad_kernel, cols),
        grid=(width // tile,),
        out_shape=jax.ShapeDtypeStruct((width, 3 * cols), BF16),
        in_specs=[col_spec] * 4
        + [pl.BlockSpec(act.shape, lambda i: (0, 0), pipeline_mode=pl.Buffered(1))],
        out_specs=pl.BlockSpec((tile, 3 * cols), lambda i: (i, 0)),
        compiler_params=pltpu.CompilerParams(vmem_limit_bytes=VMEM_LIMIT),
        cost_estimate=SMALL,
    )(*mid_halves, *cot_halves, act)


def slice_moves(n_plane, chunks, cols, total):
    for device in range(n_plane):
        for chunk in range(chunks):
            start = (device * chunks + chunk) * cols
            for kind in range(3):
                yield device, chunk, kind, kind * total + start, max(0, min(cols, total - start))


def pack_kernel(moves, cols, w_ref, out_ref):
    rows = w_ref.shape[0]
    for device, chunk, kind, source, real in moves:
        there = slice(device * rows, (device + 1) * rows)
        at = (chunk * 3 + kind) * cols
        if real:
            out_ref[there, at : at + real] = w_ref[:, source : source + real]
        if real < cols:
            out_ref[there, at + real : at + cols] = jnp.zeros((rows, cols - real), BF16)


def unpack_kernel(moves, cols, *refs):
    in_refs, out_ref = refs[:-1], refs[-1]
    rows = out_ref.shape[0]
    for device, chunk, kind, source, real in moves:
        if real:
            which = min(chunk, len(in_refs) - 1)
            at = ((chunk - which) * 3 + kind) * cols
            block = in_refs[which][device * rows : (device + 1) * rows, at : at + real]
            out_ref[:, source : source + real] = block.astype(F32)


def pack_slices(w_mlp, n_plane, chunks, cols):
    rows, total = w_mlp.shape[0], w_mlp.shape[1] // 3
    if rows % 16:
        wide = jnp.pad(
            w_mlp.reshape(rows, 3, total), ((0, 0), (0, 0), (0, n_plane * chunks * cols - total))
        )
        wide = wide.reshape(rows, 3, n_plane, chunks, cols).transpose(2, 0, 3, 1, 4)
        return wide.reshape(n_plane * rows, 3 * chunks * cols)
    moves = list(slice_moves(n_plane, chunks, cols, total))
    return pl.pallas_call(
        functools.partial(pack_kernel, moves, cols),
        out_shape=jax.ShapeDtypeStruct((n_plane * rows, 3 * chunks * cols), BF16),
        in_specs=vmem_specs(1),
        out_specs=vmem_specs(1)[0],
        compiler_params=pltpu.CompilerParams(vmem_limit_bytes=VMEM_LIMIT),
        cost_estimate=SMALL,
    )(w_mlp)


def unpack_slices(arrays, rows, total, n_plane, chunks, cols):
    if rows % 16:
        wide = jnp.concatenate(arrays, axis=1).reshape(n_plane, rows, chunks, 3, cols)
        wide = wide.transpose(1, 3, 0, 2, 4).reshape(rows, 3, -1)[:, :, :total]
        return wide.reshape(rows, 3 * total).astype(F32)
    moves = list(slice_moves(n_plane, chunks, cols, total))
    return pl.pallas_call(
        functools.partial(unpack_kernel, moves, cols),
        out_shape=jax.ShapeDtypeStruct((rows, 3 * total), F32),
        in_specs=vmem_specs(len(arrays)),
        out_specs=vmem_specs(1)[0],
        compiler_params=pltpu.CompilerParams(vmem_limit_bytes=VMEM_LIMIT),
        cost_estimate=SMALL,
    )(*arrays)


def weight_grad_kernel(n_dp, local_rows, across, dev_ref, *refs):
    count = len(across)
    lefts, rights = refs[: 2 * count : 2], refs[1 : 2 * count : 2]
    sides, (near_ref, far_ref, turned_ref, block_ref) = refs[2 * count : -4], refs[-4:]
    half = near_ref.shape[0] // (n_dp * local_rows)
    tile = block_ref.shape[1]

    def move(from_ref, at):
        cols = slice(at, at + from_ref.shape[1])
        for slot in range(2 * half):
            out_ref = near_ref if slot < half else far_ref
            for zone in range(n_dp):
                source = (zone * 2 * half + dev_ref[slot]) * local_rows
                source = pl.ds(pl.multiple_of(source, local_rows), local_rows)
                there = ((slot % half) * n_dp + zone) * local_rows
                out_ref[there : there + local_rows, cols] = from_ref[source, :]

    at = 0
    for left, right, is_across in zip(lefts, rights, across):
        turned_ref[...] = left[...].T
        cols = right.shape[0] if is_across else right.shape[1]
        for start in range(0, cols, tile):
            span = slice(start, start + tile)
            if is_across:
                block = dot(turned_ref[...], right[span, :], 1, 1)
            else:
                block = dot(turned_ref[...], right[:, span], 1, 0)
            block_ref[...] = block.astype(BF16)
            move(block_ref, at)
            at += tile
    for side_ref in sides:
        move(side_ref, at)


def weight_grads(plane, local_rows, terms, side=None):
    n_dp = lax.axis_size("dp")
    tokens, width = terms[0][0].shape
    widths = [right.shape[0 if across else 1] for _, right, across in terms]
    if local_rows % 16:
        full = jnp.concatenate(
            [dot(left, right, 0, 1 if across else 0) for left, right, across in terms], axis=1
        ).astype(BF16)
        if side is not None:
            full = jnp.concatenate([full, side], axis=1)
        full = full.reshape(n_dp, plane.count, local_rows, full.shape[1])
        blocks = [
            lax.dynamic_slice_in_dim(full, device, 1, 1).reshape(n_dp * local_rows, -1)
            for device in plane.devices
        ]
        half = plane.count // 2
        return jnp.concatenate(blocks[:half]), jnp.concatenate(blocks[half:])
    tile = 512
    extra = [] if side is None else [side]
    total = sum(widths) + sum(array.shape[1] for array in extra)
    shape = jax.ShapeDtypeStruct((width // 2, total), BF16)
    return pl.pallas_call(
        functools.partial(weight_grad_kernel, n_dp, local_rows, [term[2] for term in terms]),
        out_shape=(shape, shape),
        in_specs=[pl.BlockSpec(memory_space=pltpu.SMEM)]
        + vmem_specs(2 * len(terms) + len(extra)),
        out_specs=tuple(vmem_specs(2)),
        scratch_shapes=[pltpu.VMEM((width, tokens), BF16), pltpu.VMEM((width, tile), BF16)],
        compiler_params=pltpu.CompilerParams(vmem_limit_bytes=VMEM_LIMIT),
        cost_estimate=SMALL,
    )(jnp.stack(plane.devices), *[array for term in terms for array in term[:2]], *extra)


def spread_kernel(q_width, width, kv_cols, sum_ref, qkv_ref, out_ref, *side_refs):
    qkv_ref[:, :q_width] = sum_ref[:, :q_width].astype(F32)
    at = q_width + width
    qkv_ref[:, q_width:] = sum_ref[:, at : at + kv_cols].astype(F32)
    out_ref[...] = sum_ref[:, q_width:at].astype(F32)
    sides = sum_ref[:16, at + kv_cols :].astype(F32)
    for row, side_ref in enumerate(side_refs):
        side_ref[...] = sides[row : row + 1, : side_ref.shape[1]]


def spread_sums(attn_sum, q_width, width, kv_cols, sizes):
    rows = attn_sum.shape[0]
    at = q_width + width
    if rows % 16:
        full = attn_sum.astype(F32)
        grad_qkv = jnp.concatenate([full[:, :q_width], full[:, at : at + kv_cols]], axis=1)
        sides = [full[row, at + kv_cols : at + kv_cols + size] for row, size in enumerate(sizes)]
        return grad_qkv, full[:, q_width:at].T, *sides
    grad_qkv, grad_out, *sides = pl.pallas_call(
        functools.partial(spread_kernel, q_width, width, kv_cols),
        out_shape=(
            jax.ShapeDtypeStruct((rows, q_width + kv_cols), F32),
            jax.ShapeDtypeStruct((rows, width), F32),
            *(jax.ShapeDtypeStruct((1, size), F32) for size in sizes),
        ),
        in_specs=vmem_specs(1),
        out_specs=tuple(vmem_specs(2 + len(sizes))),
        compiler_params=pltpu.CompilerParams(vmem_limit_bytes=VMEM_LIMIT),
        cost_estimate=SMALL,
    )(attn_sum)
    return grad_qkv, grad_out.T, *(side.reshape(-1) for side in sides)


def after(array, *others):
    return lax.optimization_barrier((array, *others))[0]


class Plane:
    def __init__(self):
        ctx, uly = lax.axis_size("ctx"), lax.axis_size("uly")
        self.count = ctx * uly
        assert self.count & (self.count - 1) == 0 and ctx % 2 == 0
        self.me = lax.axis_index("ctx") * uly + lax.axis_index("uly")
        self.core = uly
        near = [1 << i for i in range(uly.bit_length() - 1)]
        far = [self.core << i for i in range(1, (ctx // 2).bit_length())]
        self.orders = (far + near, near + far)
        self.steps = len(near) + len(far)
        mine = (self.me // self.core) % 2 == 0
        masks = [[0], [0]]
        for which in (0, 1):
            for bit in self.orders[which]:
                masks[which] += [bit | mask for mask in masks[which]]
        pairs = list(zip(masks[0], masks[1]))
        near_slots = [jnp.where(mine, a, b) for a, b in pairs]
        far_slots = [jnp.where(mine, b, a) | self.core for a, b in pairs]
        self.devices = [self.me ^ mask for mask in near_slots + far_slots]

    def swap(self, array, step):
        pairs = []
        for i in range(self.count):
            if step == self.steps:
                bit = self.core
            else:
                bit = self.orders[(i // self.core) % 2][step]
            pairs.append((i, i ^ bit))
        return lax.ppermute(array, PLANE, pairs)

    def widen(self, rows, step, *others):
        moved = self.swap(rows, step)
        return jnp.concatenate([after(rows, *others) if others else rows, moved], axis=0)

    def gather(self, rows, late_step=None, *others):
        stages = [rows]
        for step in range(self.steps):
            if step == late_step:
                stages[-1] = after(stages[-1], *others)
            stages.append(self.widen(stages[-1], step))
        return stages + [self.swap(stages[-1], self.steps)]

    def fold(self, near, far, step):
        return (near.astype(F32) + self.swap(far, step).astype(F32)).astype(BF16)

    def fold_rest(self, rows, step):
        half = rows.shape[0] // 2
        return self.fold(rows[:half], rows[half:], step)


def place_info(spans, row_in_span, length_row):
    places = spans * TOK_DEV + row_in_span
    begins = jnp.zeros_like(places)
    end = jnp.int32(0)
    for doc in range(length_row.shape[0]):
        end = end + length_row[doc]
        begins = jnp.where(places >= end, jnp.maximum(begins, end), begins)
    return places, begins


def inverse_rms(values):
    return lax.rsqrt(jnp.mean(values * values, axis=-1, keepdims=True) + NORM_EPS)


def norm_backward(values, inverse, scaled):
    return inverse * scaled - values * (
        inverse**3 * jnp.mean(scaled * values, axis=-1, keepdims=True)
    )


def turn(heads, cosine, sine):
    half = HEAD // 2
    first, second = heads[..., :half], heads[..., half:]
    return jnp.concatenate(
        [first * cosine - second * sine, second * cosine + first * sine], axis=-1
    )


def shards(
    layer_input,
    span_order,
    doc_lengths,
    pad_mask,
    w_qkv,
    b_qkv,
    w_out,
    norm_gain_attn,
    norm_gain_mlp,
    w_mlp,
    cotangent,
):
    tok_rows, width = layer_input.shape
    n_dp = lax.axis_size("dp")
    n_plane = lax.axis_size("ctx") * lax.axis_size("uly")
    n_all = n_dp * n_plane
    plane = Plane()
    ffn_width = w_mlp.shape[1] // 3
    local_rows = w_mlp.shape[0]
    zone = local_rows * n_plane
    q_width, kv_width = HEADS * HEAD, KV_HEADS * HEAD
    qkv_width = q_width + 2 * kv_width
    bias_rows = b_qkv.shape[0]
    slice_tiles = -(-(ffn_width // LANES) // n_plane)
    chunks = max(c for c in (1, 2, 3) if slice_tiles % c == 0)
    chunk_cols = slice_tiles // chunks * LANES
    kv_cols = 2 * kv_width + LANES

    def swap_rows(array):
        return lax.all_to_all(array, PLANE, split_axis=0, concat_axis=0, tiled=True)

    def zone_gather(array):
        return lax.all_gather(array, "dp", axis=0, tiled=True)

    def zone_sum(array):
        return lax.psum_scatter(array, "dp", scatter_dimension=0, tiled=True)

    def whole_rows(pieces):
        cols = pieces[0].shape[1]
        full = jnp.zeros((n_dp, n_plane, local_rows, cols), BF16)
        slots = [block for piece in pieces for block in jnp.split(piece, n_plane // 2)]
        for device, block in zip(plane.devices, slots):
            piece = block.reshape(n_dp, 1, local_rows, cols)
            full = lax.dynamic_update_slice(full, piece, (0, device, 0, 0))
        return full.reshape(n_all * local_rows, cols)

    def device_blocks(array):
        cols = array.shape[1]
        full = array.reshape(n_dp, n_plane, local_rows, cols)
        return [
            lax.dynamic_slice_in_dim(full, device, 1, 1).reshape(n_dp * local_rows, cols)
            for device in plane.devices
        ]

    side = jnp.concatenate(
        [
            norm_gain_attn[:, None],
            norm_gain_mlp[:, None],
            jnp.zeros((local_rows, 62), BF16),
            jnp.pad(b_qkv[None, :], ((0, local_rows - 1), (0, 64 - bias_rows))),
        ],
        axis=1,
    )
    my_dp = lax.axis_index("dp")

    def zone_rows(array):
        full = jnp.zeros((n_dp, *array.shape), BF16)
        for step in range(n_dp):
            moved = array
            if step:
                moved = lax.ppermute(array, "dp", [(i, (i + step) % n_dp) for i in range(n_dp)])
            full = lax.dynamic_update_slice(
                full, moved[None], ((my_dp + n_dp - step) % n_dp, 0, 0)
            )
        return full.reshape(n_dp * array.shape[0], array.shape[1])

    kv_local = jnp.concatenate([w_qkv[:, q_width:], side], axis=1)
    attn_local = jnp.concatenate([kv_local, w_qkv[:, :q_width], w_out.T], axis=1)
    attn_zone = zone_rows(attn_local)
    kv_zone = attn_zone[:, : kv_local.shape[1]]
    big_zone = attn_zone[:, kv_local.shape[1] :]

    packed = pack_slices(after(w_mlp, attn_local), n_plane, chunks, chunk_cols)
    chunk_width = 3 * chunk_cols
    mlp_zone = swap_rows(packed)
    mlp_weights = [
        zone_gather(mlp_zone[:, chunk * chunk_width : (chunk + 1) * chunk_width])
        for chunk in range(chunks)
    ]

    w_kv_stages = plane.gather(kv_zone, 1, mlp_zone)
    w_q_stages = plane.gather(after(big_zone[:, :q_width], w_kv_stages[1]))
    w_out_near = after(big_zone[:, q_width:], w_q_stages[-2])
    w_out_near = plane.widen(w_out_near, 0)

    order_row, length_row, mask_row = after(
        (span_order[0], doc_lengths[0], pad_mask[0]), packed
    )
    row_in_span = jnp.arange(tok_rows, dtype=jnp.int32)
    stored_block = jnp.stack(plane.devices)
    spans = order_row[stored_block]
    own_place, own_begin = place_info(spans[0], row_in_span, length_row)
    flags = mask_row.reshape(n_plane, tok_rows)[stored_block]
    key_place = spans[:, None] * TOK_DEV + row_in_span[None, :]
    kinfo = jnp.stack(
        [jnp.where(flags == 1, key_place, FAR).reshape(-1), key_place.reshape(-1)], axis=1
    )
    qinfo = jnp.concatenate(
        [
            own_place[None],
            own_begin[None],
            flags[0][None],
            jnp.zeros((5, tok_rows), jnp.int32),
        ],
        axis=0,
    )
    need = ((spans <= spans[0]) & ((spans + 1) * TOK_DEV > own_begin[0])).astype(jnp.int32)

    inner = (own_place - own_begin).astype(F32)
    half = HEAD // 2
    frequency = ROPE_BASE ** (-(jnp.arange(half, dtype=F32) * 2.0) / HEAD)
    angles_t = frequency[:, None] * inner[None, :]
    cos_t, sin_t = jnp.cos(angles_t), jnp.sin(angles_t)
    cos_r, sin_r = cos_t.T[:, None, :], sin_t.T[:, None, :]

    w_kv_all = whole_rows(w_kv_stages[-2:])
    side_all = w_kv_all[:, 2 * kv_width :].astype(F32)
    gain_attn = side_all[:, 0]
    gain_mlp = side_all[:, 1]
    bias_all = side_all.reshape(n_all, local_rows, LANES)[:, 0, 64 : 64 + bias_rows].reshape(-1)

    inputs = layer_input.astype(F32)
    in_inverse = inverse_rms(inputs)
    normed_in = (inputs * in_inverse * gain_attn).astype(BF16)

    kv_proj = dot(normed_in, w_kv_all[:, : 2 * kv_width], 1, 0) + bias_all[q_width:]
    key_own = turn(kv_proj[:, :kv_width].reshape(tok_rows, KV_HEADS, HEAD), cos_r, sin_r)
    kv_own = jnp.concatenate([key_own.reshape(tok_rows, kv_width), kv_proj[:, kv_width:]], axis=1)
    kv_own = after(kv_own.astype(BF16), w_q_stages[-2])
    kv_stages = plane.gather(kv_own, 1, w_out_near)
    kv_all = jnp.concatenate(kv_stages[-2:], axis=0)
    w_q_all = whole_rows(w_q_stages[-2:])

    q_proj = dot(w_q_all, normed_in, 0, 1) + bias_all[:q_width, None]
    q_heads = q_proj.reshape(HEADS, 2, half, tok_rows)
    q_first, q_second = q_heads[:, 0], q_heads[:, 1]
    query_t = (
        jnp.stack(
            [q_first * cos_t - q_second * sin_t, q_second * cos_t + q_first * sin_t], axis=1
        )
        .reshape(q_width, tok_rows)
        .astype(BF16)
    )
    cot_near = plane.widen(after(cotangent, kv_stages[-2]), 0)
    need = after(need, w_out_near, cot_near)
    attended_t, lse = attention_forward(need, kinfo, qinfo, query_t, kv_all)
    for step in range(1, plane.steps):
        w_out_near = plane.widen(after(w_out_near, kv_stages[-2]), step, attended_t)
    w_out_all = whole_rows([w_out_near, plane.swap(w_out_near, plane.steps)])
    for step in range(1, plane.steps):
        cot_near = plane.widen(cot_near, step, attended_t)
    attended_t = after(attended_t, cot_near)

    middle = inputs + dot(attended_t, w_out_all, 0, 1)
    mid_inverse = inverse_rms(middle)
    normed_mid = (middle * mid_inverse * gain_mlp).astype(BF16)

    mid_near = normed_mid
    for step in range(plane.steps):
        mid_near = plane.widen(mid_near, step)
    cot_halves = cot_near, plane.swap(cot_near, plane.steps)
    mid_near = after(mid_near, mlp_weights[0])
    mid_halves = mid_near, plane.swap(mid_near, plane.steps)
    sums, chunk_grads = (), []
    if chunks > 1:
        *sums, chunk_grads = split_at(
            feed_forward(mid_halves, cot_halves, mlp_weights[:-1], (), True), 4
        )
    *sums, (extra,) = split_at(
        feed_forward(mid_halves, cot_halves, mlp_weights[-1:], tuple(sums), False), 4
    )

    def token_blocks(array):
        return [array[k * tok_rows : (k + 1) * tok_rows] for k in range(n_plane)]

    chunk_sums = [zone_sum(grad) for grad in chunk_grads]
    mid_fold = plane.fold(sums[0], sums[1], plane.steps)
    chunk_grads.append(feed_forward_grad(mid_halves, cot_halves, after(extra, mid_fold)))
    chunk_sums.append(zone_sum(chunk_grads[-1]))
    for step in range(plane.steps - 1, -1, -1):
        half = mid_fold.shape[0] // 2
        kept, sent = mid_fold[:half], mid_fold[half:]
        if step == plane.steps - 1:
            kept = after(kept, chunk_grads[-1])
        mid_fold = plane.fold(kept, sent, step)
        if step == 0:
            out_fold = plane.fold(after(sums[2], kept), sums[3], plane.steps)
    mid_grad = after(mid_fold, *chunk_sums[:-1][:1]).astype(F32)

    out_grad = cotangent.astype(F32)
    gain_mlp_grad = jnp.sum(mid_grad * (middle * mid_inverse), axis=0)
    middle_grad = out_grad + norm_backward(middle, mid_inverse, mid_grad * gain_mlp)
    middle_low = middle_grad.astype(BF16)
    attended_grad_t = dot(w_out_all, middle_low, 0, 1).astype(BF16)
    attended_grad_t = after(attended_grad_t, out_fold)
    query_grad, *kv_grads = attention_backward(
        need, kinfo, qinfo, cos_t, sin_t, query_t, kv_all, attended_t, attended_grad_t, lse
    )
    kv_fold = plane.fold(*kv_grads, plane.steps)
    mlp_out = after(out_fold, mid_fold)
    for step in range(plane.steps - 1, 0, -1):
        mlp_out = plane.fold_rest(mlp_out, step)
    big_grads = weight_grads(
        plane,
        local_rows,
        [
            (after(normed_in, mlp_out, kv_fold), query_grad, False),
            (middle_low, attended_t, True),
        ],
    )
    big_fold = plane.fold(*big_grads, plane.steps)
    mlp_out = plane.fold_rest(after(mlp_out, kv_fold), 0)
    for step in range(plane.steps - 1, -1, -1):
        rows = kv_fold.shape[0] // 2
        kept, sent = kv_fold[:rows], kv_fold[rows:]
        if step == plane.steps - 1:
            kept = after(kept, big_fold, *chunk_sums[1:-1])
        kv_fold = plane.fold(kept, sent, step)
    kv_back = after(kv_fold, mlp_out)
    kv_back = kv_back.astype(F32)
    key_back = turn(kv_back[:, :kv_width].reshape(tok_rows, KV_HEADS, HEAD), cos_r, -sin_r)
    projected_grad = jnp.concatenate(
        [query_grad, key_back.reshape(tok_rows, kv_width).astype(BF16), kv_back[:, kv_width:].astype(BF16)],
        axis=1,
    )
    in_grad = dot(projected_grad[:, :q_width], w_q_all, 1, 1) + dot(
        projected_grad[:, q_width:], w_kv_all[:, : 2 * kv_width], 1, 1
    )
    first_swapped = [swap_rows(after(array, in_grad)) for array in chunk_sums[:-1][:1]]
    gain_attn_grad = jnp.sum(in_grad * (inputs * in_inverse), axis=0)
    input_grad = middle_grad + norm_backward(inputs, in_inverse, in_grad * gain_attn)
    qkv_bias_grad = jnp.sum(projected_grad.astype(F32), axis=0)

    def side_rows(array):
        array = array.reshape(n_dp, n_plane, 1, -1)
        return jnp.pad(array, ((0, 0), (0, 0), (0, 0), (0, LANES - array.shape[-1])))

    side_grad = jnp.concatenate(
        [side_rows(gain_attn_grad), side_rows(gain_mlp_grad), side_rows(qkv_bias_grad)]
        + [jnp.zeros((n_dp, n_plane, 1, LANES), F32)] * 5,
        axis=2,
    )
    side_grad = jnp.pad(side_grad, ((0, 0), (0, 0), (0, local_rows - 8), (0, 0)))
    side_grad = side_grad.reshape(n_all * local_rows, LANES).astype(BF16)
    for step in range(plane.steps - 1, 0, -1):
        big_fold = plane.fold_rest(big_fold, step)
    small_grads = weight_grads(
        plane,
        local_rows,
        [(after(normed_in, big_fold), projected_grad[:, q_width:], False)],
        side_grad,
    )
    big_fold = plane.fold_rest(big_fold, 0)
    small_fold = plane.fold(*small_grads, plane.steps)
    for step in range(plane.steps - 1, -1, -1):
        rows = small_fold.shape[0] // 2
        kept, sent = small_fold[:rows], small_fold[rows:]
        if step == 0:
            kept = after(kept, chunk_sums[-1], *first_swapped)
        small_fold = plane.fold(kept, sent, step)
    attn_plane = jnp.concatenate([big_fold, small_fold], axis=1)
    grad_qkv, grad_out, grad_gain_attn, grad_gain_mlp, grad_bias = spread_sums(
        zone_sum(attn_plane), q_width, width, 2 * kv_width, (local_rows, local_rows, bias_rows)
    )

    late_sums = jnp.concatenate(chunk_sums[len(first_swapped) :], axis=1)
    swapped = first_swapped + [swap_rows(after(late_sums, attn_plane))]
    grad_mlp = unpack_slices(swapped, local_rows, ffn_width, n_plane, chunks, chunk_cols)
    block_output = (middle + mlp_out.astype(F32)).astype(BF16)
    return (
        block_output,
        input_grad,
        grad_qkv,
        grad_bias,
        grad_out,
        grad_gain_attn,
        grad_gain_mlp,
        grad_mlp,
    )


def solution(mesh):
    rows = P(EVERY, None)
    flat = P(EVERY)
    columns = P(None, EVERY)
    batch = P("dp", None)
    return jax.shard_map(
        shards,
        mesh=mesh,
        in_specs=(rows, batch, batch, batch, rows, flat, columns, flat, flat, rows, rows),
        out_specs=(rows, rows, rows, flat, columns, flat, flat, rows),
        check_vma=False,
    )
```

```python
import functools

import jax
import jax.numpy as jnp
from jax import lax
from jax.experimental import pallas as pl
from jax.experimental.pallas import tpu as pltpu
from jax.sharding import PartitionSpec as P

HEADS = 12
KV_HEADS = 2
HEAD = 128
TOK_DEV = 256
LANES = 128
GROUP = HEADS // KV_HEADS

NORM_EPS = 1e-06
ROPE_BASE = 1000000.0
NEG_FILL = -1e30
LOG2E = 1.4426950408889634
SCALE = HEAD ** (-0.5)
FAR = 1 << 30
PLANE = ("ctx", "uly")
EVERY = ("dp", "ctx", "uly")
VMEM_LIMIT = 56 * 1024 * 1024
SMALL = pl.CostEstimate(flops=1024, bytes_accessed=1024, transcendentals=0)
F32 = jnp.float32
BF16 = jnp.bfloat16


def dot(left, right, left_dim, right_dim):
    return lax.dot_general(
        left, right, (((left_dim,), (right_dim,)), ((), ())), preferred_element_type=F32
    )


def block_bias(kinfo_ref, qinfo_ref, rows):
    info = kinfo_ref[rows, :]
    usable, place = info[:, 0:1], info[:, 1:2]
    q_place, q_begin = qinfo_ref[0:1, :], qinfo_ref[1:2, :]
    allowed = ((usable <= q_place) & (usable >= q_begin)) | (place == q_place)
    return jnp.where(allowed, 0.0, NEG_FILL)


def beside(array_ref, wide_ref):
    cols = array_ref.shape[1]
    for head in range(HEADS):
        group, place = divmod(head, GROUP)
        wide_ref[group * HEAD : (group + 1) * HEAD, place * cols : (place + 1) * cols] = array_ref[
            head * HEAD : (head + 1) * HEAD, :
        ]


def attn_fwd_kernel(
    need_ref, kinfo_ref, qinfo_ref, q_ref, kv_ref, o_ref, lse_ref, m_ref, l_ref, acc_ref, wide_ref
):
    blocks = kv_ref.shape[0] // TOK_DEV
    cols = q_ref.shape[1]
    beside(q_ref, wide_ref)
    m_ref[...] = jnp.full(m_ref.shape, NEG_FILL, F32)
    l_ref[...] = jnp.zeros(l_ref.shape, F32)
    acc_ref[...] = jnp.zeros(acc_ref.shape, F32)

    def one_block(block, carry):
        @pl.when(need_ref[block] > 0)
        def _():
            rows = pl.ds(pl.multiple_of(block * TOK_DEV, TOK_DEV), TOK_DEV)
            bias = jnp.concatenate([block_bias(kinfo_ref, qinfo_ref, rows)] * GROUP, axis=1)
            for group in range(KV_HEADS):
                key = kv_ref[rows, group * HEAD : (group + 1) * HEAD]
                value = kv_ref[rows, (KV_HEADS + group) * HEAD : (KV_HEADS + group + 1) * HEAD]
                span = slice(group * HEAD, (group + 1) * HEAD)
                row = slice(group, group + 1)
                scores = dot(key, wide_ref[span, :], 1, 0) * (SCALE * LOG2E) + bias
                old = m_ref[row, :]
                new = jnp.maximum(old, jnp.max(scores, axis=0, keepdims=True))
                weights = jnp.exp2(scores - new)
                factor = jnp.exp2(old - new)
                m_ref[row, :] = new
                l_ref[row, :] = l_ref[row, :] * factor + jnp.sum(weights, axis=0, keepdims=True)
                acc_ref[span, :] = acc_ref[span, :] * factor + dot(
                    value.T, weights.astype(BF16), 1, 0
                )

        return carry

    lax.fori_loop(0, blocks, one_block, 0)
    real = qinfo_ref[2:3, :].astype(F32)
    lse_ref[...] = jnp.zeros(lse_ref.shape, F32)
    lse_ref[:KV_HEADS, :] = m_ref[:KV_HEADS, :] + jnp.log(l_ref[:KV_HEADS, :]) * LOG2E
    for head in range(HEADS):
        group, place = divmod(head, GROUP)
        there = slice(place * cols, (place + 1) * cols)
        total = l_ref[group : group + 1, there]
        o_ref[head * HEAD : (head + 1) * HEAD, :] = (
            acc_ref[group * HEAD : (group + 1) * HEAD, there] * (real / total)
        ).astype(BF16)


def attn_bwd_kernel(
    need_ref,
    kinfo_ref,
    qinfo_ref,
    cos_ref,
    sin_ref,
    q_ref,
    kv_ref,
    o_ref,
    do_ref,
    lse_ref,
    dq_ref,
    near_ref,
    far_ref,
    dots_ref,
    acc_ref,
    wide_ref,
    low_ref,
):
    blocks = kv_ref.shape[0] // TOK_DEV
    cols = q_ref.shape[1]
    real = qinfo_ref[2:3, :].astype(F32)
    beside(q_ref, wide_ref)
    for head in range(HEADS):
        group, place = divmod(head, GROUP)
        there = slice(place * cols, (place + 1) * cols)
        span = slice(head * HEAD, (head + 1) * HEAD)
        grad = do_ref[span, :].astype(F32) * real
        low_ref[group * HEAD : (group + 1) * HEAD, there] = grad.astype(BF16)
        dots_ref[group : group + 1, there] = jnp.sum(
            grad * o_ref[span, :].astype(F32), axis=0, keepdims=True
        )
    acc_ref[...] = jnp.zeros(acc_ref.shape, F32)

    def one_block(dkv_ref, first, at, carry):
        block = first + at
        rows = pl.ds(pl.multiple_of(block * TOK_DEV, TOK_DEV), TOK_DEV)
        out_rows = pl.ds(pl.multiple_of(at * TOK_DEV, TOK_DEV), TOK_DEV)

        @pl.when(need_ref[block] == 0)
        def _():
            dkv_ref[out_rows, :] = jnp.zeros((TOK_DEV, 2 * KV_HEADS * HEAD), BF16)

        @pl.when(need_ref[block] > 0)
        def _():
            bias = jnp.concatenate([block_bias(kinfo_ref, qinfo_ref, rows)] * GROUP, axis=1)
            for group in range(KV_HEADS):
                key_cols = slice(group * HEAD, (group + 1) * HEAD)
                value_cols = slice((KV_HEADS + group) * HEAD, (KV_HEADS + group + 1) * HEAD)
                key = kv_ref[rows, key_cols]
                value = kv_ref[rows, value_cols]
                query, grad = wide_ref[key_cols, :], low_ref[key_cols, :]
                row = slice(group, group + 1)
                scores = dot(key, query, 1, 0) * (SCALE * LOG2E) + bias
                probs = jnp.exp2(scores - lse_ref[row, :])
                prob_grad = dot(value, grad, 1, 0)
                score_grad = (probs * (prob_grad - dots_ref[row, :])).astype(BF16)
                acc_ref[key_cols, :] += dot(key.T, score_grad, 1, 0)
                dkv_ref[out_rows, key_cols] = (dot(score_grad, query, 1, 1) * SCALE).astype(BF16)
                dkv_ref[out_rows, value_cols] = dot(probs.astype(BF16), grad, 1, 1).astype(BF16)

        return carry

    half_blocks = blocks // 2
    lax.fori_loop(0, half_blocks, functools.partial(one_block, near_ref, 0), 0)
    lax.fori_loop(0, half_blocks, functools.partial(one_block, far_ref, half_blocks), 0)
    cosine, sine = cos_ref[...], sin_ref[...]
    half = HEAD // 2
    for head in range(HEADS):
        group, place = divmod(head, GROUP)
        there = slice(place * cols, (place + 1) * cols)
        whole = acc_ref[group * HEAD : (group + 1) * HEAD, there] * SCALE
        whole = whole.astype(BF16).astype(F32)
        first, second = whole[:half], whole[half:]
        turned = jnp.concatenate(
            [first * cosine + second * sine, second * cosine - first * sine], axis=0
        )
        dq_ref[:, head * HEAD : (head + 1) * HEAD] = turned.T.astype(BF16)


def vmem_specs(count):
    return [pl.BlockSpec(memory_space=pltpu.VMEM)] * count


def attention_forward(need, kinfo, qinfo, query_t, kv_all):
    rows = query_t.shape[1]
    return pl.pallas_call(
        attn_fwd_kernel,
        out_shape=(
            jax.ShapeDtypeStruct((HEADS * HEAD, rows), BF16),
            jax.ShapeDtypeStruct((8, GROUP * rows), F32),
        ),
        in_specs=[pl.BlockSpec(memory_space=pltpu.SMEM)] + vmem_specs(4),
        out_specs=tuple(vmem_specs(2)),
        scratch_shapes=[
            pltpu.VMEM((8, GROUP * rows), F32),
            pltpu.VMEM((8, GROUP * rows), F32),
            pltpu.VMEM((KV_HEADS * HEAD, GROUP * rows), F32),
            pltpu.VMEM((KV_HEADS * HEAD, GROUP * rows), BF16),
        ],
        compiler_params=pltpu.CompilerParams(vmem_limit_bytes=VMEM_LIMIT),
        cost_estimate=SMALL,
    )(need, kinfo, qinfo, query_t, kv_all)


def attention_backward(need, kinfo, qinfo, cos_t, sin_t, query_t, kv_all, out_t, grad_t, lse):
    rows = query_t.shape[1]
    return pl.pallas_call(
        attn_bwd_kernel,
        out_shape=(
            jax.ShapeDtypeStruct((rows, HEADS * HEAD), BF16),
            jax.ShapeDtypeStruct((kv_all.shape[0] // 2, kv_all.shape[1]), BF16),
            jax.ShapeDtypeStruct((kv_all.shape[0] // 2, kv_all.shape[1]), BF16),
        ),
        in_specs=[pl.BlockSpec(memory_space=pltpu.SMEM)] + vmem_specs(9),
        out_specs=tuple(vmem_specs(3)),
        scratch_shapes=[
            pltpu.VMEM((8, GROUP * rows), F32),
            pltpu.VMEM((KV_HEADS * HEAD, GROUP * rows), F32),
            pltpu.VMEM((KV_HEADS * HEAD, GROUP * rows), BF16),
            pltpu.VMEM((KV_HEADS * HEAD, GROUP * rows), BF16),
        ],
        compiler_params=pltpu.CompilerParams(vmem_limit_bytes=VMEM_LIMIT),
        cost_estimate=SMALL,
    )(need, kinfo, qinfo, cos_t, sin_t, query_t, kv_all, out_t, grad_t, lse)


def ffn_tile(cols, mid_ref, cot_ref, w_refs, sums, outs, act_refs, acc_refs):
    mid_grad = out = None
    if sums:
        mid_grad, out = sums[0][...].astype(F32), sums[1][...].astype(F32)
    for w_ref, act_ref in zip(w_refs, act_refs):
        both = dot(mid_ref[...], w_ref[:, : 2 * cols], 1, 0)
        hidden_grad = dot(cot_ref[...], w_ref[:, 2 * cols :], 1, 0)
        gate, up = both[:, :cols], both[:, cols:]
        share = 1.0 / (1.0 + jnp.exp(-gate))
        acted = gate * share
        act_ref[:, :cols] = (
            hidden_grad * up * (share * (1.0 + gate * (1.0 - share)))
        ).astype(BF16)
        act_ref[:, cols : 2 * cols] = (hidden_grad * acted).astype(BF16)
        act_ref[:, 2 * cols :] = (acted * up).astype(BF16)
        mid_term = dot(act_ref[:, : 2 * cols], w_ref[:, : 2 * cols], 1, 1)
        out_term = dot(act_ref[:, 2 * cols :], w_ref[:, 2 * cols :], 1, 1)
        mid_grad = mid_term if mid_grad is None else mid_grad + mid_term
        out = out_term if out is None else out + out_term
    outs[0][...] = mid_grad.astype(BF16)
    outs[1][...] = out.astype(BF16)
    for act_ref, acc_ref in zip(act_refs, acc_refs):
        acc_ref[:, : 2 * cols] += dot(mid_ref[...], act_ref[:, : 2 * cols], 0, 0)
        acc_ref[:, 2 * cols :] += dot(cot_ref[...], act_ref[:, 2 * cols :], 0, 0)


def ffn_kernel(cols, count, first, with_grad, *refs):
    mids, cots, w_refs, refs = refs[:2], refs[2:4], refs[4 : 4 + count], refs[4 + count :]
    mid_sums = out_sums = None
    if not first:
        mid_sums, out_sums, refs = refs[:2], refs[2:4], refs[4:]
    mid_outs, out_outs, refs = refs[:2], refs[2:4], refs[4:]
    if with_grad:
        grad_refs, act_refs, acc_refs = refs[:count], refs[count : 2 * count], refs[2 * count :]
    else:
        grad_refs, act_refs, acc_refs = (), refs, ()
    step, last = pl.program_id(0), pl.num_programs(0) - 1
    near = step < pl.num_programs(0) // 2

    @pl.when(step == 0)
    def _():
        for acc_ref in acc_refs:
            acc_ref[...] = jnp.zeros(acc_ref.shape, F32)

    def tile(which):
        sums = () if first else (mid_sums[which], out_sums[which])
        outs = (mid_outs[which], out_outs[which])
        ffn_tile(cols, mids[which], cots[which], w_refs, sums, outs, act_refs, acc_refs)

    pl.when(near)(lambda: tile(0))
    pl.when(jnp.logical_not(near))(lambda: tile(1))

    @pl.when(step == last)
    def _():
        for grad_ref, acc_ref in zip(grad_refs, acc_refs):
            grad_ref[...] = acc_ref[...].astype(BF16)


def feed_forward(mid_halves, cot_halves, weights, sums, with_grad):
    half_tokens, width = mid_halves[0].shape
    count, shape = len(weights), weights[0].shape
    cols = shape[1] // 3
    half = half_tokens // TOK_DEV
    near_spec = pl.BlockSpec((TOK_DEV, width), lambda i: (jnp.minimum(i, half - 1), 0))
    far_spec = pl.BlockSpec((TOK_DEV, width), lambda i: (jnp.maximum(i - half, 0), 0))
    act_spec = pl.BlockSpec((TOK_DEV, 3 * cols), lambda i: (i, 0))
    once = pl.BlockSpec(shape, lambda i: (0, 0), pipeline_mode=pl.Buffered(1))
    row_shape = jax.ShapeDtypeStruct((half_tokens, width), BF16)
    if with_grad:
        last_shape, last_spec = jax.ShapeDtypeStruct(shape, BF16), once
        scratch = [pltpu.VMEM((TOK_DEV, 3 * cols), BF16)] * count
        scratch += [pltpu.VMEM(shape, F32)] * count
    else:
        last_shape, last_spec = jax.ShapeDtypeStruct((2 * half_tokens, 3 * cols), BF16), act_spec
        scratch = []
    return pl.pallas_call(
        functools.partial(ffn_kernel, cols, count, not sums, with_grad),
        grid=(2 * half,),
        out_shape=(row_shape,) * 4 + (last_shape,) * count,
        in_specs=[near_spec, far_spec] * 2
        + [once] * count
        + [near_spec, far_spec] * (len(sums) // 2),
        out_specs=(near_spec, far_spec) * 2 + (last_spec,) * count,
        scratch_shapes=scratch,
        compiler_params=pltpu.CompilerParams(vmem_limit_bytes=VMEM_LIMIT),
        cost_estimate=SMALL,
    )(*mid_halves, *cot_halves, *weights, *sums)


def ffn_grad_kernel(cols, mid_near, mid_far, cot_near, cot_far, act_ref, grad_ref):
    half = mid_near.shape[0]
    for near, far, part in (
        (mid_near, mid_far, slice(0, 2 * cols)),
        (cot_near, cot_far, slice(2 * cols, 3 * cols)),
    ):
        grad_ref[:, part] = (
            dot(near[...], act_ref[:half, part], 0, 0) + dot(far[...], act_ref[half:, part], 0, 0)
        ).astype(BF16)


def split_at(arrays, count):
    return *arrays[:count], list(arrays[count:])


def feed_forward_grad(mid_halves, cot_halves, act):
    half_tokens, width = mid_halves[0].shape
    cols = act.shape[1] // 3
    tile = 512 if width % 512 == 0 else width
    col_spec = pl.BlockSpec((half_tokens, tile), lambda i: (0, i))
    return pl.pallas_call(
        functools.partial(ffn_grad_kernel, cols),
        grid=(width // tile,),
        out_shape=jax.ShapeDtypeStruct((width, 3 * cols), BF16),
        in_specs=[col_spec] * 4
        + [pl.BlockSpec(act.shape, lambda i: (0, 0), pipeline_mode=pl.Buffered(1))],
        out_specs=pl.BlockSpec((tile, 3 * cols), lambda i: (i, 0)),
        compiler_params=pltpu.CompilerParams(vmem_limit_bytes=VMEM_LIMIT),
        cost_estimate=SMALL,
    )(*mid_halves, *cot_halves, act)


def slice_moves(n_plane, chunks, cols, total):
    for device in range(n_plane):
        for chunk in range(chunks):
            start = (device * chunks + chunk) * cols
            for kind in range(3):
                yield device, chunk, kind, kind * total + start, max(0, min(cols, total - start))


def pack_kernel(moves, cols, w_ref, out_ref):
    rows = w_ref.shape[0]
    for device, chunk, kind, source, real in moves:
        there = slice(device * rows, (device + 1) * rows)
        at = (chunk * 3 + kind) * cols
        if real:
            out_ref[there, at : at + real] = w_ref[:, source : source + real]
        if real < cols:
            out_ref[there, at + real : at + cols] = jnp.zeros((rows, cols - real), BF16)


def unpack_kernel(moves, cols, *refs):
    in_refs, out_ref = refs[:-1], refs[-1]
    rows = out_ref.shape[0]
    for device, chunk, kind, source, real in moves:
        if real:
            which = min(chunk, len(in_refs) - 1)
            at = ((chunk - which) * 3 + kind) * cols
            block = in_refs[which][device * rows : (device + 1) * rows, at : at + real]
            out_ref[:, source : source + real] = block.astype(F32)


def pack_slices(w_mlp, n_plane, chunks, cols):
    rows, total = w_mlp.shape[0], w_mlp.shape[1] // 3
    if rows % 16:
        wide = jnp.pad(
            w_mlp.reshape(rows, 3, total), ((0, 0), (0, 0), (0, n_plane * chunks * cols - total))
        )
        wide = wide.reshape(rows, 3, n_plane, chunks, cols).transpose(2, 0, 3, 1, 4)
        return wide.reshape(n_plane * rows, 3 * chunks * cols)
    moves = list(slice_moves(n_plane, chunks, cols, total))
    return pl.pallas_call(
        functools.partial(pack_kernel, moves, cols),
        out_shape=jax.ShapeDtypeStruct((n_plane * rows, 3 * chunks * cols), BF16),
        in_specs=vmem_specs(1),
        out_specs=vmem_specs(1)[0],
        compiler_params=pltpu.CompilerParams(vmem_limit_bytes=VMEM_LIMIT),
        cost_estimate=SMALL,
    )(w_mlp)


def unpack_slices(arrays, rows, total, n_plane, chunks, cols):
    if rows % 16:
        wide = jnp.concatenate(arrays, axis=1).reshape(n_plane, rows, chunks, 3, cols)
        wide = wide.transpose(1, 3, 0, 2, 4).reshape(rows, 3, -1)[:, :, :total]
        return wide.reshape(rows, 3 * total).astype(F32)
    moves = list(slice_moves(n_plane, chunks, cols, total))
    return pl.pallas_call(
        functools.partial(unpack_kernel, moves, cols),
        out_shape=jax.ShapeDtypeStruct((rows, 3 * total), F32),
        in_specs=vmem_specs(len(arrays)),
        out_specs=vmem_specs(1)[0],
        compiler_params=pltpu.CompilerParams(vmem_limit_bytes=VMEM_LIMIT),
        cost_estimate=SMALL,
    )(*arrays)


def weight_grad_kernel(n_dp, local_rows, across, dev_ref, *refs):
    count = len(across)
    lefts, rights = refs[: 2 * count : 2], refs[1 : 2 * count : 2]
    sides, (near_ref, far_ref, turned_ref, block_ref) = refs[2 * count : -4], refs[-4:]
    half = near_ref.shape[0] // (n_dp * local_rows)
    tile = block_ref.shape[1]

    def move(from_ref, at):
        cols = slice(at, at + from_ref.shape[1])
        for slot in range(2 * half):
            out_ref = near_ref if slot < half else far_ref
            for zone in range(n_dp):
                source = (zone * 2 * half + dev_ref[slot]) * local_rows
                source = pl.ds(pl.multiple_of(source, local_rows), local_rows)
                there = ((slot % half) * n_dp + zone) * local_rows
                out_ref[there : there + local_rows, cols] = from_ref[source, :]

    at = 0
    for left, right, is_across in zip(lefts, rights, across):
        turned_ref[...] = left[...].T
        cols = right.shape[0] if is_across else right.shape[1]
        for start in range(0, cols, tile):
            span = slice(start, start + tile)
            if is_across:
                block = dot(turned_ref[...], right[span, :], 1, 1)
            else:
                block = dot(turned_ref[...], right[:, span], 1, 0)
            block_ref[...] = block.astype(BF16)
            move(block_ref, at)
            at += tile
    for side_ref in sides:
        move(side_ref, at)


def weight_grads(plane, local_rows, terms, side=None):
    n_dp = lax.axis_size("dp")
    tokens, width = terms[0][0].shape
    widths = [right.shape[0 if across else 1] for _, right, across in terms]
    if local_rows % 16:
        full = jnp.concatenate(
            [dot(left, right, 0, 1 if across else 0) for left, right, across in terms], axis=1
        ).astype(BF16)
        if side is not None:
            full = jnp.concatenate([full, side], axis=1)
        full = full.reshape(n_dp, plane.count, local_rows, full.shape[1])
        blocks = [
            lax.dynamic_slice_in_dim(full, device, 1, 1).reshape(n_dp * local_rows, -1)
            for device in plane.devices
        ]
        half = plane.count // 2
        return jnp.concatenate(blocks[:half]), jnp.concatenate(blocks[half:])
    tile = 512
    extra = [] if side is None else [side]
    total = sum(widths) + sum(array.shape[1] for array in extra)
    shape = jax.ShapeDtypeStruct((width // 2, total), BF16)
    return pl.pallas_call(
        functools.partial(weight_grad_kernel, n_dp, local_rows, [term[2] for term in terms]),
        out_shape=(shape, shape),
        in_specs=[pl.BlockSpec(memory_space=pltpu.SMEM)]
        + vmem_specs(2 * len(terms) + len(extra)),
        out_specs=tuple(vmem_specs(2)),
        scratch_shapes=[pltpu.VMEM((width, tokens), BF16), pltpu.VMEM((width, tile), BF16)],
        compiler_params=pltpu.CompilerParams(vmem_limit_bytes=VMEM_LIMIT),
        cost_estimate=SMALL,
    )(jnp.stack(plane.devices), *[array for term in terms for array in term[:2]], *extra)


def spread_kernel(q_width, width, kv_cols, sum_ref, qkv_ref, out_ref, *side_refs):
    qkv_ref[:, :q_width] = sum_ref[:, :q_width].astype(F32)
    at = q_width + width
    qkv_ref[:, q_width:] = sum_ref[:, at : at + kv_cols].astype(F32)
    out_ref[...] = sum_ref[:, q_width:at].astype(F32)
    sides = sum_ref[:16, at + kv_cols :].astype(F32)
    for row, side_ref in enumerate(side_refs):
        side_ref[...] = sides[row : row + 1, : side_ref.shape[1]]


def spread_sums(attn_sum, q_width, width, kv_cols, sizes):
    rows = attn_sum.shape[0]
    at = q_width + width
    if rows % 16:
        full = attn_sum.astype(F32)
        grad_qkv = jnp.concatenate([full[:, :q_width], full[:, at : at + kv_cols]], axis=1)
        sides = [full[row, at + kv_cols : at + kv_cols + size] for row, size in enumerate(sizes)]
        return grad_qkv, full[:, q_width:at].T, *sides
    grad_qkv, grad_out, *sides = pl.pallas_call(
        functools.partial(spread_kernel, q_width, width, kv_cols),
        out_shape=(
            jax.ShapeDtypeStruct((rows, q_width + kv_cols), F32),
            jax.ShapeDtypeStruct((rows, width), F32),
            *(jax.ShapeDtypeStruct((1, size), F32) for size in sizes),
        ),
        in_specs=vmem_specs(1),
        out_specs=tuple(vmem_specs(2 + len(sizes))),
        compiler_params=pltpu.CompilerParams(vmem_limit_bytes=VMEM_LIMIT),
        cost_estimate=SMALL,
    )(attn_sum)
    return grad_qkv, grad_out.T, *(side.reshape(-1) for side in sides)


def after(array, *others):
    return lax.optimization_barrier((array, *others))[0]


class Plane:
    def __init__(self):
        ctx, uly = lax.axis_size("ctx"), lax.axis_size("uly")
        self.count = ctx * uly
        assert self.count & (self.count - 1) == 0 and ctx % 2 == 0
        self.me = lax.axis_index("ctx") * uly + lax.axis_index("uly")
        self.core = uly
        near = [1 << i for i in range(uly.bit_length() - 1)]
        far = [self.core << i for i in range(1, (ctx // 2).bit_length())]
        self.orders = (far + near, near + far)
        self.steps = len(near) + len(far)
        mine = (self.me // self.core) % 2 == 0
        masks = [[0], [0]]
        for which in (0, 1):
            for bit in self.orders[which]:
                masks[which] += [bit | mask for mask in masks[which]]
        pairs = list(zip(masks[0], masks[1]))
        near_slots = [jnp.where(mine, a, b) for a, b in pairs]
        far_slots = [jnp.where(mine, b, a) | self.core for a, b in pairs]
        self.devices = [self.me ^ mask for mask in near_slots + far_slots]

    def swap(self, array, step):
        pairs = []
        for i in range(self.count):
            if step == self.steps:
                bit = self.core
            else:
                bit = self.orders[(i // self.core) % 2][step]
            pairs.append((i, i ^ bit))
        return lax.ppermute(array, PLANE, pairs)

    def widen(self, rows, step, *others):
        moved = self.swap(rows, step)
        return jnp.concatenate([after(rows, *others) if others else rows, moved], axis=0)

    def gather(self, rows, late_step=None, *others):
        stages = [rows]
        for step in range(self.steps):
            if step == late_step:
                stages[-1] = after(stages[-1], *others)
            stages.append(self.widen(stages[-1], step))
        return stages + [self.swap(stages[-1], self.steps)]

    def fold(self, near, far, step):
        return (near.astype(F32) + self.swap(far, step).astype(F32)).astype(BF16)

    def fold_rest(self, rows, step):
        half = rows.shape[0] // 2
        return self.fold(rows[:half], rows[half:], step)


def place_info(spans, row_in_span, length_row):
    places = spans * TOK_DEV + row_in_span
    begins = jnp.zeros_like(places)
    end = jnp.int32(0)
    for doc in range(length_row.shape[0]):
        end = end + length_row[doc]
        begins = jnp.where(places >= end, jnp.maximum(begins, end), begins)
    return places, begins


def inverse_rms(values):
    return lax.rsqrt(jnp.mean(values * values, axis=-1, keepdims=True) + NORM_EPS)


def norm_backward(values, inverse, scaled):
    return inverse * scaled - values * (
        inverse**3 * jnp.mean(scaled * values, axis=-1, keepdims=True)
    )


def turn(heads, cosine, sine):
    half = HEAD // 2
    first, second = heads[..., :half], heads[..., half:]
    return jnp.concatenate(
        [first * cosine - second * sine, second * cosine + first * sine], axis=-1
    )


def shards(
    layer_input,
    span_order,
    doc_lengths,
    pad_mask,
    w_qkv,
    b_qkv,
    w_out,
    norm_gain_attn,
    norm_gain_mlp,
    w_mlp,
    cotangent,
):
    tok_rows, width = layer_input.shape
    n_dp = lax.axis_size("dp")
    n_plane = lax.axis_size("ctx") * lax.axis_size("uly")
    n_all = n_dp * n_plane
    plane = Plane()
    ffn_width = w_mlp.shape[1] // 3
    local_rows = w_mlp.shape[0]
    zone = local_rows * n_plane
    q_width, kv_width = HEADS * HEAD, KV_HEADS * HEAD
    qkv_width = q_width + 2 * kv_width
    bias_rows = b_qkv.shape[0]
    slice_tiles = -(-(ffn_width // LANES) // n_plane)
    chunks = max(c for c in (1, 2, 3) if slice_tiles % c == 0)
    chunk_cols = slice_tiles // chunks * LANES
    kv_cols = 2 * kv_width + LANES

    def swap_rows(array):
        return lax.all_to_all(array, PLANE, split_axis=0, concat_axis=0, tiled=True)

    def zone_gather(array):
        return lax.all_gather(array, "dp", axis=0, tiled=True)

    def zone_sum(array):
        return lax.psum_scatter(array, "dp", scatter_dimension=0, tiled=True)

    def whole_rows(pieces):
        cols = pieces[0].shape[1]
        full = jnp.zeros((n_dp, n_plane, local_rows, cols), BF16)
        slots = [block for piece in pieces for block in jnp.split(piece, n_plane // 2)]
        for device, block in zip(plane.devices, slots):
            piece = block.reshape(n_dp, 1, local_rows, cols)
            full = lax.dynamic_update_slice(full, piece, (0, device, 0, 0))
        return full.reshape(n_all * local_rows, cols)

    def device_blocks(array):
        cols = array.shape[1]
        full = array.reshape(n_dp, n_plane, local_rows, cols)
        return [
            lax.dynamic_slice_in_dim(full, device, 1, 1).reshape(n_dp * local_rows, cols)
            for device in plane.devices
        ]

    side = jnp.concatenate(
        [
            norm_gain_attn[:, None],
            norm_gain_mlp[:, None],
            jnp.zeros((local_rows, 62), BF16),
            jnp.pad(b_qkv[None, :], ((0, local_rows - 1), (0, 64 - bias_rows))),
        ],
        axis=1,
    )
    my_dp = lax.axis_index("dp")

    def zone_rows(array):
        full = jnp.zeros((n_dp, *array.shape), BF16)
        for step in range(n_dp):
            moved = array
            if step:
                moved = lax.ppermute(array, "dp", [(i, (i + step) % n_dp) for i in range(n_dp)])
            full = lax.dynamic_update_slice(
                full, moved[None], ((my_dp + n_dp - step) % n_dp, 0, 0)
            )
        return full.reshape(n_dp * array.shape[0], array.shape[1])

    kv_local = jnp.concatenate([w_qkv[:, q_width:], side], axis=1)
    attn_local = jnp.concatenate([kv_local, w_qkv[:, :q_width], w_out.T], axis=1)
    attn_zone = zone_rows(attn_local)
    kv_zone = attn_zone[:, : kv_local.shape[1]]
    big_zone = attn_zone[:, kv_local.shape[1] :]

    packed = pack_slices(after(w_mlp, attn_local), n_plane, chunks, chunk_cols)
    chunk_width = 3 * chunk_cols
    mlp_zone = swap_rows(packed)
    mlp_weights = [
        zone_gather(mlp_zone[:, chunk * chunk_width : (chunk + 1) * chunk_width])
        for chunk in range(chunks)
    ]

    w_kv_stages = plane.gather(kv_zone, 1, mlp_zone)
    w_q_stages = plane.gather(after(big_zone[:, :q_width], w_kv_stages[1]))
    w_out_near = after(big_zone[:, q_width:], w_q_stages[-2])
    w_out_near = plane.widen(w_out_near, 0)

    order_row, length_row, mask_row = after(
        (span_order[0], doc_lengths[0], pad_mask[0]), packed
    )
    row_in_span = jnp.arange(tok_rows, dtype=jnp.int32)
    stored_block = jnp.stack(plane.devices)
    spans = order_row[stored_block]
    own_place, own_begin = place_info(spans[0], row_in_span, length_row)
    flags = mask_row.reshape(n_plane, tok_rows)[stored_block]
    key_place = spans[:, None] * TOK_DEV + row_in_span[None, :]
    kinfo = jnp.stack(
        [jnp.where(flags == 1, key_place, FAR).reshape(-1), key_place.reshape(-1)], axis=1
    )
    qinfo = jnp.concatenate(
        [
            own_place[None],
            own_begin[None],
            flags[0][None],
            jnp.zeros((5, tok_rows), jnp.int32),
        ],
        axis=0,
    )
    need = ((spans <= spans[0]) & ((spans + 1) * TOK_DEV > own_begin[0])).astype(jnp.int32)

    inner = (own_place - own_begin).astype(F32)
    half = HEAD // 2
    frequency = ROPE_BASE ** (-(jnp.arange(half, dtype=F32) * 2.0) / HEAD)
    angles_t = frequency[:, None] * inner[None, :]
    cos_t, sin_t = jnp.cos(angles_t), jnp.sin(angles_t)
    cos_r, sin_r = cos_t.T[:, None, :], sin_t.T[:, None, :]

    w_kv_all = whole_rows(w_kv_stages[-2:])
    side_all = w_kv_all[:, 2 * kv_width :].astype(F32)
    gain_attn = side_all[:, 0]
    gain_mlp = side_all[:, 1]
    bias_all = side_all.reshape(n_all, local_rows, LANES)[:, 0, 64 : 64 + bias_rows].reshape(-1)

    inputs = layer_input.astype(F32)
    in_inverse = inverse_rms(inputs)
    normed_in = (inputs * in_inverse * gain_attn).astype(BF16)

    kv_proj = dot(normed_in, w_kv_all[:, : 2 * kv_width], 1, 0) + bias_all[q_width:]
    key_own = turn(kv_proj[:, :kv_width].reshape(tok_rows, KV_HEADS, HEAD), cos_r, sin_r)
    kv_own = jnp.concatenate([key_own.reshape(tok_rows, kv_width), kv_proj[:, kv_width:]], axis=1)
    kv_own = after(kv_own.astype(BF16), w_q_stages[-2])
    kv_stages = plane.gather(kv_own, 1, w_out_near)
    kv_all = jnp.concatenate(kv_stages[-2:], axis=0)
    w_q_all = whole_rows(w_q_stages[-2:])

    q_proj = dot(w_q_all, normed_in, 0, 1) + bias_all[:q_width, None]
    q_heads = q_proj.reshape(HEADS, 2, half, tok_rows)
    q_first, q_second = q_heads[:, 0], q_heads[:, 1]
    query_t = (
        jnp.stack(
            [q_first * cos_t - q_second * sin_t, q_second * cos_t + q_first * sin_t], axis=1
        )
        .reshape(q_width, tok_rows)
        .astype(BF16)
    )
    cot_near = plane.widen(after(cotangent, kv_stages[-2]), 0)
    need = after(need, w_out_near, cot_near)
    attended_t, lse = attention_forward(need, kinfo, qinfo, query_t, kv_all)
    for step in range(1, plane.steps):
        w_out_near = plane.widen(after(w_out_near, kv_stages[-2]), step, attended_t)
    w_out_all = whole_rows([w_out_near, plane.swap(w_out_near, plane.steps)])
    for step in range(1, plane.steps):
        cot_near = plane.widen(cot_near, step, attended_t)
    attended_t = after(attended_t, cot_near)

    middle = inputs + dot(attended_t, w_out_all, 0, 1)
    mid_inverse = inverse_rms(middle)
    normed_mid = (middle * mid_inverse * gain_mlp).astype(BF16)

    mid_near = normed_mid
    for step in range(plane.steps):
        mid_near = plane.widen(mid_near, step)
    cot_halves = cot_near, plane.swap(cot_near, plane.steps)
    mid_near = after(mid_near, mlp_weights[0])
    mid_halves = mid_near, plane.swap(mid_near, plane.steps)
    sums, chunk_grads = (), []
    if chunks > 1:
        *sums, chunk_grads = split_at(
            feed_forward(mid_halves, cot_halves, mlp_weights[:-1], (), True), 4
        )
    *sums, (extra,) = split_at(
        feed_forward(mid_halves, cot_halves, mlp_weights[-1:], tuple(sums), False), 4
    )

    def token_blocks(array):
        return [array[k * tok_rows : (k + 1) * tok_rows] for k in range(n_plane)]

    chunk_sums = [zone_sum(grad) for grad in chunk_grads]
    mid_fold = plane.fold(sums[0], sums[1], plane.steps)
    chunk_grads.append(feed_forward_grad(mid_halves, cot_halves, after(extra, mid_fold)))
    chunk_sums.append(zone_sum(chunk_grads[-1]))
    for step in range(plane.steps - 1, -1, -1):
        half = mid_fold.shape[0] // 2
        kept, sent = mid_fold[:half], mid_fold[half:]
        if step == plane.steps - 1:
            kept = after(kept, chunk_grads[-1])
        mid_fold = plane.fold(kept, sent, step)
        if step == 0:
            out_fold = plane.fold(after(sums[2], kept), sums[3], plane.steps)
    mid_grad = after(mid_fold, *chunk_sums[:-1][:1]).astype(F32)

    out_grad = cotangent.astype(F32)
    gain_mlp_grad = jnp.sum(mid_grad * (middle * mid_inverse), axis=0)
    middle_grad = out_grad + norm_backward(middle, mid_inverse, mid_grad * gain_mlp)
    middle_low = middle_grad.astype(BF16)
    attended_grad_t = dot(w_out_all, middle_low, 0, 1).astype(BF16)
    attended_grad_t = after(attended_grad_t, out_fold)
    query_grad, *kv_grads = attention_backward(
        need, kinfo, qinfo, cos_t, sin_t, query_t, kv_all, attended_t, attended_grad_t, lse
    )
    kv_fold = plane.fold(*kv_grads, plane.steps)
    mlp_out = after(out_fold, mid_fold)
    for step in range(plane.steps - 1, 0, -1):
        mlp_out = plane.fold_rest(mlp_out, step)
    big_grads = weight_grads(
        plane,
        local_rows,
        [
            (after(normed_in, mlp_out, kv_fold), query_grad, False),
            (middle_low, attended_t, True),
        ],
    )
    big_fold = plane.fold(*big_grads, plane.steps)
    mlp_out = plane.fold_rest(after(mlp_out, kv_fold), 0)
    for step in range(plane.steps - 1, -1, -1):
        rows = kv_fold.shape[0] // 2
        kept, sent = kv_fold[:rows], kv_fold[rows:]
        if step == plane.steps - 1:
            kept = after(kept, big_fold, *chunk_sums[1:-1])
        kv_fold = plane.fold(kept, sent, step)
    kv_back = after(kv_fold, mlp_out)
    kv_back = kv_back.astype(F32)
    key_back = turn(kv_back[:, :kv_width].reshape(tok_rows, KV_HEADS, HEAD), cos_r, -sin_r)
    projected_grad = jnp.concatenate(
        [query_grad, key_back.reshape(tok_rows, kv_width).astype(BF16), kv_back[:, kv_width:].astype(BF16)],
        axis=1,
    )
    in_grad = dot(projected_grad[:, :q_width], w_q_all, 1, 1) + dot(
        projected_grad[:, q_width:], w_kv_all[:, : 2 * kv_width], 1, 1
    )
    first_swapped = [swap_rows(after(array, in_grad)) for array in chunk_sums[:-1][:1]]
    gain_attn_grad = jnp.sum(in_grad * (inputs * in_inverse), axis=0)
    input_grad = middle_grad + norm_backward(inputs, in_inverse, in_grad * gain_attn)
    qkv_bias_grad = jnp.sum(projected_grad.astype(F32), axis=0)

    def side_rows(array):
        array = array.reshape(n_dp, n_plane, 1, -1)
        return jnp.pad(array, ((0, 0), (0, 0), (0, 0), (0, LANES - array.shape[-1])))

    side_grad = jnp.concatenate(
        [side_rows(gain_attn_grad), side_rows(gain_mlp_grad), side_rows(qkv_bias_grad)]
        + [jnp.zeros((n_dp, n_plane, 1, LANES), F32)] * 5,
        axis=2,
    )
    side_grad = jnp.pad(side_grad, ((0, 0), (0, 0), (0, local_rows - 8), (0, 0)))
    side_grad = side_grad.reshape(n_all * local_rows, LANES).astype(BF16)
    for step in range(plane.steps - 1, 0, -1):
        big_fold = plane.fold_rest(big_fold, step)
    small_grads = weight_grads(
        plane,
        local_rows,
        [(after(normed_in, big_fold), projected_grad[:, q_width:], False)],
        side_grad,
    )
    big_fold = plane.fold_rest(big_fold, 0)
    small_fold = plane.fold(*small_grads, plane.steps)
    for step in range(plane.steps - 1, -1, -1):
        rows = small_fold.shape[0] // 2
        kept, sent = small_fold[:rows], small_fold[rows:]
        if step == 0:
            kept = after(kept, chunk_sums[-1], *first_swapped)
        small_fold = plane.fold(kept, sent, step)
    attn_plane = jnp.concatenate([big_fold, small_fold], axis=1)
    grad_qkv, grad_out, grad_gain_attn, grad_gain_mlp, grad_bias = spread_sums(
        zone_sum(attn_plane), q_width, width, 2 * kv_width, (local_rows, local_rows, bias_rows)
    )

    late_sums = jnp.concatenate(chunk_sums[len(first_swapped) :], axis=1)
    swapped = first_swapped + [swap_rows(after(late_sums, attn_plane))]
    grad_mlp = unpack_slices(swapped, local_rows, ffn_width, n_plane, chunks, chunk_cols)
    block_output = (middle + mlp_out.astype(F32)).astype(BF16)
    return (
        block_output,
        input_grad,
        grad_qkv,
        grad_bias,
        grad_out,
        grad_gain_attn,
        grad_gain_mlp,
        grad_mlp,
    )


def solution(mesh):
    rows = P(EVERY, None)
    flat = P(EVERY)
    columns = P(None, EVERY)
    batch = P("dp", None)
    return jax.shard_map(
        shards,
        mesh=mesh,
        in_specs=(rows, batch, batch, batch, rows, flat, columns, flat, flat, rows, rows),
        out_specs=(rows, rows, rows, flat, columns, flat, flat, rows),
        check_vma=False,
    )
```

```python
import functools

import jax
import jax.numpy as jnp
from jax import lax
from jax.experimental import pallas as pl
from jax.experimental.pallas import tpu as pltpu
from jax.sharding import PartitionSpec as P

HEADS = 12
KV_HEADS = 2
HEAD = 128
TOK_DEV = 256
LANES = 128
GROUP = HEADS // KV_HEADS

NORM_EPS = 1e-06
ROPE_BASE = 1000000.0
NEG_FILL = -1e30
LOG2E = 1.4426950408889634
SCALE = HEAD ** (-0.5)
FAR = 1 << 30
PLANE = ("ctx", "uly")
EVERY = ("dp", "ctx", "uly")
VMEM_LIMIT = 56 * 1024 * 1024
SMALL = pl.CostEstimate(flops=1024, bytes_accessed=1024, transcendentals=0)
F32 = jnp.float32
BF16 = jnp.bfloat16


def dot(left, right, left_dim, right_dim):
    return lax.dot_general(
        left, right, (((left_dim,), (right_dim,)), ((), ())), preferred_element_type=F32
    )


def block_bias(kinfo_ref, qinfo_ref, rows):
    info = kinfo_ref[rows, :]
    usable, place = info[:, 0:1], info[:, 1:2]
    q_place, q_begin = qinfo_ref[0:1, :], qinfo_ref[1:2, :]
    allowed = ((usable <= q_place) & (usable >= q_begin)) | (place == q_place)
    return jnp.where(allowed, 0.0, NEG_FILL)


def beside(array_ref, wide_ref):
    cols = array_ref.shape[1]
    for head in range(HEADS):
        group, place = divmod(head, GROUP)
        wide_ref[group * HEAD : (group + 1) * HEAD, place * cols : (place + 1) * cols] = array_ref[
            head * HEAD : (head + 1) * HEAD, :
        ]


def attn_fwd_kernel(
    need_ref, kinfo_ref, qinfo_ref, q_ref, kv_ref, o_ref, lse_ref, m_ref, l_ref, acc_ref, wide_ref
):
    blocks = kv_ref.shape[0] // TOK_DEV
    cols = q_ref.shape[1]
    beside(q_ref, wide_ref)
    m_ref[...] = jnp.full(m_ref.shape, NEG_FILL, F32)
    l_ref[...] = jnp.zeros(l_ref.shape, F32)
    acc_ref[...] = jnp.zeros(acc_ref.shape, F32)

    def one_block(block, carry):
        @pl.when(need_ref[block] > 0)
        def _():
            rows = pl.ds(pl.multiple_of(block * TOK_DEV, TOK_DEV), TOK_DEV)
            bias = jnp.concatenate([block_bias(kinfo_ref, qinfo_ref, rows)] * GROUP, axis=1)
            for group in range(KV_HEADS):
                key = kv_ref[rows, group * HEAD : (group + 1) * HEAD]
                value = kv_ref[rows, (KV_HEADS + group) * HEAD : (KV_HEADS + group + 1) * HEAD]
                span = slice(group * HEAD, (group + 1) * HEAD)
                row = slice(group, group + 1)
                scores = dot(key, wide_ref[span, :], 1, 0) * (SCALE * LOG2E) + bias
                old = m_ref[row, :]
                new = jnp.maximum(old, jnp.max(scores, axis=0, keepdims=True))
                weights = jnp.exp2(scores - new)
                factor = jnp.exp2(old - new)
                m_ref[row, :] = new
                l_ref[row, :] = l_ref[row, :] * factor + jnp.sum(weights, axis=0, keepdims=True)
                acc_ref[span, :] = acc_ref[span, :] * factor + dot(
                    value.T, weights.astype(BF16), 1, 0
                )

        return carry

    lax.fori_loop(0, blocks, one_block, 0)
    real = qinfo_ref[2:3, :].astype(F32)
    lse_ref[...] = jnp.zeros(lse_ref.shape, F32)
    lse_ref[:KV_HEADS, :] = m_ref[:KV_HEADS, :] + jnp.log(l_ref[:KV_HEADS, :]) * LOG2E
    for head in range(HEADS):
        group, place = divmod(head, GROUP)
        there = slice(place * cols, (place + 1) * cols)
        total = l_ref[group : group + 1, there]
        o_ref[head * HEAD : (head + 1) * HEAD, :] = (
            acc_ref[group * HEAD : (group + 1) * HEAD, there] * (real / total)
        ).astype(BF16)


def attn_bwd_kernel(
    need_ref,
    kinfo_ref,
    qinfo_ref,
    cos_ref,
    sin_ref,
    q_ref,
    kv_ref,
    o_ref,
    do_ref,
    lse_ref,
    dq_ref,
    near_ref,
    far_ref,
    dots_ref,
    acc_ref,
    wide_ref,
    low_ref,
):
    blocks = kv_ref.shape[0] // TOK_DEV
    cols = q_ref.shape[1]
    real = qinfo_ref[2:3, :].astype(F32)
    beside(q_ref, wide_ref)
    for head in range(HEADS):
        group, place = divmod(head, GROUP)
        there = slice(place * cols, (place + 1) * cols)
        span = slice(head * HEAD, (head + 1) * HEAD)
        grad = do_ref[span, :].astype(F32) * real
        low_ref[group * HEAD : (group + 1) * HEAD, there] = grad.astype(BF16)
        dots_ref[group : group + 1, there] = jnp.sum(
            grad * o_ref[span, :].astype(F32), axis=0, keepdims=True
        )
    acc_ref[...] = jnp.zeros(acc_ref.shape, F32)

    def one_block(dkv_ref, first, at, carry):
        block = first + at
        rows = pl.ds(pl.multiple_of(block * TOK_DEV, TOK_DEV), TOK_DEV)
        out_rows = pl.ds(pl.multiple_of(at * TOK_DEV, TOK_DEV), TOK_DEV)

        @pl.when(need_ref[block] == 0)
        def _():
            dkv_ref[out_rows, :] = jnp.zeros((TOK_DEV, 2 * KV_HEADS * HEAD), BF16)

        @pl.when(need_ref[block] > 0)
        def _():
            bias = jnp.concatenate([block_bias(kinfo_ref, qinfo_ref, rows)] * GROUP, axis=1)
            for group in range(KV_HEADS):
                key_cols = slice(group * HEAD, (group + 1) * HEAD)
                value_cols = slice((KV_HEADS + group) * HEAD, (KV_HEADS + group + 1) * HEAD)
                key = kv_ref[rows, key_cols]
                value = kv_ref[rows, value_cols]
                query, grad = wide_ref[key_cols, :], low_ref[key_cols, :]
                row = slice(group, group + 1)
                scores = dot(key, query, 1, 0) * (SCALE * LOG2E) + bias
                probs = jnp.exp2(scores - lse_ref[row, :])
                prob_grad = dot(value, grad, 1, 0)
                score_grad = (probs * (prob_grad - dots_ref[row, :])).astype(BF16)
                acc_ref[key_cols, :] += dot(key.T, score_grad, 1, 0)
                dkv_ref[out_rows, key_cols] = (dot(score_grad, query, 1, 1) * SCALE).astype(BF16)
                dkv_ref[out_rows, value_cols] = dot(probs.astype(BF16), grad, 1, 1).astype(BF16)

        return carry

    half_blocks = blocks // 2
    lax.fori_loop(0, half_blocks, functools.partial(one_block, near_ref, 0), 0)
    lax.fori_loop(0, half_blocks, functools.partial(one_block, far_ref, half_blocks), 0)
    cosine, sine = cos_ref[...], sin_ref[...]
    half = HEAD // 2
    for head in range(HEADS):
        group, place = divmod(head, GROUP)
        there = slice(place * cols, (place + 1) * cols)
        whole = acc_ref[group * HEAD : (group + 1) * HEAD, there] * SCALE
        whole = whole.astype(BF16).astype(F32)
        first, second = whole[:half], whole[half:]
        turned = jnp.concatenate(
            [first * cosine + second * sine, second * cosine - first * sine], axis=0
        )
        dq_ref[:, head * HEAD : (head + 1) * HEAD] = turned.T.astype(BF16)


def vmem_specs(count):
    return [pl.BlockSpec(memory_space=pltpu.VMEM)] * count


def attention_forward(need, kinfo, qinfo, query_t, kv_all):
    rows = query_t.shape[1]
    return pl.pallas_call(
        attn_fwd_kernel,
        out_shape=(
            jax.ShapeDtypeStruct((HEADS * HEAD, rows), BF16),
            jax.ShapeDtypeStruct((8, GROUP * rows), F32),
        ),
        in_specs=[pl.BlockSpec(memory_space=pltpu.SMEM)] + vmem_specs(4),
        out_specs=tuple(vmem_specs(2)),
        scratch_shapes=[
            pltpu.VMEM((8, GROUP * rows), F32),
            pltpu.VMEM((8, GROUP * rows), F32),
            pltpu.VMEM((KV_HEADS * HEAD, GROUP * rows), F32),
            pltpu.VMEM((KV_HEADS * HEAD, GROUP * rows), BF16),
        ],
        compiler_params=pltpu.CompilerParams(vmem_limit_bytes=VMEM_LIMIT),
        cost_estimate=SMALL,
    )(need, kinfo, qinfo, query_t, kv_all)


def attention_backward(need, kinfo, qinfo, cos_t, sin_t, query_t, kv_all, out_t, grad_t, lse):
    rows = query_t.shape[1]
    return pl.pallas_call(
        attn_bwd_kernel,
        out_shape=(
            jax.ShapeDtypeStruct((rows, HEADS * HEAD), BF16),
            jax.ShapeDtypeStruct((kv_all.shape[0] // 2, kv_all.shape[1]), BF16),
            jax.ShapeDtypeStruct((kv_all.shape[0] // 2, kv_all.shape[1]), BF16),
        ),
        in_specs=[pl.BlockSpec(memory_space=pltpu.SMEM)] + vmem_specs(9),
        out_specs=tuple(vmem_specs(3)),
        scratch_shapes=[
            pltpu.VMEM((8, GROUP * rows), F32),
            pltpu.VMEM((KV_HEADS * HEAD, GROUP * rows), F32),
            pltpu.VMEM((KV_HEADS * HEAD, GROUP * rows), BF16),
            pltpu.VMEM((KV_HEADS * HEAD, GROUP * rows), BF16),
        ],
        compiler_params=pltpu.CompilerParams(vmem_limit_bytes=VMEM_LIMIT),
        cost_estimate=SMALL,
    )(need, kinfo, qinfo, cos_t, sin_t, query_t, kv_all, out_t, grad_t, lse)


def ffn_tile(cols, mid_ref, cot_ref, w_refs, sums, outs, act_refs, acc_refs):
    mid_grad = out = None
    if sums:
        mid_grad, out = sums[0][...].astype(F32), sums[1][...].astype(F32)
    for w_ref, act_ref in zip(w_refs, act_refs):
        both = dot(mid_ref[...], w_ref[:, : 2 * cols], 1, 0)
        hidden_grad = dot(cot_ref[...], w_ref[:, 2 * cols :], 1, 0)
        gate, up = both[:, :cols], both[:, cols:]
        share = 1.0 / (1.0 + jnp.exp(-gate))
        acted = gate * share
        act_ref[:, :cols] = (
            hidden_grad * up * (share * (1.0 + gate * (1.0 - share)))
        ).astype(BF16)
        act_ref[:, cols : 2 * cols] = (hidden_grad * acted).astype(BF16)
        act_ref[:, 2 * cols :] = (acted * up).astype(BF16)
        mid_term = dot(act_ref[:, : 2 * cols], w_ref[:, : 2 * cols], 1, 1)
        out_term = dot(act_ref[:, 2 * cols :], w_ref[:, 2 * cols :], 1, 1)
        mid_grad = mid_term if mid_grad is None else mid_grad + mid_term
        out = out_term if out is None else out + out_term
    outs[0][...] = mid_grad.astype(BF16)
    outs[1][...] = out.astype(BF16)
    for act_ref, acc_ref in zip(act_refs, acc_refs):
        acc_ref[:, : 2 * cols] += dot(mid_ref[...], act_ref[:, : 2 * cols], 0, 0)
        acc_ref[:, 2 * cols :] += dot(cot_ref[...], act_ref[:, 2 * cols :], 0, 0)


def ffn_kernel(cols, count, first, with_grad, *refs):
    mids, cots, w_refs, refs = refs[:2], refs[2:4], refs[4 : 4 + count], refs[4 + count :]
    mid_sums = out_sums = None
    if not first:
        mid_sums, out_sums, refs = refs[:2], refs[2:4], refs[4:]
    mid_outs, out_outs, refs = refs[:2], refs[2:4], refs[4:]
    if with_grad:
        grad_refs, act_refs, acc_refs = refs[:count], refs[count : 2 * count], refs[2 * count :]
    else:
        grad_refs, act_refs, acc_refs = (), refs, ()
    step, last = pl.program_id(0), pl.num_programs(0) - 1
    near = step < pl.num_programs(0) // 2

    @pl.when(step == 0)
    def _():
        for acc_ref in acc_refs:
            acc_ref[...] = jnp.zeros(acc_ref.shape, F32)

    def tile(which):
        sums = () if first else (mid_sums[which], out_sums[which])
        outs = (mid_outs[which], out_outs[which])
        ffn_tile(cols, mids[which], cots[which], w_refs, sums, outs, act_refs, acc_refs)

    pl.when(near)(lambda: tile(0))
    pl.when(jnp.logical_not(near))(lambda: tile(1))

    @pl.when(step == last)
    def _():
        for grad_ref, acc_ref in zip(grad_refs, acc_refs):
            grad_ref[...] = acc_ref[...].astype(BF16)


def feed_forward(mid_halves, cot_halves, weights, sums, with_grad):
    half_tokens, width = mid_halves[0].shape
    count, shape = len(weights), weights[0].shape
    cols = shape[1] // 3
    half = half_tokens // TOK_DEV
    near_spec = pl.BlockSpec((TOK_DEV, width), lambda i: (jnp.minimum(i, half - 1), 0))
    far_spec = pl.BlockSpec((TOK_DEV, width), lambda i: (jnp.maximum(i - half, 0), 0))
    act_spec = pl.BlockSpec((TOK_DEV, 3 * cols), lambda i: (i, 0))
    once = pl.BlockSpec(shape, lambda i: (0, 0), pipeline_mode=pl.Buffered(1))
    row_shape = jax.ShapeDtypeStruct((half_tokens, width), BF16)
    if with_grad:
        last_shape, last_spec = jax.ShapeDtypeStruct(shape, BF16), once
        scratch = [pltpu.VMEM((TOK_DEV, 3 * cols), BF16)] * count
        scratch += [pltpu.VMEM(shape, F32)] * count
    else:
        last_shape, last_spec = jax.ShapeDtypeStruct((2 * half_tokens, 3 * cols), BF16), act_spec
        scratch = []
    return pl.pallas_call(
        functools.partial(ffn_kernel, cols, count, not sums, with_grad),
        grid=(2 * half,),
        out_shape=(row_shape,) * 4 + (last_shape,) * count,
        in_specs=[near_spec, far_spec] * 2
        + [once] * count
        + [near_spec, far_spec] * (len(sums) // 2),
        out_specs=(near_spec, far_spec) * 2 + (last_spec,) * count,
        scratch_shapes=scratch,
        compiler_params=pltpu.CompilerParams(vmem_limit_bytes=VMEM_LIMIT),
        cost_estimate=SMALL,
    )(*mid_halves, *cot_halves, *weights, *sums)


def ffn_grad_kernel(cols, mid_near, mid_far, cot_near, cot_far, act_ref, grad_ref):
    half = mid_near.shape[0]
    for near, far, part in (
        (mid_near, mid_far, slice(0, 2 * cols)),
        (cot_near, cot_far, slice(2 * cols, 3 * cols)),
    ):
        grad_ref[:, part] = (
            dot(near[...], act_ref[:half, part], 0, 0) + dot(far[...], act_ref[half:, part], 0, 0)
        ).astype(BF16)


def split_at(arrays, count):
    return *arrays[:count], list(arrays[count:])


def feed_forward_grad(mid_halves, cot_halves, act):
    half_tokens, width = mid_halves[0].shape
    cols = act.shape[1] // 3
    tile = 512 if width % 512 == 0 else width
    col_spec = pl.BlockSpec((half_tokens, tile), lambda i: (0, i))
    return pl.pallas_call(
        functools.partial(ffn_grad_kernel, cols),
        grid=(width // tile,),
        out_shape=jax.ShapeDtypeStruct((width, 3 * cols), BF16),
        in_specs=[col_spec] * 4
        + [pl.BlockSpec(act.shape, lambda i: (0, 0), pipeline_mode=pl.Buffered(1))],
        out_specs=pl.BlockSpec((tile, 3 * cols), lambda i: (i, 0)),
        compiler_params=pltpu.CompilerParams(vmem_limit_bytes=VMEM_LIMIT),
        cost_estimate=SMALL,
    )(*mid_halves, *cot_halves, act)


def slice_moves(n_plane, chunks, cols, total):
    for device in range(n_plane):
        for chunk in range(chunks):
            start = (device * chunks + chunk) * cols
            for kind in range(3):
                yield device, chunk, kind, kind * total + start, max(0, min(cols, total - start))


def pack_kernel(moves, cols, w_ref, out_ref):
    rows = w_ref.shape[0]
    for device, chunk, kind, source, real in moves:
        there = slice(device * rows, (device + 1) * rows)
        at = (chunk * 3 + kind) * cols
        if real:
            out_ref[there, at : at + real] = w_ref[:, source : source + real]
        if real < cols:
            out_ref[there, at + real : at + cols] = jnp.zeros((rows, cols - real), BF16)


def unpack_kernel(moves, cols, *refs):
    in_refs, out_ref = refs[:-1], refs[-1]
    rows = out_ref.shape[0]
    for device, chunk, kind, source, real in moves:
        if real:
            which = min(chunk, len(in_refs) - 1)
            at = ((chunk - which) * 3 + kind) * cols
            block = in_refs[which][device * rows : (device + 1) * rows, at : at + real]
            out_ref[:, source : source + real] = block.astype(F32)


def pack_slices(w_mlp, n_plane, chunks, cols):
    rows, total = w_mlp.shape[0], w_mlp.shape[1] // 3
    if rows % 16:
        wide = jnp.pad(
            w_mlp.reshape(rows, 3, total), ((0, 0), (0, 0), (0, n_plane * chunks * cols - total))
        )
        wide = wide.reshape(rows, 3, n_plane, chunks, cols).transpose(2, 0, 3, 1, 4)
        return wide.reshape(n_plane * rows, 3 * chunks * cols)
    moves = list(slice_moves(n_plane, chunks, cols, total))
    return pl.pallas_call(
        functools.partial(pack_kernel, moves, cols),
        out_shape=jax.ShapeDtypeStruct((n_plane * rows, 3 * chunks * cols), BF16),
        in_specs=vmem_specs(1),
        out_specs=vmem_specs(1)[0],
        compiler_params=pltpu.CompilerParams(vmem_limit_bytes=VMEM_LIMIT),
        cost_estimate=SMALL,
    )(w_mlp)


def unpack_slices(arrays, rows, total, n_plane, chunks, cols):
    if rows % 16:
        wide = jnp.concatenate(arrays, axis=1).reshape(n_plane, rows, chunks, 3, cols)
        wide = wide.transpose(1, 3, 0, 2, 4).reshape(rows, 3, -1)[:, :, :total]
        return wide.reshape(rows, 3 * total).astype(F32)
    moves = list(slice_moves(n_plane, chunks, cols, total))
    return pl.pallas_call(
        functools.partial(unpack_kernel, moves, cols),
        out_shape=jax.ShapeDtypeStruct((rows, 3 * total), F32),
        in_specs=vmem_specs(len(arrays)),
        out_specs=vmem_specs(1)[0],
        compiler_params=pltpu.CompilerParams(vmem_limit_bytes=VMEM_LIMIT),
        cost_estimate=SMALL,
    )(*arrays)


def weight_grad_kernel(n_dp, local_rows, across, dev_ref, *refs):
    count = len(across)
    lefts, rights = refs[: 2 * count : 2], refs[1 : 2 * count : 2]
    sides, (near_ref, far_ref, turned_ref, block_ref) = refs[2 * count : -4], refs[-4:]
    half = near_ref.shape[0] // (n_dp * local_rows)
    tile = block_ref.shape[1]

    def move(from_ref, at):
        cols = slice(at, at + from_ref.shape[1])
        for slot in range(2 * half):
            out_ref = near_ref if slot < half else far_ref
            for zone in range(n_dp):
                source = (zone * 2 * half + dev_ref[slot]) * local_rows
                source = pl.ds(pl.multiple_of(source, local_rows), local_rows)
                there = ((slot % half) * n_dp + zone) * local_rows
                out_ref[there : there + local_rows, cols] = from_ref[source, :]

    at = 0
    for left, right, is_across in zip(lefts, rights, across):
        turned_ref[...] = left[...].T
        cols = right.shape[0] if is_across else right.shape[1]
        for start in range(0, cols, tile):
            span = slice(start, start + tile)
            if is_across:
                block = dot(turned_ref[...], right[span, :], 1, 1)
            else:
                block = dot(turned_ref[...], right[:, span], 1, 0)
            block_ref[...] = block.astype(BF16)
            move(block_ref, at)
            at += tile
    for side_ref in sides:
        move(side_ref, at)


def weight_grads(plane, local_rows, terms, side=None):
    n_dp = lax.axis_size("dp")
    tokens, width = terms[0][0].shape
    widths = [right.shape[0 if across else 1] for _, right, across in terms]
    if local_rows % 16:
        full = jnp.concatenate(
            [dot(left, right, 0, 1 if across else 0) for left, right, across in terms], axis=1
        ).astype(BF16)
        if side is not None:
            full = jnp.concatenate([full, side], axis=1)
        full = full.reshape(n_dp, plane.count, local_rows, full.shape[1])
        blocks = [
            lax.dynamic_slice_in_dim(full, device, 1, 1).reshape(n_dp * local_rows, -1)
            for device in plane.devices
        ]
        half = plane.count // 2
        return jnp.concatenate(blocks[:half]), jnp.concatenate(blocks[half:])
    tile = 512
    extra = [] if side is None else [side]
    total = sum(widths) + sum(array.shape[1] for array in extra)
    shape = jax.ShapeDtypeStruct((width // 2, total), BF16)
    return pl.pallas_call(
        functools.partial(weight_grad_kernel, n_dp, local_rows, [term[2] for term in terms]),
        out_shape=(shape, shape),
        in_specs=[pl.BlockSpec(memory_space=pltpu.SMEM)]
        + vmem_specs(2 * len(terms) + len(extra)),
        out_specs=tuple(vmem_specs(2)),
        scratch_shapes=[pltpu.VMEM((width, tokens), BF16), pltpu.VMEM((width, tile), BF16)],
        compiler_params=pltpu.CompilerParams(vmem_limit_bytes=VMEM_LIMIT),
        cost_estimate=SMALL,
    )(jnp.stack(plane.devices), *[array for term in terms for array in term[:2]], *extra)


def spread_kernel(q_width, width, kv_cols, sum_ref, qkv_ref, out_ref, *side_refs):
    qkv_ref[:, :q_width] = sum_ref[:, :q_width].astype(F32)
    at = q_width + width
    qkv_ref[:, q_width:] = sum_ref[:, at : at + kv_cols].astype(F32)
    out_ref[...] = sum_ref[:, q_width:at].astype(F32)
    sides = sum_ref[:16, at + kv_cols :].astype(F32)
    for row, side_ref in enumerate(side_refs):
        side_ref[...] = sides[row : row + 1, : side_ref.shape[1]]


def spread_sums(attn_sum, q_width, width, kv_cols, sizes):
    rows = attn_sum.shape[0]
    at = q_width + width
    if rows % 16:
        full = attn_sum.astype(F32)
        grad_qkv = jnp.concatenate([full[:, :q_width], full[:, at : at + kv_cols]], axis=1)
        sides = [full[row, at + kv_cols : at + kv_cols + size] for row, size in enumerate(sizes)]
        return grad_qkv, full[:, q_width:at].T, *sides
    grad_qkv, grad_out, *sides = pl.pallas_call(
        functools.partial(spread_kernel, q_width, width, kv_cols),
        out_shape=(
            jax.ShapeDtypeStruct((rows, q_width + kv_cols), F32),
            jax.ShapeDtypeStruct((rows, width), F32),
            *(jax.ShapeDtypeStruct((1, size), F32) for size in sizes),
        ),
        in_specs=vmem_specs(1),
        out_specs=tuple(vmem_specs(2 + len(sizes))),
        compiler_params=pltpu.CompilerParams(vmem_limit_bytes=VMEM_LIMIT),
        cost_estimate=SMALL,
    )(attn_sum)
    return grad_qkv, grad_out.T, *(side.reshape(-1) for side in sides)


def after(array, *others):
    return lax.optimization_barrier((array, *others))[0]


class Plane:
    def __init__(self):
        ctx, uly = lax.axis_size("ctx"), lax.axis_size("uly")
        self.count = ctx * uly
        assert self.count & (self.count - 1) == 0 and ctx % 2 == 0
        self.me = lax.axis_index("ctx") * uly + lax.axis_index("uly")
        self.core = uly
        near = [1 << i for i in range(uly.bit_length() - 1)]
        far = [self.core << i for i in range(1, (ctx // 2).bit_length())]
        self.orders = (far + near, near + far)
        self.steps = len(near) + len(far)
        mine = (self.me // self.core) % 2 == 0
        masks = [[0], [0]]
        for which in (0, 1):
            for bit in self.orders[which]:
                masks[which] += [bit | mask for mask in masks[which]]
        pairs = list(zip(masks[0], masks[1]))
        near_slots = [jnp.where(mine, a, b) for a, b in pairs]
        far_slots = [jnp.where(mine, b, a) | self.core for a, b in pairs]
        self.devices = [self.me ^ mask for mask in near_slots + far_slots]

    def swap(self, array, step):
        pairs = []
        for i in range(self.count):
            if step == self.steps:
                bit = self.core
            else:
                bit = self.orders[(i // self.core) % 2][step]
            pairs.append((i, i ^ bit))
        return lax.ppermute(array, PLANE, pairs)

    def widen(self, rows, step, *others):
        moved = self.swap(rows, step)
        return jnp.concatenate([after(rows, *others) if others else rows, moved], axis=0)

    def gather(self, rows, late_step=None, *others):
        stages = [rows]
        for step in range(self.steps):
            if step == late_step:
                stages[-1] = after(stages[-1], *others)
            stages.append(self.widen(stages[-1], step))
        return stages + [self.swap(stages[-1], self.steps)]

    def fold(self, near, far, step):
        return (near.astype(F32) + self.swap(far, step).astype(F32)).astype(BF16)

    def fold_rest(self, rows, step):
        half = rows.shape[0] // 2
        return self.fold(rows[:half], rows[half:], step)


def place_info(spans, row_in_span, length_row):
    places = spans * TOK_DEV + row_in_span
    begins = jnp.zeros_like(places)
    end = jnp.int32(0)
    for doc in range(length_row.shape[0]):
        end = end + length_row[doc]
        begins = jnp.where(places >= end, jnp.maximum(begins, end), begins)
    return places, begins


def inverse_rms(values):
    return lax.rsqrt(jnp.mean(values * values, axis=-1, keepdims=True) + NORM_EPS)


def norm_backward(values, inverse, scaled):
    return inverse * scaled - values * (
        inverse**3 * jnp.mean(scaled * values, axis=-1, keepdims=True)
    )


def turn(heads, cosine, sine):
    half = HEAD // 2
    first, second = heads[..., :half], heads[..., half:]
    return jnp.concatenate(
        [first * cosine - second * sine, second * cosine + first * sine], axis=-1
    )


def shards(
    layer_input,
    span_order,
    doc_lengths,
    pad_mask,
    w_qkv,
    b_qkv,
    w_out,
    norm_gain_attn,
    norm_gain_mlp,
    w_mlp,
    cotangent,
):
    tok_rows, width = layer_input.shape
    n_dp = lax.axis_size("dp")
    n_plane = lax.axis_size("ctx") * lax.axis_size("uly")
    n_all = n_dp * n_plane
    plane = Plane()
    ffn_width = w_mlp.shape[1] // 3
    local_rows = w_mlp.shape[0]
    zone = local_rows * n_plane
    q_width, kv_width = HEADS * HEAD, KV_HEADS * HEAD
    qkv_width = q_width + 2 * kv_width
    bias_rows = b_qkv.shape[0]
    slice_tiles = -(-(ffn_width // LANES) // n_plane)
    chunks = max(c for c in (1, 2, 3) if slice_tiles % c == 0)
    chunk_cols = slice_tiles // chunks * LANES
    kv_cols = 2 * kv_width + LANES

    def swap_rows(array):
        return lax.all_to_all(array, PLANE, split_axis=0, concat_axis=0, tiled=True)

    def zone_gather(array):
        return lax.all_gather(array, "dp", axis=0, tiled=True)

    def zone_sum(array):
        return lax.psum_scatter(array, "dp", scatter_dimension=0, tiled=True)

    def whole_rows(pieces):
        cols = pieces[0].shape[1]
        full = jnp.zeros((n_dp, n_plane, local_rows, cols), BF16)
        slots = [block for piece in pieces for block in jnp.split(piece, n_plane // 2)]
        for device, block in zip(plane.devices, slots):
            piece = block.reshape(n_dp, 1, local_rows, cols)
            full = lax.dynamic_update_slice(full, piece, (0, device, 0, 0))
        return full.reshape(n_all * local_rows, cols)

    def device_blocks(array):
        cols = array.shape[1]
        full = array.reshape(n_dp, n_plane, local_rows, cols)
        return [
            lax.dynamic_slice_in_dim(full, device, 1, 1).reshape(n_dp * local_rows, cols)
            for device in plane.devices
        ]

    side = jnp.concatenate(
        [
            norm_gain_attn[:, None],
            norm_gain_mlp[:, None],
            jnp.zeros((local_rows, 62), BF16),
            jnp.pad(b_qkv[None, :], ((0, local_rows - 1), (0, 64 - bias_rows))),
        ],
        axis=1,
    )
    my_dp = lax.axis_index("dp")

    def zone_rows(array):
        full = jnp.zeros((n_dp, *array.shape), BF16)
        for step in range(n_dp):
            moved = array
            if step:
                moved = lax.ppermute(array, "dp", [(i, (i + step) % n_dp) for i in range(n_dp)])
            full = lax.dynamic_update_slice(
                full, moved[None], ((my_dp + n_dp - step) % n_dp, 0, 0)
            )
        return full.reshape(n_dp * array.shape[0], array.shape[1])

    kv_local = jnp.concatenate([w_qkv[:, q_width:], side], axis=1)
    attn_local = jnp.concatenate([kv_local, w_qkv[:, :q_width], w_out.T], axis=1)
    attn_zone = zone_rows(attn_local)
    kv_zone = attn_zone[:, : kv_local.shape[1]]
    big_zone = attn_zone[:, kv_local.shape[1] :]

    packed = pack_slices(after(w_mlp, attn_local), n_plane, chunks, chunk_cols)
    chunk_width = 3 * chunk_cols
    mlp_zone = swap_rows(packed)
    mlp_weights = [
        zone_gather(mlp_zone[:, chunk * chunk_width : (chunk + 1) * chunk_width])
        for chunk in range(chunks)
    ]

    w_kv_stages = plane.gather(kv_zone, 1, mlp_zone)
    w_q_stages = plane.gather(after(big_zone[:, :q_width], w_kv_stages[1]))
    w_out_near = after(big_zone[:, q_width:], w_q_stages[-2])
    w_out_near = plane.widen(w_out_near, 0)

    order_row, length_row, mask_row = after(
        (span_order[0], doc_lengths[0], pad_mask[0]), packed
    )
    row_in_span = jnp.arange(tok_rows, dtype=jnp.int32)
    stored_block = jnp.stack(plane.devices)
    spans = order_row[stored_block]
    own_place, own_begin = place_info(spans[0], row_in_span, length_row)
    flags = mask_row.reshape(n_plane, tok_rows)[stored_block]
    key_place = spans[:, None] * TOK_DEV + row_in_span[None, :]
    kinfo = jnp.stack(
        [jnp.where(flags == 1, key_place, FAR).reshape(-1), key_place.reshape(-1)], axis=1
    )
    qinfo = jnp.concatenate(
        [
            own_place[None],
            own_begin[None],
            flags[0][None],
            jnp.zeros((5, tok_rows), jnp.int32),
        ],
        axis=0,
    )
    need = ((spans <= spans[0]) & ((spans + 1) * TOK_DEV > own_begin[0])).astype(jnp.int32)

    inner = (own_place - own_begin).astype(F32)
    half = HEAD // 2
    frequency = ROPE_BASE ** (-(jnp.arange(half, dtype=F32) * 2.0) / HEAD)
    angles_t = frequency[:, None] * inner[None, :]
    cos_t, sin_t = jnp.cos(angles_t), jnp.sin(angles_t)
    cos_r, sin_r = cos_t.T[:, None, :], sin_t.T[:, None, :]

    w_kv_all = whole_rows(w_kv_stages[-2:])
    side_all = w_kv_all[:, 2 * kv_width :].astype(F32)
    gain_attn = side_all[:, 0]
    gain_mlp = side_all[:, 1]
    bias_all = side_all.reshape(n_all, local_rows, LANES)[:, 0, 64 : 64 + bias_rows].reshape(-1)

    inputs = layer_input.astype(F32)
    in_inverse = inverse_rms(inputs)
    normed_in = (inputs * in_inverse * gain_attn).astype(BF16)

    kv_proj = dot(normed_in, w_kv_all[:, : 2 * kv_width], 1, 0) + bias_all[q_width:]
    key_own = turn(kv_proj[:, :kv_width].reshape(tok_rows, KV_HEADS, HEAD), cos_r, sin_r)
    kv_own = jnp.concatenate([key_own.reshape(tok_rows, kv_width), kv_proj[:, kv_width:]], axis=1)
    kv_own = after(kv_own.astype(BF16), w_q_stages[-2])
    kv_stages = plane.gather(kv_own, 1, w_out_near)
    kv_all = jnp.concatenate(kv_stages[-2:], axis=0)
    w_q_all = whole_rows(w_q_stages[-2:])

    q_proj = dot(w_q_all, normed_in, 0, 1) + bias_all[:q_width, None]
    q_heads = q_proj.reshape(HEADS, 2, half, tok_rows)
    q_first, q_second = q_heads[:, 0], q_heads[:, 1]
    query_t = (
        jnp.stack(
            [q_first * cos_t - q_second * sin_t, q_second * cos_t + q_first * sin_t], axis=1
        )
        .reshape(q_width, tok_rows)
        .astype(BF16)
    )
    cot_near = plane.widen(after(cotangent, kv_stages[-2]), 0)
    need = after(need, w_out_near, cot_near)
    attended_t, lse = attention_forward(need, kinfo, qinfo, query_t, kv_all)
    for step in range(1, plane.steps):
        w_out_near = plane.widen(after(w_out_near, kv_stages[-2]), step, attended_t)
    w_out_all = whole_rows([w_out_near, plane.swap(w_out_near, plane.steps)])
    for step in range(1, plane.steps):
        cot_near = plane.widen(cot_near, step, attended_t)
    attended_t = after(attended_t, cot_near)

    middle = inputs + dot(attended_t, w_out_all, 0, 1)
    mid_inverse = inverse_rms(middle)
    normed_mid = (middle * mid_inverse * gain_mlp).astype(BF16)

    mid_near = normed_mid
    for step in range(plane.steps):
        mid_near = plane.widen(mid_near, step)
    cot_halves = cot_near, plane.swap(cot_near, plane.steps)
    mid_near = after(mid_near, mlp_weights[0])
    mid_halves = mid_near, plane.swap(mid_near, plane.steps)
    sums, chunk_grads = (), []
    if chunks > 1:
        *sums, chunk_grads = split_at(
            feed_forward(mid_halves, cot_halves, mlp_weights[:-1], (), True), 4
        )
    *sums, (extra,) = split_at(
        feed_forward(mid_halves, cot_halves, mlp_weights[-1:], tuple(sums), False), 4
    )

    def token_blocks(array):
        return [array[k * tok_rows : (k + 1) * tok_rows] for k in range(n_plane)]

    chunk_sums = [zone_sum(grad) for grad in chunk_grads]
    mid_fold = plane.fold(sums[0], sums[1], plane.steps)
    chunk_grads.append(feed_forward_grad(mid_halves, cot_halves, after(extra, mid_fold)))
    chunk_sums.append(zone_sum(chunk_grads[-1]))
    for step in range(plane.steps - 1, -1, -1):
        half = mid_fold.shape[0] // 2
        kept, sent = mid_fold[:half], mid_fold[half:]
        if step == plane.steps - 1:
            kept = after(kept, chunk_grads[-1])
        mid_fold = plane.fold(kept, sent, step)
        if step == 0:
            out_fold = plane.fold(after(sums[2], kept), sums[3], plane.steps)
    mid_grad = after(mid_fold, *chunk_sums[:-1][:1]).astype(F32)

    out_grad = cotangent.astype(F32)
    gain_mlp_grad = jnp.sum(mid_grad * (middle * mid_inverse), axis=0)
    middle_grad = out_grad + norm_backward(middle, mid_inverse, mid_grad * gain_mlp)
    middle_low = middle_grad.astype(BF16)
    attended_grad_t = dot(w_out_all, middle_low, 0, 1).astype(BF16)
    attended_grad_t = after(attended_grad_t, out_fold)
    query_grad, *kv_grads = attention_backward(
        need, kinfo, qinfo, cos_t, sin_t, query_t, kv_all, attended_t, attended_grad_t, lse
    )
    kv_fold = plane.fold(*kv_grads, plane.steps)
    first_swapped = [swap_rows(after(array, mid_fold)) for array in chunk_sums[:-1][:1]]
    mlp_out = after(out_fold, mid_fold)
    for step in range(plane.steps - 1, 0, -1):
        mlp_out = plane.fold_rest(mlp_out, step)
    big_grads = weight_grads(
        plane,
        local_rows,
        [
            (after(normed_in, mlp_out, kv_fold, *first_swapped), query_grad, False),
            (middle_low, attended_t, True),
        ],
    )
    big_fold = plane.fold(*big_grads, plane.steps)
    mlp_out = plane.fold_rest(after(mlp_out, kv_fold), 0)
    for step in range(plane.steps - 1, -1, -1):
        rows = kv_fold.shape[0] // 2
        kept, sent = kv_fold[:rows], kv_fold[rows:]
        if step == plane.steps - 1:
            kept = after(kept, big_fold, *chunk_sums[1:-1])
        kv_fold = plane.fold(kept, sent, step)
    kv_back = after(kv_fold, mlp_out)
    kv_back = kv_back.astype(F32)
    key_back = turn(kv_back[:, :kv_width].reshape(tok_rows, KV_HEADS, HEAD), cos_r, -sin_r)
    projected_grad = jnp.concatenate(
        [query_grad, key_back.reshape(tok_rows, kv_width).astype(BF16), kv_back[:, kv_width:].astype(BF16)],
        axis=1,
    )
    in_grad = dot(projected_grad[:, :q_width], w_q_all, 1, 1) + dot(
        projected_grad[:, q_width:], w_kv_all[:, : 2 * kv_width], 1, 1
    )
    gain_attn_grad = jnp.sum(in_grad * (inputs * in_inverse), axis=0)
    input_grad = middle_grad + norm_backward(inputs, in_inverse, in_grad * gain_attn)
    qkv_bias_grad = jnp.sum(projected_grad.astype(F32), axis=0)

    def side_rows(array):
        array = array.reshape(n_dp, n_plane, 1, -1)
        return jnp.pad(array, ((0, 0), (0, 0), (0, 0), (0, LANES - array.shape[-1])))

    side_grad = jnp.concatenate(
        [side_rows(gain_attn_grad), side_rows(gain_mlp_grad), side_rows(qkv_bias_grad)]
        + [jnp.zeros((n_dp, n_plane, 1, LANES), F32)] * 5,
        axis=2,
    )
    side_grad = jnp.pad(side_grad, ((0, 0), (0, 0), (0, local_rows - 8), (0, 0)))
    side_grad = side_grad.reshape(n_all * local_rows, LANES).astype(BF16)
    for step in range(plane.steps - 1, 0, -1):
        big_fold = plane.fold_rest(big_fold, step)
    small_grads = weight_grads(
        plane,
        local_rows,
        [(after(normed_in, big_fold), projected_grad[:, q_width:], False)],
        side_grad,
    )
    big_fold = plane.fold_rest(big_fold, 0)
    small_fold = plane.fold(*small_grads, plane.steps)
    for step in range(plane.steps - 1, -1, -1):
        rows = small_fold.shape[0] // 2
        kept, sent = small_fold[:rows], small_fold[rows:]
        if step == 0:
            kept = after(kept, chunk_sums[-1])
        small_fold = plane.fold(kept, sent, step)
    attn_plane = jnp.concatenate([big_fold, small_fold], axis=1)
    grad_qkv, grad_out, grad_gain_attn, grad_gain_mlp, grad_bias = spread_sums(
        zone_sum(attn_plane), q_width, width, 2 * kv_width, (local_rows, local_rows, bias_rows)
    )

    late_sums = jnp.concatenate(chunk_sums[len(first_swapped) :], axis=1)
    swapped = first_swapped + [swap_rows(after(late_sums, attn_plane))]
    grad_mlp = unpack_slices(swapped, local_rows, ffn_width, n_plane, chunks, chunk_cols)
    block_output = (middle + mlp_out.astype(F32)).astype(BF16)
    return (
        block_output,
        input_grad,
        grad_qkv,
        grad_bias,
        grad_out,
        grad_gain_attn,
        grad_gain_mlp,
        grad_mlp,
    )


def solution(mesh):
    rows = P(EVERY, None)
    flat = P(EVERY)
    columns = P(None, EVERY)
    batch = P("dp", None)
    return jax.shard_map(
        shards,
        mesh=mesh,
        in_specs=(rows, batch, batch, batch, rows, flat, columns, flat, flat, rows, rows),
        out_specs=(rows, rows, rows, flat, columns, flat, flat, rows),
        check_vma=False,
    )
```

```python
import functools

import jax
import jax.numpy as jnp
from jax import lax
from jax.experimental import pallas as pl
from jax.experimental.pallas import tpu as pltpu
from jax.sharding import PartitionSpec as P

HEADS = 12
KV_HEADS = 2
HEAD = 128
TOK_DEV = 256
LANES = 128
GROUP = HEADS // KV_HEADS

NORM_EPS = 1e-06
ROPE_BASE = 1000000.0
NEG_FILL = -1e30
LOG2E = 1.4426950408889634
SCALE = HEAD ** (-0.5)
FAR = 1 << 30
PLANE = ("ctx", "uly")
EVERY = ("dp", "ctx", "uly")
VMEM_LIMIT = 56 * 1024 * 1024
SMALL = pl.CostEstimate(flops=1024, bytes_accessed=1024, transcendentals=0)
F32 = jnp.float32
BF16 = jnp.bfloat16


def dot(left, right, left_dim, right_dim):
    return lax.dot_general(
        left, right, (((left_dim,), (right_dim,)), ((), ())), preferred_element_type=F32
    )


def block_bias(kinfo_ref, qinfo_ref, rows):
    info = kinfo_ref[rows, :]
    usable, place = info[:, 0:1], info[:, 1:2]
    q_place, q_begin = qinfo_ref[0:1, :], qinfo_ref[1:2, :]
    allowed = ((usable <= q_place) & (usable >= q_begin)) | (place == q_place)
    return jnp.where(allowed, 0.0, NEG_FILL)


def beside(array_ref, wide_ref):
    cols = array_ref.shape[1]
    for head in range(HEADS):
        group, place = divmod(head, GROUP)
        wide_ref[group * HEAD : (group + 1) * HEAD, place * cols : (place + 1) * cols] = array_ref[
            head * HEAD : (head + 1) * HEAD, :
        ]


def attn_fwd_kernel(
    need_ref, kinfo_ref, qinfo_ref, q_ref, kv_ref, o_ref, lse_ref, m_ref, l_ref, acc_ref, wide_ref
):
    blocks = kv_ref.shape[0] // TOK_DEV
    cols = q_ref.shape[1]
    beside(q_ref, wide_ref)
    m_ref[...] = jnp.full(m_ref.shape, NEG_FILL, F32)
    l_ref[...] = jnp.zeros(l_ref.shape, F32)
    acc_ref[...] = jnp.zeros(acc_ref.shape, F32)

    def one_block(block, carry):
        @pl.when(need_ref[block] > 0)
        def _():
            rows = pl.ds(pl.multiple_of(block * TOK_DEV, TOK_DEV), TOK_DEV)
            bias = jnp.concatenate([block_bias(kinfo_ref, qinfo_ref, rows)] * GROUP, axis=1)
            for group in range(KV_HEADS):
                key = kv_ref[rows, group * HEAD : (group + 1) * HEAD]
                value = kv_ref[rows, (KV_HEADS + group) * HEAD : (KV_HEADS + group + 1) * HEAD]
                span = slice(group * HEAD, (group + 1) * HEAD)
                row = slice(group, group + 1)
                scores = dot(key, wide_ref[span, :], 1, 0) * (SCALE * LOG2E) + bias
                old = m_ref[row, :]
                new = jnp.maximum(old, jnp.max(scores, axis=0, keepdims=True))
                weights = jnp.exp2(scores - new)
                factor = jnp.exp2(old - new)
                m_ref[row, :] = new
                l_ref[row, :] = l_ref[row, :] * factor + jnp.sum(weights, axis=0, keepdims=True)
                acc_ref[span, :] = acc_ref[span, :] * factor + dot(
                    value.T, weights.astype(BF16), 1, 0
                )

        return carry

    lax.fori_loop(0, blocks, one_block, 0)
    real = qinfo_ref[2:3, :].astype(F32)
    lse_ref[...] = jnp.zeros(lse_ref.shape, F32)
    lse_ref[:KV_HEADS, :] = m_ref[:KV_HEADS, :] + jnp.log(l_ref[:KV_HEADS, :]) * LOG2E
    for head in range(HEADS):
        group, place = divmod(head, GROUP)
        there = slice(place * cols, (place + 1) * cols)
        total = l_ref[group : group + 1, there]
        o_ref[head * HEAD : (head + 1) * HEAD, :] = (
            acc_ref[group * HEAD : (group + 1) * HEAD, there] * (real / total)
        ).astype(BF16)


def attn_bwd_kernel(
    need_ref,
    kinfo_ref,
    qinfo_ref,
    cos_ref,
    sin_ref,
    q_ref,
    kv_ref,
    o_ref,
    do_ref,
    lse_ref,
    dq_ref,
    near_ref,
    far_ref,
    dots_ref,
    acc_ref,
    wide_ref,
    low_ref,
):
    blocks = kv_ref.shape[0] // TOK_DEV
    cols = q_ref.shape[1]
    real = qinfo_ref[2:3, :].astype(F32)
    beside(q_ref, wide_ref)
    for head in range(HEADS):
        group, place = divmod(head, GROUP)
        there = slice(place * cols, (place + 1) * cols)
        span = slice(head * HEAD, (head + 1) * HEAD)
        grad = do_ref[span, :].astype(F32) * real
        low_ref[group * HEAD : (group + 1) * HEAD, there] = grad.astype(BF16)
        dots_ref[group : group + 1, there] = jnp.sum(
            grad * o_ref[span, :].astype(F32), axis=0, keepdims=True
        )
    acc_ref[...] = jnp.zeros(acc_ref.shape, F32)

    def one_block(dkv_ref, first, at, carry):
        block = first + at
        rows = pl.ds(pl.multiple_of(block * TOK_DEV, TOK_DEV), TOK_DEV)
        out_rows = pl.ds(pl.multiple_of(at * TOK_DEV, TOK_DEV), TOK_DEV)

        @pl.when(need_ref[block] == 0)
        def _():
            dkv_ref[out_rows, :] = jnp.zeros((TOK_DEV, 2 * KV_HEADS * HEAD), BF16)

        @pl.when(need_ref[block] > 0)
        def _():
            bias = jnp.concatenate([block_bias(kinfo_ref, qinfo_ref, rows)] * GROUP, axis=1)
            for group in range(KV_HEADS):
                key_cols = slice(group * HEAD, (group + 1) * HEAD)
                value_cols = slice((KV_HEADS + group) * HEAD, (KV_HEADS + group + 1) * HEAD)
                key = kv_ref[rows, key_cols]
                value = kv_ref[rows, value_cols]
                query, grad = wide_ref[key_cols, :], low_ref[key_cols, :]
                row = slice(group, group + 1)
                scores = dot(key, query, 1, 0) * (SCALE * LOG2E) + bias
                probs = jnp.exp2(scores - lse_ref[row, :])
                prob_grad = dot(value, grad, 1, 0)
                score_grad = (probs * (prob_grad - dots_ref[row, :])).astype(BF16)
                acc_ref[key_cols, :] += dot(key.T, score_grad, 1, 0)
                dkv_ref[out_rows, key_cols] = (dot(score_grad, query, 1, 1) * SCALE).astype(BF16)
                dkv_ref[out_rows, value_cols] = dot(probs.astype(BF16), grad, 1, 1).astype(BF16)

        return carry

    half_blocks = blocks // 2
    lax.fori_loop(0, half_blocks, functools.partial(one_block, near_ref, 0), 0)
    lax.fori_loop(0, half_blocks, functools.partial(one_block, far_ref, half_blocks), 0)
    cosine, sine = cos_ref[...], sin_ref[...]
    half = HEAD // 2
    for head in range(HEADS):
        group, place = divmod(head, GROUP)
        there = slice(place * cols, (place + 1) * cols)
        whole = acc_ref[group * HEAD : (group + 1) * HEAD, there] * SCALE
        whole = whole.astype(BF16).astype(F32)
        first, second = whole[:half], whole[half:]
        turned = jnp.concatenate(
            [first * cosine + second * sine, second * cosine - first * sine], axis=0
        )
        dq_ref[:, head * HEAD : (head + 1) * HEAD] = turned.T.astype(BF16)


def vmem_specs(count):
    return [pl.BlockSpec(memory_space=pltpu.VMEM)] * count


def attention_forward(need, kinfo, qinfo, query_t, kv_all):
    rows = query_t.shape[1]
    return pl.pallas_call(
        attn_fwd_kernel,
        out_shape=(
            jax.ShapeDtypeStruct((HEADS * HEAD, rows), BF16),
            jax.ShapeDtypeStruct((8, GROUP * rows), F32),
        ),
        in_specs=[pl.BlockSpec(memory_space=pltpu.SMEM)] + vmem_specs(4),
        out_specs=tuple(vmem_specs(2)),
        scratch_shapes=[
            pltpu.VMEM((8, GROUP * rows), F32),
            pltpu.VMEM((8, GROUP * rows), F32),
            pltpu.VMEM((KV_HEADS * HEAD, GROUP * rows), F32),
            pltpu.VMEM((KV_HEADS * HEAD, GROUP * rows), BF16),
        ],
        compiler_params=pltpu.CompilerParams(vmem_limit_bytes=VMEM_LIMIT),
        cost_estimate=SMALL,
    )(need, kinfo, qinfo, query_t, kv_all)


def attention_backward(need, kinfo, qinfo, cos_t, sin_t, query_t, kv_all, out_t, grad_t, lse):
    rows = query_t.shape[1]
    return pl.pallas_call(
        attn_bwd_kernel,
        out_shape=(
            jax.ShapeDtypeStruct((rows, HEADS * HEAD), BF16),
            jax.ShapeDtypeStruct((kv_all.shape[0] // 2, kv_all.shape[1]), BF16),
            jax.ShapeDtypeStruct((kv_all.shape[0] // 2, kv_all.shape[1]), BF16),
        ),
        in_specs=[pl.BlockSpec(memory_space=pltpu.SMEM)] + vmem_specs(9),
        out_specs=tuple(vmem_specs(3)),
        scratch_shapes=[
            pltpu.VMEM((8, GROUP * rows), F32),
            pltpu.VMEM((KV_HEADS * HEAD, GROUP * rows), F32),
            pltpu.VMEM((KV_HEADS * HEAD, GROUP * rows), BF16),
            pltpu.VMEM((KV_HEADS * HEAD, GROUP * rows), BF16),
        ],
        compiler_params=pltpu.CompilerParams(vmem_limit_bytes=VMEM_LIMIT),
        cost_estimate=SMALL,
    )(need, kinfo, qinfo, cos_t, sin_t, query_t, kv_all, out_t, grad_t, lse)


def ffn_tile(cols, mid_ref, cot_ref, w_refs, sums, outs, act_refs, acc_refs):
    mid_grad = out = None
    if sums:
        mid_grad, out = sums[0][...].astype(F32), sums[1][...].astype(F32)
    for w_ref, act_ref in zip(w_refs, act_refs):
        both = dot(mid_ref[...], w_ref[:, : 2 * cols], 1, 0)
        hidden_grad = dot(cot_ref[...], w_ref[:, 2 * cols :], 1, 0)
        gate, up = both[:, :cols], both[:, cols:]
        share = 1.0 / (1.0 + jnp.exp(-gate))
        acted = gate * share
        act_ref[:, :cols] = (
            hidden_grad * up * (share * (1.0 + gate * (1.0 - share)))
        ).astype(BF16)
        act_ref[:, cols : 2 * cols] = (hidden_grad * acted).astype(BF16)
        act_ref[:, 2 * cols :] = (acted * up).astype(BF16)
        mid_term = dot(act_ref[:, : 2 * cols], w_ref[:, : 2 * cols], 1, 1)
        out_term = dot(act_ref[:, 2 * cols :], w_ref[:, 2 * cols :], 1, 1)
        mid_grad = mid_term if mid_grad is None else mid_grad + mid_term
        out = out_term if out is None else out + out_term
    outs[0][...] = mid_grad.astype(BF16)
    outs[1][...] = out.astype(BF16)
    for act_ref, acc_ref in zip(act_refs, acc_refs):
        acc_ref[:, : 2 * cols] += dot(mid_ref[...], act_ref[:, : 2 * cols], 0, 0)
        acc_ref[:, 2 * cols :] += dot(cot_ref[...], act_ref[:, 2 * cols :], 0, 0)


def ffn_kernel(cols, count, first, with_grad, *refs):
    mids, cots, w_refs, refs = refs[:2], refs[2:4], refs[4 : 4 + count], refs[4 + count :]
    mid_sums = out_sums = None
    if not first:
        mid_sums, out_sums, refs = refs[:2], refs[2:4], refs[4:]
    mid_outs, out_outs, refs = refs[:2], refs[2:4], refs[4:]
    if with_grad:
        grad_refs, act_refs, acc_refs = refs[:count], refs[count : 2 * count], refs[2 * count :]
    else:
        grad_refs, act_refs, acc_refs = (), refs, ()
    step, last = pl.program_id(0), pl.num_programs(0) - 1
    near = step < pl.num_programs(0) // 2

    @pl.when(step == 0)
    def _():
        for acc_ref in acc_refs:
            acc_ref[...] = jnp.zeros(acc_ref.shape, F32)

    def tile(which):
        sums = () if first else (mid_sums[which], out_sums[which])
        outs = (mid_outs[which], out_outs[which])
        ffn_tile(cols, mids[which], cots[which], w_refs, sums, outs, act_refs, acc_refs)

    pl.when(near)(lambda: tile(0))
    pl.when(jnp.logical_not(near))(lambda: tile(1))

    @pl.when(step == last)
    def _():
        for grad_ref, acc_ref in zip(grad_refs, acc_refs):
            grad_ref[...] = acc_ref[...].astype(BF16)


def feed_forward(mid_halves, cot_halves, weights, sums, with_grad):
    half_tokens, width = mid_halves[0].shape
    count, shape = len(weights), weights[0].shape
    cols = shape[1] // 3
    half = half_tokens // TOK_DEV
    near_spec = pl.BlockSpec((TOK_DEV, width), lambda i: (jnp.minimum(i, half - 1), 0))
    far_spec = pl.BlockSpec((TOK_DEV, width), lambda i: (jnp.maximum(i - half, 0), 0))
    act_spec = pl.BlockSpec((TOK_DEV, 3 * cols), lambda i: (i, 0))
    once = pl.BlockSpec(shape, lambda i: (0, 0), pipeline_mode=pl.Buffered(1))
    row_shape = jax.ShapeDtypeStruct((half_tokens, width), BF16)
    if with_grad:
        last_shape, last_spec = jax.ShapeDtypeStruct(shape, BF16), once
        scratch = [pltpu.VMEM((TOK_DEV, 3 * cols), BF16)] * count
        scratch += [pltpu.VMEM(shape, F32)] * count
    else:
        last_shape, last_spec = jax.ShapeDtypeStruct((2 * half_tokens, 3 * cols), BF16), act_spec
        scratch = []
    return pl.pallas_call(
        functools.partial(ffn_kernel, cols, count, not sums, with_grad),
        grid=(2 * half,),
        out_shape=(row_shape,) * 4 + (last_shape,) * count,
        in_specs=[near_spec, far_spec] * 2
        + [once] * count
        + [near_spec, far_spec] * (len(sums) // 2),
        out_specs=(near_spec, far_spec) * 2 + (last_spec,) * count,
        scratch_shapes=scratch,
        compiler_params=pltpu.CompilerParams(vmem_limit_bytes=VMEM_LIMIT),
        cost_estimate=SMALL,
    )(*mid_halves, *cot_halves, *weights, *sums)


def ffn_grad_kernel(cols, mid_near, mid_far, cot_near, cot_far, act_ref, grad_ref):
    half = mid_near.shape[0]
    for near, far, part in (
        (mid_near, mid_far, slice(0, 2 * cols)),
        (cot_near, cot_far, slice(2 * cols, 3 * cols)),
    ):
        grad_ref[:, part] = (
            dot(near[...], act_ref[:half, part], 0, 0) + dot(far[...], act_ref[half:, part], 0, 0)
        ).astype(BF16)


def split_at(arrays, count):
    return *arrays[:count], list(arrays[count:])


def feed_forward_grad(mid_halves, cot_halves, act):
    half_tokens, width = mid_halves[0].shape
    cols = act.shape[1] // 3
    tile = 512 if width % 512 == 0 else width
    col_spec = pl.BlockSpec((half_tokens, tile), lambda i: (0, i))
    return pl.pallas_call(
        functools.partial(ffn_grad_kernel, cols),
        grid=(width // tile,),
        out_shape=jax.ShapeDtypeStruct((width, 3 * cols), BF16),
        in_specs=[col_spec] * 4
        + [pl.BlockSpec(act.shape, lambda i: (0, 0), pipeline_mode=pl.Buffered(1))],
        out_specs=pl.BlockSpec((tile, 3 * cols), lambda i: (i, 0)),
        compiler_params=pltpu.CompilerParams(vmem_limit_bytes=VMEM_LIMIT),
        cost_estimate=SMALL,
    )(*mid_halves, *cot_halves, act)


def slice_moves(n_plane, chunks, cols, total):
    for device in range(n_plane):
        for chunk in range(chunks):
            start = (device * chunks + chunk) * cols
            for kind in range(3):
                yield device, chunk, kind, kind * total + start, max(0, min(cols, total - start))


def pack_kernel(moves, cols, w_ref, out_ref):
    rows = w_ref.shape[0]
    for device, chunk, kind, source, real in moves:
        there = slice(device * rows, (device + 1) * rows)
        at = (chunk * 3 + kind) * cols
        if real:
            out_ref[there, at : at + real] = w_ref[:, source : source + real]
        if real < cols:
            out_ref[there, at + real : at + cols] = jnp.zeros((rows, cols - real), BF16)


def unpack_kernel(moves, cols, total, *refs):
    in_refs, out_ref = refs[:-1], refs[-1]
    rows = out_ref.shape[0]

    def one_kind(kind_now):
        for device, chunk, kind, source, real in moves:
            if real and kind == kind_now:
                which = min(chunk, len(in_refs) - 1)
                at = ((chunk - which) * 3 + kind) * cols
                block = in_refs[which][device * rows : (device + 1) * rows, at : at + real]
                start = source - kind * total
                out_ref[:, start : start + real] = block.astype(F32)

    for kind in range(3):
        pl.when(pl.program_id(0) == kind)(functools.partial(one_kind, kind))


def pack_slices(w_mlp, n_plane, chunks, cols):
    rows, total = w_mlp.shape[0], w_mlp.shape[1] // 3
    if rows % 16:
        wide = jnp.pad(
            w_mlp.reshape(rows, 3, total), ((0, 0), (0, 0), (0, n_plane * chunks * cols - total))
        )
        wide = wide.reshape(rows, 3, n_plane, chunks, cols).transpose(2, 0, 3, 1, 4)
        return wide.reshape(n_plane * rows, 3 * chunks * cols)
    moves = list(slice_moves(n_plane, chunks, cols, total))
    return pl.pallas_call(
        functools.partial(pack_kernel, moves, cols),
        out_shape=jax.ShapeDtypeStruct((n_plane * rows, 3 * chunks * cols), BF16),
        in_specs=vmem_specs(1),
        out_specs=vmem_specs(1)[0],
        compiler_params=pltpu.CompilerParams(vmem_limit_bytes=VMEM_LIMIT),
        cost_estimate=SMALL,
    )(w_mlp)


def unpack_slices(arrays, rows, total, n_plane, chunks, cols):
    if rows % 16:
        wide = jnp.concatenate(arrays, axis=1).reshape(n_plane, rows, chunks, 3, cols)
        wide = wide.transpose(1, 3, 0, 2, 4).reshape(rows, 3, -1)[:, :, :total]
        return wide.reshape(rows, 3 * total).astype(F32)
    moves = list(slice_moves(n_plane, chunks, cols, total))
    return pl.pallas_call(
        functools.partial(unpack_kernel, moves, cols, total),
        grid=(3,),
        out_shape=jax.ShapeDtypeStruct((rows, 3 * total), F32),
        in_specs=[
            pl.BlockSpec(array.shape, lambda i: (0, 0), pipeline_mode=pl.Buffered(1))
            for array in arrays
        ],
        out_specs=pl.BlockSpec((rows, total), lambda i: (0, i)),
        compiler_params=pltpu.CompilerParams(vmem_limit_bytes=VMEM_LIMIT),
        cost_estimate=SMALL,
    )(*arrays)


def weight_grad_kernel(n_dp, local_rows, across, dev_ref, *refs):
    count = len(across)
    lefts, rights = refs[: 2 * count : 2], refs[1 : 2 * count : 2]
    sides, (near_ref, far_ref, turned_ref, block_ref) = refs[2 * count : -4], refs[-4:]
    half = near_ref.shape[0] // (n_dp * local_rows)
    tile = block_ref.shape[1]

    def move(from_ref, at):
        cols = slice(at, at + from_ref.shape[1])
        for slot in range(2 * half):
            out_ref = near_ref if slot < half else far_ref
            for zone in range(n_dp):
                source = (zone * 2 * half + dev_ref[slot]) * local_rows
                source = pl.ds(pl.multiple_of(source, local_rows), local_rows)
                there = ((slot % half) * n_dp + zone) * local_rows
                out_ref[there : there + local_rows, cols] = from_ref[source, :]

    at = 0
    for left, right, is_across in zip(lefts, rights, across):
        turned_ref[...] = left[...].T
        cols = right.shape[0] if is_across else right.shape[1]
        for start in range(0, cols, tile):
            span = slice(start, start + tile)
            if is_across:
                block = dot(turned_ref[...], right[span, :], 1, 1)
            else:
                block = dot(turned_ref[...], right[:, span], 1, 0)
            block_ref[...] = block.astype(BF16)
            move(block_ref, at)
            at += tile
    for side_ref in sides:
        move(side_ref, at)


def weight_grads(plane, local_rows, terms, side=None):
    n_dp = lax.axis_size("dp")
    tokens, width = terms[0][0].shape
    widths = [right.shape[0 if across else 1] for _, right, across in terms]
    if local_rows % 16:
        full = jnp.concatenate(
            [dot(left, right, 0, 1 if across else 0) for left, right, across in terms], axis=1
        ).astype(BF16)
        if side is not None:
            full = jnp.concatenate([full, side], axis=1)
        full = full.reshape(n_dp, plane.count, local_rows, full.shape[1])
        blocks = [
            lax.dynamic_slice_in_dim(full, device, 1, 1).reshape(n_dp * local_rows, -1)
            for device in plane.devices
        ]
        half = plane.count // 2
        return jnp.concatenate(blocks[:half]), jnp.concatenate(blocks[half:])
    tile = 512
    extra = [] if side is None else [side]
    total = sum(widths) + sum(array.shape[1] for array in extra)
    shape = jax.ShapeDtypeStruct((width // 2, total), BF16)
    return pl.pallas_call(
        functools.partial(weight_grad_kernel, n_dp, local_rows, [term[2] for term in terms]),
        out_shape=(shape, shape),
        in_specs=[pl.BlockSpec(memory_space=pltpu.SMEM)]
        + vmem_specs(2 * len(terms) + len(extra)),
        out_specs=tuple(vmem_specs(2)),
        scratch_shapes=[pltpu.VMEM((width, tokens), BF16), pltpu.VMEM((width, tile), BF16)],
        compiler_params=pltpu.CompilerParams(vmem_limit_bytes=VMEM_LIMIT),
        cost_estimate=SMALL,
    )(jnp.stack(plane.devices), *[array for term in terms for array in term[:2]], *extra)


def spread_kernel(q_width, width, kv_cols, sum_ref, qkv_ref, out_ref, *side_refs):
    qkv_ref[:, :q_width] = sum_ref[:, :q_width].astype(F32)
    at = q_width + width
    qkv_ref[:, q_width:] = sum_ref[:, at : at + kv_cols].astype(F32)
    out_ref[...] = sum_ref[:, q_width:at].astype(F32)
    sides = sum_ref[:16, at + kv_cols :].astype(F32)
    for row, side_ref in enumerate(side_refs):
        side_ref[...] = sides[row : row + 1, : side_ref.shape[1]]


def spread_sums(attn_sum, q_width, width, kv_cols, sizes):
    rows = attn_sum.shape[0]
    at = q_width + width
    if rows % 16:
        full = attn_sum.astype(F32)
        grad_qkv = jnp.concatenate([full[:, :q_width], full[:, at : at + kv_cols]], axis=1)
        sides = [full[row, at + kv_cols : at + kv_cols + size] for row, size in enumerate(sizes)]
        return grad_qkv, full[:, q_width:at].T, *sides
    grad_qkv, grad_out, *sides = pl.pallas_call(
        functools.partial(spread_kernel, q_width, width, kv_cols),
        out_shape=(
            jax.ShapeDtypeStruct((rows, q_width + kv_cols), F32),
            jax.ShapeDtypeStruct((rows, width), F32),
            *(jax.ShapeDtypeStruct((1, size), F32) for size in sizes),
        ),
        in_specs=vmem_specs(1),
        out_specs=tuple(vmem_specs(2 + len(sizes))),
        compiler_params=pltpu.CompilerParams(vmem_limit_bytes=VMEM_LIMIT),
        cost_estimate=SMALL,
    )(attn_sum)
    return grad_qkv, grad_out.T, *(side.reshape(-1) for side in sides)


def after(array, *others):
    return lax.optimization_barrier((array, *others))[0]


class Plane:
    def __init__(self):
        ctx, uly = lax.axis_size("ctx"), lax.axis_size("uly")
        self.count = ctx * uly
        assert self.count & (self.count - 1) == 0 and ctx % 2 == 0
        self.me = lax.axis_index("ctx") * uly + lax.axis_index("uly")
        self.core = uly
        near = [1 << i for i in range(uly.bit_length() - 1)]
        far = [self.core << i for i in range(1, (ctx // 2).bit_length())]
        self.orders = (far + near, near + far)
        self.steps = len(near) + len(far)
        mine = (self.me // self.core) % 2 == 0
        masks = [[0], [0]]
        for which in (0, 1):
            for bit in self.orders[which]:
                masks[which] += [bit | mask for mask in masks[which]]
        pairs = list(zip(masks[0], masks[1]))
        near_slots = [jnp.where(mine, a, b) for a, b in pairs]
        far_slots = [jnp.where(mine, b, a) | self.core for a, b in pairs]
        self.devices = [self.me ^ mask for mask in near_slots + far_slots]

    def swap(self, array, step):
        pairs = []
        for i in range(self.count):
            if step == self.steps:
                bit = self.core
            else:
                bit = self.orders[(i // self.core) % 2][step]
            pairs.append((i, i ^ bit))
        return lax.ppermute(array, PLANE, pairs)

    def widen(self, rows, step, *others):
        moved = self.swap(rows, step)
        return jnp.concatenate([after(rows, *others) if others else rows, moved], axis=0)

    def gather(self, rows, late_step=None, *others):
        stages = [rows]
        for step in range(self.steps):
            if step == late_step:
                stages[-1] = after(stages[-1], *others)
            stages.append(self.widen(stages[-1], step))
        return stages + [self.swap(stages[-1], self.steps)]

    def fold(self, near, far, step):
        return (near.astype(F32) + self.swap(far, step).astype(F32)).astype(BF16)

    def fold_rest(self, rows, step):
        half = rows.shape[0] // 2
        return self.fold(rows[:half], rows[half:], step)


def place_info(spans, row_in_span, length_row):
    places = spans * TOK_DEV + row_in_span
    begins = jnp.zeros_like(places)
    end = jnp.int32(0)
    for doc in range(length_row.shape[0]):
        end = end + length_row[doc]
        begins = jnp.where(places >= end, jnp.maximum(begins, end), begins)
    return places, begins


def inverse_rms(values):
    return lax.rsqrt(jnp.mean(values * values, axis=-1, keepdims=True) + NORM_EPS)


def norm_backward(values, inverse, scaled):
    return inverse * scaled - values * (
        inverse**3 * jnp.mean(scaled * values, axis=-1, keepdims=True)
    )


def turn(heads, cosine, sine):
    half = HEAD // 2
    first, second = heads[..., :half], heads[..., half:]
    return jnp.concatenate(
        [first * cosine - second * sine, second * cosine + first * sine], axis=-1
    )


def shards(
    layer_input,
    span_order,
    doc_lengths,
    pad_mask,
    w_qkv,
    b_qkv,
    w_out,
    norm_gain_attn,
    norm_gain_mlp,
    w_mlp,
    cotangent,
):
    tok_rows, width = layer_input.shape
    n_dp = lax.axis_size("dp")
    n_plane = lax.axis_size("ctx") * lax.axis_size("uly")
    n_all = n_dp * n_plane
    plane = Plane()
    ffn_width = w_mlp.shape[1] // 3
    local_rows = w_mlp.shape[0]
    zone = local_rows * n_plane
    q_width, kv_width = HEADS * HEAD, KV_HEADS * HEAD
    qkv_width = q_width + 2 * kv_width
    bias_rows = b_qkv.shape[0]
    slice_tiles = -(-(ffn_width // LANES) // n_plane)
    chunks = max(c for c in (1, 2, 3) if slice_tiles % c == 0)
    chunk_cols = slice_tiles // chunks * LANES
    kv_cols = 2 * kv_width + LANES

    def swap_rows(array):
        return lax.all_to_all(array, PLANE, split_axis=0, concat_axis=0, tiled=True)

    def zone_gather(array):
        return lax.all_gather(array, "dp", axis=0, tiled=True)

    def zone_sum(array):
        return lax.psum_scatter(array, "dp", scatter_dimension=0, tiled=True)

    def whole_rows(pieces):
        cols = pieces[0].shape[1]
        full = jnp.zeros((n_dp, n_plane, local_rows, cols), BF16)
        slots = [block for piece in pieces for block in jnp.split(piece, n_plane // 2)]
        for device, block in zip(plane.devices, slots):
            piece = block.reshape(n_dp, 1, local_rows, cols)
            full = lax.dynamic_update_slice(full, piece, (0, device, 0, 0))
        return full.reshape(n_all * local_rows, cols)

    def device_blocks(array):
        cols = array.shape[1]
        full = array.reshape(n_dp, n_plane, local_rows, cols)
        return [
            lax.dynamic_slice_in_dim(full, device, 1, 1).reshape(n_dp * local_rows, cols)
            for device in plane.devices
        ]

    side = jnp.concatenate(
        [
            norm_gain_attn[:, None],
            norm_gain_mlp[:, None],
            jnp.zeros((local_rows, 62), BF16),
            jnp.pad(b_qkv[None, :], ((0, local_rows - 1), (0, 64 - bias_rows))),
        ],
        axis=1,
    )
    my_dp = lax.axis_index("dp")

    def zone_rows(array):
        full = jnp.zeros((n_dp, *array.shape), BF16)
        for step in range(n_dp):
            moved = array
            if step:
                moved = lax.ppermute(array, "dp", [(i, (i + step) % n_dp) for i in range(n_dp)])
            full = lax.dynamic_update_slice(
                full, moved[None], ((my_dp + n_dp - step) % n_dp, 0, 0)
            )
        return full.reshape(n_dp * array.shape[0], array.shape[1])

    kv_local = jnp.concatenate([w_qkv[:, q_width:], side], axis=1)
    attn_local = jnp.concatenate([kv_local, w_qkv[:, :q_width], w_out.T], axis=1)
    attn_zone = zone_rows(attn_local)
    kv_zone = attn_zone[:, : kv_local.shape[1]]
    big_zone = attn_zone[:, kv_local.shape[1] :]

    packed = pack_slices(after(w_mlp, attn_local), n_plane, chunks, chunk_cols)
    chunk_width = 3 * chunk_cols
    mlp_zone = swap_rows(packed)
    mlp_weights = [
        zone_gather(mlp_zone[:, chunk * chunk_width : (chunk + 1) * chunk_width])
        for chunk in range(chunks)
    ]

    w_kv_stages = plane.gather(kv_zone, 1, mlp_zone)
    w_q_stages = plane.gather(after(big_zone[:, :q_width], w_kv_stages[1]))
    w_out_near = after(big_zone[:, q_width:], w_q_stages[-2])
    w_out_near = plane.widen(w_out_near, 0)

    order_row, length_row, mask_row = after(
        (span_order[0], doc_lengths[0], pad_mask[0]), packed
    )
    row_in_span = jnp.arange(tok_rows, dtype=jnp.int32)
    stored_block = jnp.stack(plane.devices)
    spans = order_row[stored_block]
    own_place, own_begin = place_info(spans[0], row_in_span, length_row)
    flags = mask_row.reshape(n_plane, tok_rows)[stored_block]
    key_place = spans[:, None] * TOK_DEV + row_in_span[None, :]
    kinfo = jnp.stack(
        [jnp.where(flags == 1, key_place, FAR).reshape(-1), key_place.reshape(-1)], axis=1
    )
    qinfo = jnp.concatenate(
        [
            own_place[None],
            own_begin[None],
            flags[0][None],
            jnp.zeros((5, tok_rows), jnp.int32),
        ],
        axis=0,
    )
    need = ((spans <= spans[0]) & ((spans + 1) * TOK_DEV > own_begin[0])).astype(jnp.int32)

    inner = (own_place - own_begin).astype(F32)
    half = HEAD // 2
    frequency = ROPE_BASE ** (-(jnp.arange(half, dtype=F32) * 2.0) / HEAD)
    angles_t = frequency[:, None] * inner[None, :]
    cos_t, sin_t = jnp.cos(angles_t), jnp.sin(angles_t)
    cos_r, sin_r = cos_t.T[:, None, :], sin_t.T[:, None, :]

    w_kv_all = whole_rows(w_kv_stages[-2:])
    side_all = w_kv_all[:, 2 * kv_width :].astype(F32)
    gain_attn = side_all[:, 0]
    gain_mlp = side_all[:, 1]
    bias_all = side_all.reshape(n_all, local_rows, LANES)[:, 0, 64 : 64 + bias_rows].reshape(-1)

    inputs = layer_input.astype(F32)
    in_inverse = inverse_rms(inputs)
    normed_in = (inputs * in_inverse * gain_attn).astype(BF16)

    kv_proj = dot(normed_in, w_kv_all[:, : 2 * kv_width], 1, 0) + bias_all[q_width:]
    key_own = turn(kv_proj[:, :kv_width].reshape(tok_rows, KV_HEADS, HEAD), cos_r, sin_r)
    kv_own = jnp.concatenate([key_own.reshape(tok_rows, kv_width), kv_proj[:, kv_width:]], axis=1)
    kv_own = after(kv_own.astype(BF16), w_q_stages[-2])
    kv_stages = plane.gather(kv_own, 1, w_out_near)
    kv_all = jnp.concatenate(kv_stages[-2:], axis=0)
    w_q_all = whole_rows(w_q_stages[-2:])

    q_proj = dot(w_q_all, normed_in, 0, 1) + bias_all[:q_width, None]
    q_heads = q_proj.reshape(HEADS, 2, half, tok_rows)
    q_first, q_second = q_heads[:, 0], q_heads[:, 1]
    query_t = (
        jnp.stack(
            [q_first * cos_t - q_second * sin_t, q_second * cos_t + q_first * sin_t], axis=1
        )
        .reshape(q_width, tok_rows)
        .astype(BF16)
    )
    cot_near = plane.widen(after(cotangent, kv_stages[-2]), 0)
    need = after(need, w_out_near, cot_near)
    attended_t, lse = attention_forward(need, kinfo, qinfo, query_t, kv_all)
    for step in range(1, plane.steps):
        w_out_near = plane.widen(after(w_out_near, kv_stages[-2]), step, attended_t)
    w_out_all = whole_rows([w_out_near, plane.swap(w_out_near, plane.steps)])
    for step in range(1, plane.steps):
        cot_near = plane.widen(cot_near, step, attended_t)
    attended_t = after(attended_t, cot_near)

    middle = inputs + dot(attended_t, w_out_all, 0, 1)
    mid_inverse = inverse_rms(middle)
    normed_mid = (middle * mid_inverse * gain_mlp).astype(BF16)

    mid_near = normed_mid
    for step in range(plane.steps):
        mid_near = plane.widen(mid_near, step)
    cot_halves = cot_near, plane.swap(cot_near, plane.steps)
    mid_near = after(mid_near, mlp_weights[0])
    mid_halves = mid_near, plane.swap(mid_near, plane.steps)
    sums, chunk_grads = (), []
    if chunks > 1:
        *sums, chunk_grads = split_at(
            feed_forward(mid_halves, cot_halves, mlp_weights[:-1], (), True), 4
        )
    *sums, (extra,) = split_at(
        feed_forward(mid_halves, cot_halves, mlp_weights[-1:], tuple(sums), False), 4
    )

    def token_blocks(array):
        return [array[k * tok_rows : (k + 1) * tok_rows] for k in range(n_plane)]

    chunk_sums = [zone_sum(grad) for grad in chunk_grads]
    mid_fold = plane.fold(sums[0], sums[1], plane.steps)
    chunk_grads.append(feed_forward_grad(mid_halves, cot_halves, after(extra, mid_fold)))
    chunk_sums.append(zone_sum(chunk_grads[-1]))
    for step in range(plane.steps - 1, -1, -1):
        half = mid_fold.shape[0] // 2
        kept, sent = mid_fold[:half], mid_fold[half:]
        if step == plane.steps - 1:
            kept = after(kept, chunk_grads[-1])
        mid_fold = plane.fold(kept, sent, step)
        if step == 0:
            out_fold = plane.fold(after(sums[2], kept), sums[3], plane.steps)
    mid_grad = after(mid_fold, *chunk_sums[:-1][:1]).astype(F32)

    out_grad = cotangent.astype(F32)
    gain_mlp_grad = jnp.sum(mid_grad * (middle * mid_inverse), axis=0)
    middle_grad = out_grad + norm_backward(middle, mid_inverse, mid_grad * gain_mlp)
    middle_low = middle_grad.astype(BF16)
    attended_grad_t = dot(w_out_all, middle_low, 0, 1).astype(BF16)
    attended_grad_t = after(attended_grad_t, out_fold)
    query_grad, *kv_grads = attention_backward(
        need, kinfo, qinfo, cos_t, sin_t, query_t, kv_all, attended_t, attended_grad_t, lse
    )
    kv_fold = plane.fold(*kv_grads, plane.steps)
    first_swapped = [swap_rows(after(array, mid_fold)) for array in chunk_sums[:-1][:1]]
    mlp_out = after(out_fold, mid_fold)
    for step in range(plane.steps - 1, 0, -1):
        mlp_out = plane.fold_rest(mlp_out, step)
    big_grads = weight_grads(
        plane,
        local_rows,
        [
            (after(normed_in, mlp_out, kv_fold, *first_swapped), query_grad, False),
            (middle_low, attended_t, True),
        ],
    )
    big_fold = plane.fold(*big_grads, plane.steps)
    mlp_out = plane.fold_rest(after(mlp_out, kv_fold), 0)
    for step in range(plane.steps - 1, -1, -1):
        rows = kv_fold.shape[0] // 2
        kept, sent = kv_fold[:rows], kv_fold[rows:]
        if step == plane.steps - 1:
            kept = after(kept, big_fold, *chunk_sums[1:-1])
        kv_fold = plane.fold(kept, sent, step)
    kv_back = after(kv_fold, mlp_out)
    kv_back = kv_back.astype(F32)
    key_back = turn(kv_back[:, :kv_width].reshape(tok_rows, KV_HEADS, HEAD), cos_r, -sin_r)
    projected_grad = jnp.concatenate(
        [query_grad, key_back.reshape(tok_rows, kv_width).astype(BF16), kv_back[:, kv_width:].astype(BF16)],
        axis=1,
    )
    in_grad = dot(projected_grad[:, :q_width], w_q_all, 1, 1) + dot(
        projected_grad[:, q_width:], w_kv_all[:, : 2 * kv_width], 1, 1
    )
    gain_attn_grad = jnp.sum(in_grad * (inputs * in_inverse), axis=0)
    input_grad = middle_grad + norm_backward(inputs, in_inverse, in_grad * gain_attn)
    qkv_bias_grad = jnp.sum(projected_grad.astype(F32), axis=0)

    def side_rows(array):
        array = array.reshape(n_dp, n_plane, 1, -1)
        return jnp.pad(array, ((0, 0), (0, 0), (0, 0), (0, LANES - array.shape[-1])))

    side_grad = jnp.concatenate(
        [side_rows(gain_attn_grad), side_rows(gain_mlp_grad), side_rows(qkv_bias_grad)]
        + [jnp.zeros((n_dp, n_plane, 1, LANES), F32)] * 5,
        axis=2,
    )
    side_grad = jnp.pad(side_grad, ((0, 0), (0, 0), (0, local_rows - 8), (0, 0)))
    side_grad = side_grad.reshape(n_all * local_rows, LANES).astype(BF16)
    for step in range(plane.steps - 1, 0, -1):
        big_fold = plane.fold_rest(big_fold, step)
    small_grads = weight_grads(
        plane,
        local_rows,
        [(after(normed_in, big_fold), projected_grad[:, q_width:], False)],
        side_grad,
    )
    big_fold = plane.fold_rest(big_fold, 0)
    small_fold = plane.fold(*small_grads, plane.steps)
    for step in range(plane.steps - 1, -1, -1):
        rows = small_fold.shape[0] // 2
        kept, sent = small_fold[:rows], small_fold[rows:]
        if step == 0:
            kept = after(kept, chunk_sums[-1])
        small_fold = plane.fold(kept, sent, step)
    attn_plane = jnp.concatenate([big_fold, small_fold], axis=1)
    grad_qkv, grad_out, grad_gain_attn, grad_gain_mlp, grad_bias = spread_sums(
        zone_sum(attn_plane), q_width, width, 2 * kv_width, (local_rows, local_rows, bias_rows)
    )

    late_sums = jnp.concatenate(chunk_sums[len(first_swapped) :], axis=1)
    swapped = first_swapped + [swap_rows(after(late_sums, attn_plane))]
    grad_mlp = unpack_slices(swapped, local_rows, ffn_width, n_plane, chunks, chunk_cols)
    block_output = (middle + mlp_out.astype(F32)).astype(BF16)
    return (
        block_output,
        input_grad,
        grad_qkv,
        grad_bias,
        grad_out,
        grad_gain_attn,
        grad_gain_mlp,
        grad_mlp,
    )


def solution(mesh):
    rows = P(EVERY, None)
    flat = P(EVERY)
    columns = P(None, EVERY)
    batch = P("dp", None)
    return jax.shard_map(
        shards,
        mesh=mesh,
        in_specs=(rows, batch, batch, batch, rows, flat, columns, flat, flat, rows, rows),
        out_specs=(rows, rows, rows, flat, columns, flat, flat, rows),
        check_vma=False,
    )
```
